32 devices in a mesh: grp: 2 (over x), gx: 16 (over z, y, core).
Axes of the slice: x: 2, y: 2, z: 4, core: 2. Of those that a mesh axis runs over, the one named last changes fastest.
Arguments:
- phase_lin: float32 [64, 128, 512], P(('grp', 'gx')), parts along dimension 0, may hold values from -1.1 to 1.1
- phase_state: float32 [64, 128, 512], P(('grp', 'gx')), parts along dimension 0, may hold values from -1 to 1
- cotangent: float32 [2, 64, 128, 512], P(None, ('grp', 'gx')), parts along dimension 1, may hold values from -4 to 4
- warm_start: float32 [2, 64, 128, 512], P(None, ('grp', 'gx')), parts along dimension 1, may hold values from -3 to 3
Outputs:
- adjoint: float32 [2, 64, 128, 512], P(None, ('grp', 'gx')), parts along dimension 1
- design_grad: float32 [64, 128, 512], P(('grp', 'gx')), parts along dimension 0
The draws below stay inside these ranges and needn't reach their ends.
There are 2 independent parts, one for each index of `grp`. The reference program is written for one: setup_inputs(seed, part) draws one part's arguments, and reference() takes and returns one part's arrays. A program takes and returns all parts, laid end to end along the dimension named above; each array names one. Nothing has to cross between parts.
All inputs are finite; a program needn't handle non-finite values.
Results may differ from the reference program's by a relative error of at most 0.0001.
Values sent between devices are 32-bit elements; how exact they have to be, the bound alone decides.
No kernel may reach another device: no remote copies, remote signals or barrier semaphores. Data moves between devices by JAX's collectives and lax.ppermute only.
A program may use at most 192 MiB of HBM per device.

```python
import jax
import jax.numpy as jnp

NY = 128
NZ = 512
SWEEPS = 2
COARSE_SWEEPS = 4
CYCLES = 1
NX = 32


def draw_cotangent(key, part):
    key = jax.random.fold_in(key, 7)
    extent = (2, NX, NY, NZ)
    values = jnp.clip(jax.random.normal(key, extent, jnp.float32), -4.0, 4.0)
    return values


def steps_of(own_key, shape, cuts, low, high):
    def one(dim, shards_of):
        draws = jax.random.uniform(jax.random.fold_in(jax.random.fold_in(own_key, 6), dim), (shards_of,), jnp.float32, low / len(cuts), high / len(cuts))
        return jnp.repeat(jnp.exp(draws), shape[dim] // shards_of).reshape((-1,) + (1,) * (len(shape) - dim - 1))

    factor_of = one(*cuts[0])
    for cut in cuts[1:]:
        factor_of = factor_of * one(*cut)
    return factor_of


def gaussian(own_key, shape, width, reach, shards=(), kind=jnp.bfloat16):
    values = jax.random.normal(own_key, shape, jnp.float32) * width
    if len(shards) > 0:
        values = steps_of(own_key, shape, shards, -0.22, 0.18) * values
    return jnp.clip(values, min=-reach, max=reach).astype(kind)


def setup_inputs(seed: int = 0, part: int = 0) -> dict:
    arg_keys = jax.random.split(jax.random.key(seed), 5)
    own_keys = jax.random.split(jax.random.fold_in(arg_keys[4], part), 5)
    phase_lin = jnp.clip(jax.random.uniform(own_keys[0], (NX, NY, NZ), jnp.float32, -1.1, 1.1) * steps_of(own_keys[0], (NX, NY, NZ), ((0, 16),), -0.4, 0.0), -1.1, 1.1)
    phase_state = jnp.clip(jax.random.uniform(own_keys[1], (NX, NY, NZ), jnp.float32, -1.0, 1.0) * steps_of(own_keys[1], (NX, NY, NZ), ((0, 16),), -0.4, 0.0), -1.0, 1.0)
    cotangent = draw_cotangent(jax.random.fold_in(jax.random.fold_in(arg_keys[4], part), 71), part)
    warm_start = gaussian(own_keys[3], (2, NX, NY, NZ), 0.5, 3.0, ((1, 16),), jnp.float32)
    return dict(phase_lin=phase_lin, phase_state=phase_state, cotangent=cotangent, warm_start=warm_start)


GRADIENT_ENERGY = 1.0
TIME_STEP = 0.02
DAMPING = 0.8


def neighbour_sum(field):
    padded = jnp.pad(field, ((0, 0), (1, 1), (1, 1), (1, 1)))
    total = padded[:, 2:, 1:-1, 1:-1] + padded[:, :-2, 1:-1, 1:-1]
    total = total + padded[:, 1:-1, 2:, 1:-1] + padded[:, 1:-1, :-2, 1:-1]
    total = total + padded[:, 1:-1, 1:-1, 2:] + padded[:, 1:-1, 1:-1, :-2]
    return total


def residual_of(state, curvature, source, energy, step):
    laplace = neighbour_sum(state) - 6.0 * state
    resid_phase = source[0] - (state[0] - curvature * state[1] + energy * laplace[1])
    resid_chem = source[1] - (-step * laplace[0] + state[1])
    return resid_phase, resid_chem


def relax_cells(state, curvature, source, energy, step):
    resid_phase, resid_chem = residual_of(state, curvature, source, energy, step)
    coupling = curvature + 6.0 * energy
    determinant = 1.0 + 6.0 * step * coupling
    new_phase = state[0] + DAMPING * (resid_phase + coupling * resid_chem) / determinant
    new_chem = state[1] + DAMPING * (resid_chem - 6.0 * step * resid_phase) / determinant
    return jnp.stack([new_phase, new_chem])


def coarsen(field):
    lead = field.shape[:-3]
    planes, rows_y, cols_z = field.shape[-3:]
    blocks = field.reshape(lead + (planes // 2, 2, rows_y // 2, 2, cols_z // 2, 2))
    return jnp.mean(blocks, axis=(-5, -3, -1))


def refine(field):
    return jnp.repeat(jnp.repeat(jnp.repeat(field, 2, -3), 2, -2), 2, -1)


def reference(phase_lin, phase_state, cotangent, warm_start):
    curvature = 3.0 * phase_lin * phase_lin - 1.0
    coarse_curv = coarsen(curvature)
    state = warm_start
    for cycle_index in range(CYCLES):
        for sweep_index in range(SWEEPS):
            state = relax_cells(state, curvature, cotangent, GRADIENT_ENERGY, TIME_STEP)
        resid_phase, resid_chem = residual_of(state, curvature, cotangent, GRADIENT_ENERGY, TIME_STEP)
        coarse_source = coarsen(jnp.stack([resid_phase, resid_chem]))
        correction = jnp.zeros_like(coarse_source)
        for sweep_index in range(COARSE_SWEEPS):
            correction = relax_cells(correction, coarse_curv, coarse_source, GRADIENT_ENERGY / 4.0, TIME_STEP / 4.0)
        state = state + refine(correction)
        for sweep_index in range(SWEEPS):
            state = relax_cells(state, curvature, cotangent, GRADIENT_ENERGY, TIME_STEP)
    design_grad = 6.0 * phase_lin * phase_state * state[1]
    return state, design_grad
```

```python
import jax
import jax.numpy as jnp
from jax import lax
from jax.sharding import PartitionSpec as P

SWEEPS = 2
COARSE_SWEEPS = 4

GRADIENT_ENERGY = 1.0
TIME_STEP = 0.02
DAMPING = 0.8


def chip_pairs(count):
    return [(i, i ^ 1) for i in range(count)]


def cross_pairs(groups, count):
    pairs = []
    for g in range(groups):
        pairs += [(g * count + i, g * count + i + 1) for i in range(1, count - 1, 2)]
    for g in range(0, groups - 1, 2):
        pairs += [(g * count + i, (g + 1) * count + i) for i in (0, count - 1)]
    swaps = pairs + [(b, a) for a, b in pairs]
    if groups % 2 == 1:
        swaps += [((groups - 1) * count + i,) * 2 for i in (0, count - 1)]
    return swaps


def in_plane(x):
    lead = ((0, 0),) * (x.ndim - 2)
    rows = jnp.pad(x, lead + ((1, 1), (0, 0)))
    cols = jnp.pad(x, lead + ((0, 0), (1, 1)))
    return rows[..., 2:, :] + rows[..., :-2, :] + cols[..., 2:] + cols[..., :-2]


def pair_matrix(size):
    row = lax.broadcasted_iota(jnp.int32, (size, size // 2), 0)
    col = lax.broadcasted_iota(jnp.int32, (size, size // 2), 1)
    return (row // 2 == col).astype(jnp.float32)


def pooled(x):
    rows, cols = x.shape[-2:]
    lead = x.shape[:-2]
    flat = x.reshape((-1, cols))
    half = jnp.dot(flat, pair_matrix(cols), precision=lax.Precision.HIGHEST)
    half = half.reshape((-1, rows, cols // 2))
    out = jnp.einsum("ry,nyc->nrc", pair_matrix(rows).T, half, precision=lax.Precision.HIGHEST)
    return out.reshape(lead + (rows // 2, cols // 2))


def spread(x):
    rows, cols = x.shape[-2:]
    lead = x.shape[:-2]
    tall = jnp.einsum("ry,nyc->nrc", pair_matrix(2 * rows), x.reshape((-1, rows, cols)), precision=lax.Precision.HIGHEST)
    wide = jnp.dot(tall.reshape((-1, cols)), pair_matrix(2 * cols).T, precision=lax.Precision.HIGHEST)
    return wide.reshape(lead + (2 * rows, 2 * cols))


class Level:
    def __init__(self, curvature, source, energy, step):
        self.energy, self.step = energy, step
        coupling = curvature + 6.0 * energy
        self.gain = DAMPING / (1.0 + 6.0 * step * coupling)
        self.gain_coupling = self.gain * coupling * step
        self.own = (
            self.gain * (source[0] + coupling * source[1]),
            self.gain * (source[1] - 6.0 * step * source[0]),
        )

    def add(self, base, nb):
        phase = base[0] - self.gain * (self.energy * nb[1]) + self.gain_coupling * nb[0]
        chem = base[1] + self.gain * (self.step * (nb[0] + 6.0 * self.energy * nb[1]))
        return jnp.stack([phase, chem])

    def begin(self, state, nb):
        keep = 1.0 - DAMPING
        return self.add((keep * state[0] + self.own[0], keep * state[1] + self.own[1]), nb)


def on_device(phase_lin, phase_state, cotangent, warm_start):
    groups, count = lax.axis_size("grp"), lax.axis_size("gx")
    me = lax.axis_index("gx")
    cross = me % 2
    inner = 1 - cross
    at_end = (me == 0) | (me == count - 1)
    across = cross_pairs(groups, count)
    on_chip = chip_pairs(count)

    def swap_cross(x):
        return lax.ppermute(x, ("grp", "gx"), across)

    def swap_chip(x):
        return lax.ppermute(x, "gx", on_chip)

    def masked(x):
        return jnp.where(at_end, 0.0, x)

    def plane(x, which, axis):
        return lax.dynamic_index_in_dim(x, which, axis, keepdims=False)

    fence = lax.optimization_barrier

    state = (plane(warm_start, cross, 1), plane(warm_start, inner, 1))
    phi = (plane(phase_lin, cross, 0), plane(phase_lin, inner, 0))
    cot = (plane(cotangent, cross, 1), plane(cotangent, inner, 1))
    curvature = tuple(3.0 * v * v - 1.0 for v in phi)
    fine = tuple(Level(c, s, GRADIENT_ENERGY, TIME_STEP) for c, s in zip(curvature, cot))

    def sweep(state, halo):
        part = fence(tuple(fine[i].begin(state[i], in_plane(state[i]) + state[1 - i]) for i in range(2)))
        return tuple(fine[i].add(part[i], halo[i]) for i in range(2))

    def halos(state):
        far = swap_cross(state[0])
        near = swap_chip(state[1])
        return (masked(far), near)

    for sweep_index in range(SWEEPS):
        state = sweep(state, halos(state))
    state = fence(state)

    coarse_halos = halos(tuple(pooled(v) for v in state))
    state_halos = halos(state)

    def local_defect(i):
        own, nb = state[i], in_plane(state[i]) + state[1 - i]
        lap = nb - 6.0 * own
        r0 = cot[i][0] - (own[0] - curvature[i] * own[1] + GRADIENT_ENERGY * lap[1])
        r1 = cot[i][1] - (-TIME_STEP * lap[0] + own[1])
        return jnp.stack([r0, r1])

    coarse_curv = pooled(curvature[0] + curvature[1]) / 8.0
    local = fence(pooled(local_defect(0) + local_defect(1)) / 8.0)
    both = (coarse_halos[0] + coarse_halos[1]) / 8.0
    source = (local[0] - GRADIENT_ENERGY * both[1], local[1] + TIME_STEP * both[0])

    coarse = Level(coarse_curv, source, GRADIENT_ENERGY / 4.0, TIME_STEP / 4.0)
    fix = jnp.stack(coarse.own)
    for sweep_index in range(COARSE_SWEEPS - 1):
        far, near = halos((fix, fix))
        part = fence(coarse.begin(fix, in_plane(fix)))
        fix = coarse.add(part, far + near)

    fix_halos = halos((fix, fix))
    fine_fix = spread(fix)
    state = tuple(v + fine_fix for v in state)
    part = fence(tuple(fine[i].begin(state[i], in_plane(state[i]) + state[1 - i]) for i in range(2)))
    part = fence(tuple(fine[i].add(part[i], state_halos[i]) for i in range(2)))
    state = tuple(fine[i].add(part[i], spread(fix_halos[i])) for i in range(2))
    for sweep_index in range(SWEEPS - 1):
        state = sweep(state, halos(state))

    first = jnp.where(cross == 0, state[0], state[1])
    second = jnp.where(cross == 0, state[1], state[0])
    adjoint = jnp.stack([first, second], axis=1)
    design_grad = 6.0 * phase_lin * phase_state * adjoint[1]
    return (adjoint, design_grad)


def solution(mesh):
    in_specs = (
        P(("grp", "gx"), None, None),
        P(("grp", "gx"), None, None),
        P(None, ("grp", "gx"), None, None),
        P(None, ("grp", "gx"), None, None),
    )
    out_specs = (P(None, ("grp", "gx"), None, None), P(("grp", "gx"), None, None))
    return jax.shard_map(
        on_device, mesh=mesh, in_specs=in_specs, out_specs=out_specs, check_vma=False
    )
```

```python
import functools

import jax
import jax.numpy as jnp
from jax import lax
from jax.experimental import pallas as pl
from jax.experimental.pallas import tpu as pltpu
from jax.sharding import PartitionSpec as P

SWEEPS = 2
COARSE_SWEEPS = 4

GRADIENT_ENERGY = 1.0
TIME_STEP = 0.02
DAMPING = 0.8
KEEP = 1.0 - DAMPING
COARSE_ENERGY = GRADIENT_ENERGY / 4.0
COARSE_STEP = TIME_STEP / 4.0


VMEM = pl.BlockSpec(memory_space=pltpu.VMEM)
SMEM = pl.BlockSpec(memory_space=pltpu.SMEM)
ANY = pl.BlockSpec(memory_space=pl.ANY)
BLOCK = 16
F32 = jnp.float32


def chip_pairs(count):
    return [(i, i ^ 1) for i in range(count)]


def cross_pairs(groups, count):
    pairs = []
    for g in range(groups):
        pairs += [(g * count + i, g * count + i + 1) for i in range(1, count - 1, 2)]
    for g in range(0, groups - 1, 2):
        pairs += [(g * count + i, (g + 1) * count + i) for i in (0, count - 1)]
    swaps = pairs + [(b, a) for a, b in pairs]
    if groups % 2 == 1:
        swaps += [((groups - 1) * count + i,) * 2 for i in (0, count - 1)]
    return swaps


def call(body, name, outs, args, in_specs=None, out_specs=None, scratch=(), aliases=None, work=30):
    shapes = [jax.ShapeDtypeStruct(s, F32) for s in outs]
    size = sum(int(a.size) for a in args)
    made = sum(s.size for s in shapes)
    return pl.pallas_call(
        body,
        out_shape=shapes,
        in_specs=in_specs or [VMEM] * len(args),
        out_specs=out_specs or [VMEM] * len(outs),
        scratch_shapes=list(scratch),
        input_output_aliases=aliases or {},
        name=name,
        cost_estimate=pl.CostEstimate(flops=work * made, bytes_accessed=4 * (size + made), transcendentals=0),
        compiler_params=pltpu.CompilerParams(vmem_limit_bytes=24 * 1024 * 1024),
    )(*args)


def blocks(rows):
    return range(0, rows, BLOCK)


def around(read, r, rows):
    x = read(r, r + BLOCK)
    cols = x.shape[-1]
    row = lax.broadcasted_iota(jnp.int32, x.shape, 0)
    col = lax.broadcasted_iota(jnp.int32, x.shape, 1)
    up = read(r - 1, r - 1 + BLOCK) if r > 0 else jnp.where(row == 0, 0.0, pltpu.roll(x, 1, 0))
    if r + BLOCK < rows:
        down = read(r + 1, r + 1 + BLOCK)
    else:
        down = jnp.where(row == BLOCK - 1, 0.0, pltpu.roll(x, BLOCK - 1, 0))
    left = jnp.where(col == 0, 0.0, pltpu.roll(x, 1, 1))
    right = jnp.where(col == cols - 1, 0.0, pltpu.roll(x, cols - 1, 1))
    return x, (up + down) + (left + right)


def reader(ref, *lead):
    return lambda lo, hi: ref[(*lead, slice(lo, hi))]


def add_terms(base_p, base_m, gain, gain_kt, nb_p, nb_m, energy, step):
    new_p = base_p - gain * (energy * nb_m) + gain_kt * nb_p
    new_m = base_m + gain * (step * nb_p + (6.0 * step * energy) * nb_m)
    return new_p, new_m


def parts3(x):
    high = x.astype(jnp.bfloat16)
    rest = x - high.astype(F32)
    middle = rest.astype(jnp.bfloat16)
    low = (rest - middle.astype(F32)).astype(jnp.bfloat16)
    return high, middle, low


def pair_cols(x, pair):
    return sum(jnp.dot(v, pair, preferred_element_type=F32) for v in parts3(x))


def copy_cols(x, pair):
    dims = (((1,), (1,)), ((), ()))
    return sum(lax.dot_general(v, pair, dims, preferred_element_type=F32) for v in parts3(x))


LANES = 128


def tiles(rows, cols):
    return pltpu.VMEM((cols // LANES, rows, LANES), F32)


def put_rows(ref, rows, x):
    for j in range(ref.shape[0]):
        ref[j, rows] = x[:, j * LANES : (j + 1) * LANES]


def get_rows(ref, rows):
    return jnp.concatenate([ref[j, rows] for j in range(ref.shape[0])], axis=1)


def even_odd(ref):
    half = ref.shape[1] // 2
    return pl.ds(0, half, stride=2), pl.ds(1, half, stride=2)


def pair_rows(ref):
    even, odd = even_odd(ref)
    return get_rows(ref, even) + get_rows(ref, odd)


def split_body(where, warm, far, near, sems):
    c = where[0]
    first = pltpu.make_async_copy(warm.at[:, c], far, sems.at[0])
    second = pltpu.make_async_copy(warm.at[:, 1 - c], near, sems.at[1])
    first.start()
    second.start()
    first.wait()
    second.wait()


def setup_body(where, phi, cot, gain, gain_kt, own):
    c = where[0]
    for i in range(2):
        plane = c if i == 0 else 1 - c
        for r in blocks(phi.shape[1]):
            rows = slice(r, r + BLOCK)
            v = phi[plane, rows]
            k = 3.0 * v * v - 1.0 + 6.0 * GRADIENT_ENERGY
            g = DAMPING / (1.0 + 6.0 * TIME_STEP * k)
            s0, s1 = cot[0, plane, rows], cot[1, plane, rows]
            gain[i, rows] = g
            gain_kt[i, rows] = g * k * TIME_STEP
            own[i, 0, rows] = g * (s0 + k * s1)
            own[i, 1, rows] = g * (s1 - 6.0 * TIME_STEP * s0)


def coarse_setup_body(phi, pair, gain, gain_kt, both):
    for r in blocks(phi.shape[1]):
        rows = slice(r, r + BLOCK)
        a, b = phi[0, rows], phi[1, rows]
        put_rows(both, rows, (3.0 * a * a - 1.0) + (3.0 * b * b - 1.0))
    k = pair_cols(pair_rows(both), pair[...]) / 8.0 + 6.0 * COARSE_ENERGY
    g = DAMPING / (1.0 + 6.0 * COARSE_STEP * k)
    gain[...] = g
    gain_kt[...] = g * k * COARSE_STEP


def part_body(far, near, gain, gain_kt, own, far_out, near_out):
    rows_all = far.shape[1]
    for i, (mine, other, out) in enumerate(((far, near, far_out), (near, far, near_out))):
        for r in blocks(rows_all):
            rows = slice(r, r + BLOCK)
            p, nb_p = around(reader(mine, 0), r, rows_all)
            m, nb_m = around(reader(mine, 1), r, rows_all)
            out[0, rows], out[1, rows] = add_terms(
                KEEP * p + own[i, 0, rows],
                KEEP * m + own[i, 1, rows],
                gain[i, rows],
                gain_kt[i, rows],
                nb_p + other[0, rows],
                nb_m + other[1, rows],
                GRADIENT_ENERGY,
                TIME_STEP,
            )


def finish_body(i, keep, part, halo, gain, gain_kt, out):
    for r in blocks(part.shape[1]):
        rows = slice(r, r + BLOCK)
        hp, hm = halo[0, rows], halo[1, rows]
        if i == 0:
            hp, hm = hp * keep[0], hm * keep[0]
        out[0, rows], out[1, rows] = add_terms(
            part[0, rows], part[1, rows], gain[i, rows], gain_kt[i, rows], hp, hm, GRADIENT_ENERGY, TIME_STEP
        )


def finish_pool_body(i, keep, part, halo, gain, gain_kt, pair, pool, out, tile):
    finish_body(i, keep, part, halo, gain, gain_kt, out)
    for f in range(2):
        for r in blocks(part.shape[1]):
            rows = slice(r, r + BLOCK)
            put_rows(tile, rows, out[f, rows])
        pool[f] = pair_cols(pair_rows(tile), pair[...])


def defect_body(where, far, near, phi, cot, pair, out, total, tile):
    c = where[0]
    rows_all = far.shape[1]
    for i, (mine, other) in enumerate(((far, near), (near, far))):
        plane = c if i == 0 else 1 - c
        for r in blocks(rows_all):
            rows = slice(r, r + BLOCK)
            p, nb_p = around(reader(mine, 0), r, rows_all)
            m, nb_m = around(reader(mine, 1), r, rows_all)
            v = phi[plane, rows]
            lap_p = nb_p + other[0, rows] - 6.0 * p
            lap_m = nb_m + other[1, rows] - 6.0 * m
            r0 = cot[0, plane, rows] - (p - (3.0 * v * v - 1.0) * m + GRADIENT_ENERGY * lap_m)
            r1 = cot[1, plane, rows] - (m - TIME_STEP * lap_p)
            total[0, rows] = r0 if i == 0 else total[0, rows] + r0
            total[1, rows] = r1 if i == 0 else total[1, rows] + r1
    for f in range(2):
        for r in blocks(rows_all):
            rows = slice(r, r + BLOCK)
            put_rows(tile, rows, total[f, rows])
        out[f] = pair_cols(pair_rows(tile), pair[...]) / 8.0


def coarse_first_body(keep, local, far, near, gain, gain_kt, out):
    for r in blocks(local.shape[1]):
        rows = slice(r, r + BLOCK)
        s0 = local[0, rows] - (GRADIENT_ENERGY / 8.0) * (far[1, rows] * keep[0] + near[1, rows])
        s1 = local[1, rows] + (TIME_STEP / 8.0) * (far[0, rows] * keep[0] + near[0, rows])
        g = gain[rows]
        out[0, rows] = g * s0 + (gain_kt[rows] / COARSE_STEP) * s1
        out[1, rows] = g * (s1 - 6.0 * COARSE_STEP * s0)


def coarse_part_body(fix, own, gain, gain_kt, out):
    rows_all = fix.shape[1]
    for r in blocks(rows_all):
        rows = slice(r, r + BLOCK)
        p, nb_p = around(reader(fix, 0), r, rows_all)
        m, nb_m = around(reader(fix, 1), r, rows_all)
        out[0, rows], out[1, rows] = add_terms(
            KEEP * p + own[0, rows],
            KEEP * m + own[1, rows],
            gain[rows],
            gain_kt[rows],
            nb_p,
            nb_m,
            COARSE_ENERGY,
            COARSE_STEP,
        )


def coarse_finish_body(keep, part, far, near, gain, gain_kt, out):
    for r in blocks(part.shape[1]):
        rows = slice(r, r + BLOCK)
        out[0, rows], out[1, rows] = add_terms(
            part[0, rows],
            part[1, rows],
            gain[rows],
            gain_kt[rows],
            far[0, rows] * keep[0] + near[0, rows],
            far[1, rows] * keep[0] + near[1, rows],
            COARSE_ENERGY,
            COARSE_STEP,
        )


def spread_into(tile, fix, pair):
    wide = copy_cols(fix, pair)
    for rows in even_odd(tile):
        put_rows(tile, rows, wide)


def correct_body(far, near, fix, pair, far_out, near_out, tile):
    for f in range(2):
        spread_into(tile, fix[f], pair[...])
        for r in blocks(far.shape[1]):
            rows = slice(r, r + BLOCK)
            wide = get_rows(tile, rows)
            far_out[f, rows] = far[f, rows] + wide
            near_out[f, rows] = near[f, rows] + wide


def finish_fix_body(i, keep, part, halo, pair, gain, gain_kt, out, phase, chem):
    spread_into(phase, halo[0], pair[...])
    spread_into(chem, halo[1], pair[...])
    for r in blocks(part.shape[1]):
        rows = slice(r, r + BLOCK)
        hp, hm = get_rows(phase, rows), get_rows(chem, rows)
        if i == 0:
            hp, hm = hp * keep[0], hm * keep[0]
        out[0, rows], out[1, rows] = add_terms(
            part[0, rows], part[1, rows], gain[i, rows], gain_kt[i, rows], hp, hm, GRADIENT_ENERGY, TIME_STEP
        )


def final_plane(i, where, keep, part, halo, gain, gain_kt, phi, psi, adjoint, design, plane_out, grad_out, sems):
    c = where[0]
    plane = c if i == 0 else 1 - c
    rows_all = part.shape[1]
    step = rows_all // 2
    copies = []
    for n, lo in enumerate(range(0, rows_all, step)):
        for r in range(lo, lo + step, BLOCK):
            rows = slice(r, r + BLOCK)
            hp, hm = halo[0, rows], halo[1, rows]
            if i == 0:
                hp, hm = hp * keep[0], hm * keep[0]
            p, m = add_terms(
                part[0, rows], part[1, rows], gain[i, rows], gain_kt[i, rows], hp, hm, GRADIENT_ENERGY, TIME_STEP
            )
            plane_out[0, rows] = p
            plane_out[1, rows] = m
            grad_out[rows] = 6.0 * phi[plane, rows] * psi[plane, rows] * m
        rows = pl.ds(lo, step)
        copies.append(pltpu.make_async_copy(plane_out.at[:, rows], adjoint.at[:, plane, rows], sems.at[2 * n]))
        copies.append(pltpu.make_async_copy(grad_out.at[rows], design.at[plane, rows], sems.at[2 * n + 1]))
        copies[-2].start()
        copies[-1].start()
    for copy in copies:
        copy.wait()


def last_near_body(where, keep, part, halo, gain, gain_kt, phi, psi, adjoint, design, plane_out, grad_out, sems):
    final_plane(1, where, keep, part, halo, gain, gain_kt, phi, psi, adjoint, design, plane_out, grad_out, sems)


def last_far_body(
    where, keep, part, halo, gain, gain_kt, phi, psi, a_in, d_in, adjoint, design, plane_out, grad_out, sems
):
    final_plane(0, where, keep, part, halo, gain, gain_kt, phi, psi, adjoint, design, plane_out, grad_out, sems)


def on_device(phase_lin, phase_state, cotangent, warm_start):
    groups, count = lax.axis_size("grp"), lax.axis_size("gx")
    me = lax.axis_index("gx")
    where = jnp.reshape(me % 2, (1,)).astype(jnp.int32)
    keep = jnp.reshape(((me > 0) & (me < count - 1)).astype(F32), (1,))
    across, on_chip = cross_pairs(groups, count), chip_pairs(count)
    rows, cols = phase_lin.shape[1:]
    full, half = (2, rows, cols), (2, rows // 2, cols // 2)
    pair = lax.broadcasted_iota(jnp.int32, (cols, cols // 2), 0) // 2
    pair = (pair == lax.broadcasted_iota(jnp.int32, (cols, cols // 2), 1)).astype(jnp.bfloat16)

    def swap_far(x):
        return lax.ppermute(x, ("grp", "gx"), across)

    def swap_near(x):
        return lax.ppermute(x, "gx", on_chip)

    def finish(i, part, halo):
        body = functools.partial(finish_body, i)
        return call(body, "finish", [full], (keep, part, halo, gain, gain_kt), [SMEM] + [VMEM] * 4, work=8)[0]

    far, near = call(
        split_body, "split", [full, full], (where, warm_start), [SMEM, ANY], scratch=[pltpu.SemaphoreType.DMA((2,))]
    )
    far_halo, near_halo = swap_far(far), swap_near(near)
    gain, gain_kt, own = call(
        setup_body, "setup", [full, full, (2, 2, rows, cols)], (where, phase_lin, cotangent), [SMEM, VMEM, VMEM]
    )

    def part_of(far, near):
        return call(part_body, "part", [full, full], (far, near, gain, gain_kt, own))

    far_part, near_part = part_of(far, near)
    far, near = finish(0, far_part, far_halo), finish(1, near_part, near_halo)
    for sweep_index in range(SWEEPS - 2):
        far_halo, near_halo = swap_far(far), swap_near(near)
        far_part, near_part = part_of(far, near)
        far, near = finish(0, far_part, far_halo), finish(1, near_part, near_halo)

    far_halo, near_halo = swap_far(far), swap_near(near)
    far_part, near_part = part_of(far, near)
    coarse_gain, coarse_kt = call(
        coarse_setup_body, "coarse_setup", [half[1:], half[1:]], (phase_lin, pair), scratch=[tiles(rows, cols)]
    )

    def finish_pool(i, part, halo):
        body = functools.partial(finish_pool_body, i)
        specs = [SMEM] + [VMEM] * 5
        args = (keep, part, halo, gain, gain_kt, pair)
        return call(body, "finish_pool", [half, full], args, specs, scratch=[tiles(rows, cols)], work=8)

    near_pool, near = finish_pool(1, near_part, near_halo)
    far_pool, far = finish_pool(0, far_part, far_halo)

    far_sums, near_sums = swap_far(far_pool), swap_near(near_pool)
    near_halo = swap_near(near)
    piece = rows // COARSE_SWEEPS
    far_pieces = [far[:, n * piece : (n + 1) * piece] for n in range(COARSE_SWEEPS)]
    arrived = [swap_far(far_pieces[0])]
    local = call(
        defect_body,
        "defect",
        [half],
        (where, far, near, phase_lin, cotangent, pair),
        [SMEM] + [VMEM] * 5,
        scratch=[pltpu.VMEM(full, F32), tiles(rows, cols)],
    )[0]
    fix = call(
        coarse_first_body,
        "coarse_first",
        [half],
        (keep, local, far_sums, near_sums, coarse_gain, coarse_kt),
        [SMEM] + [VMEM] * 5,
        work=8,
    )[0]
    first = fix
    for sweep_index in range(COARSE_SWEEPS - 1):
        far_sums, near_sums = swap_far(fix), swap_near(fix)
        fix, held = lax.optimization_barrier((fix, far_pieces[sweep_index + 1]))
        arrived.append(swap_far(held))
        part = call(coarse_part_body, "coarse_part", [half], (fix, first, coarse_gain, coarse_kt))[0]
        part, arrived[sweep_index] = lax.optimization_barrier((part, arrived[sweep_index]))
        fix = call(
            coarse_finish_body,
            "coarse_finish",
            [half],
            (keep, part, far_sums, near_sums, coarse_gain, coarse_kt),
            [SMEM] + [VMEM] * 5,
            work=8,
        )[0]

    far_sums, near_sums = swap_far(fix), swap_near(fix)
    far, near = call(
        correct_body, "correct", [full, full], (far, near, fix, pair), scratch=[tiles(rows, cols)], work=4
    )
    far_part, near_part = part_of(far, near)
    far_part = finish(0, far_part, jnp.concatenate(arrived, axis=1))
    near_part = finish(1, near_part, near_halo)

    def finish_fix(i, part, halo):
        body = functools.partial(finish_fix_body, i)
        args = (keep, part, halo, pair, gain, gain_kt)
        scratch = [tiles(rows, cols)] * 2
        return call(body, "finish_fix", [full], args, [SMEM] + [VMEM] * 5, scratch=scratch, work=8)[0]

    near = finish_fix(1, near_part, near_sums)
    far = finish_fix(0, far_part, far_sums)
    for sweep_index in range(SWEEPS - 2):
        far_halo, near_halo = swap_far(far), swap_near(near)
        far_part, near_part = part_of(far, near)
        far, near = finish(0, far_part, far_halo), finish(1, near_part, near_halo)

    far_halo, near_halo = swap_far(far), swap_near(near)
    far_part, near_part = part_of(far, near)
    outs = [(2, 2, rows, cols), full]
    scratch = [pltpu.VMEM(full, F32), pltpu.VMEM((rows, cols), F32), pltpu.SemaphoreType.DMA((4,))]
    args = (gain, gain_kt, phase_lin, phase_state)
    adjoint, design = call(
        last_near_body,
        "last_near",
        outs,
        (where, keep, near_part, near_halo, *args),
        [SMEM, SMEM] + [VMEM] * 6,
        [ANY, ANY],
        scratch,
        work=10,
    )
    adjoint, design = call(
        last_far_body,
        "last_far",
        outs,
        (where, keep, far_part, far_halo, *args, adjoint, design),
        [SMEM, SMEM] + [VMEM] * 6 + [ANY, ANY],
        [ANY, ANY],
        scratch,
        {8: 0, 9: 1},
        work=10,
    )
    return (adjoint, design)


def solution(mesh):
    in_specs = (
        P(("grp", "gx"), None, None),
        P(("grp", "gx"), None, None),
        P(None, ("grp", "gx"), None, None),
        P(None, ("grp", "gx"), None, None),
    )
    out_specs = (P(None, ("grp", "gx"), None, None), P(("grp", "gx"), None, None))
    return jax.shard_map(
        on_device, mesh=mesh, in_specs=in_specs, out_specs=out_specs, check_vma=False
    )
```

```python
import functools

import jax
import jax.numpy as jnp
from jax import lax
from jax.experimental import pallas as pl
from jax.experimental.pallas import tpu as pltpu
from jax.sharding import PartitionSpec as P

SWEEPS = 2
COARSE_SWEEPS = 4

GRADIENT_ENERGY = 1.0
TIME_STEP = 0.02
DAMPING = 0.8
KEEP = 1.0 - DAMPING
COARSE_ENERGY = GRADIENT_ENERGY / 4.0
COARSE_STEP = TIME_STEP / 4.0


VMEM = pl.BlockSpec(memory_space=pltpu.VMEM)
SMEM = pl.BlockSpec(memory_space=pltpu.SMEM)
ANY = pl.BlockSpec(memory_space=pl.ANY)
HBM = pl.BlockSpec(memory_space=pltpu.HBM)
BLOCK = 16
F32 = jnp.float32


def chip_pairs(count):
    return [(i, i ^ 1) for i in range(count)]


def cross_pairs(groups, count):
    pairs = []
    for g in range(groups):
        pairs += [(g * count + i, g * count + i + 1) for i in range(1, count - 1, 2)]
    for g in range(0, groups - 1, 2):
        pairs += [(g * count + i, (g + 1) * count + i) for i in (0, count - 1)]
    swaps = pairs + [(b, a) for a, b in pairs]
    if groups % 2 == 1:
        swaps += [((groups - 1) * count + i,) * 2 for i in (0, count - 1)]
    return swaps


def chunk_sizes(rows):
    return [rows // 2, rows // 2]


def call(body, name, outs, args, in_specs=None, out_specs=None, scratch=(), aliases=None, work=30):
    shapes = [jax.ShapeDtypeStruct(s, F32) for s in outs]
    return pl.pallas_call(
        body,
        out_shape=shapes,
        in_specs=in_specs or [VMEM] * len(args),
        out_specs=out_specs or [VMEM] * len(outs),
        scratch_shapes=list(scratch),
        input_output_aliases=aliases or {},
        name=name,
        cost_estimate=pl.CostEstimate(flops=work, bytes_accessed=work, transcendentals=0),
        compiler_params=pltpu.CompilerParams(vmem_limit_bytes=24 * 1024 * 1024),
    )(*args)


def blocks(rows):
    return range(0, rows, BLOCK)


def around(read, r, rows):
    x = read(r, r + BLOCK)
    cols = x.shape[-1]
    row = lax.broadcasted_iota(jnp.int32, x.shape, 0)
    col = lax.broadcasted_iota(jnp.int32, x.shape, 1)
    up = read(r - 1, r - 1 + BLOCK) if r > 0 else jnp.where(row == 0, 0.0, pltpu.roll(x, 1, 0))
    if r + BLOCK < rows:
        down = read(r + 1, r + 1 + BLOCK)
    else:
        down = jnp.where(row == BLOCK - 1, 0.0, pltpu.roll(x, BLOCK - 1, 0))
    left = jnp.where(col == 0, 0.0, pltpu.roll(x, 1, 1))
    right = jnp.where(col == cols - 1, 0.0, pltpu.roll(x, cols - 1, 1))
    return x, (up + down) + (left + right)


def reader(ref, *lead):
    return lambda lo, hi: ref[(*lead, slice(lo, hi))]


def add_terms(base_p, base_m, gain, gain_kt, nb_p, nb_m, energy, step):
    new_p = base_p - gain * (energy * nb_m) + gain_kt * nb_p
    new_m = base_m + gain * (step * nb_p + (6.0 * step * energy) * nb_m)
    return new_p, new_m


def parts3(x):
    high = x.astype(jnp.bfloat16)
    rest = x - high.astype(F32)
    middle = rest.astype(jnp.bfloat16)
    low = (rest - middle.astype(F32)).astype(jnp.bfloat16)
    return high, middle, low


def pair_cols(x, pair):
    return sum(jnp.dot(v, pair, preferred_element_type=F32) for v in parts3(x))


def copy_cols(x, pair):
    dims = (((1,), (1,)), ((), ()))
    return sum(lax.dot_general(v, pair, dims, preferred_element_type=F32) for v in parts3(x))


LANES = 128


def tiles(rows, cols):
    return pltpu.VMEM((cols // LANES, rows, LANES), F32)


def put_rows(ref, rows, x):
    for j in range(ref.shape[0]):
        ref[j, rows] = x[:, j * LANES : (j + 1) * LANES]


def get_rows(ref, rows):
    return jnp.concatenate([ref[j, rows] for j in range(ref.shape[0])], axis=1)


def even_odd(ref):
    half = ref.shape[1] // 2
    return pl.ds(0, half, stride=2), pl.ds(1, half, stride=2)


def pair_rows(ref):
    even, odd = even_odd(ref)
    return get_rows(ref, even) + get_rows(ref, odd)


def take_body(what, where, warm, *refs):
    outs, sems = refs[:-1], refs[-1]
    c = where[0]
    copies = []
    for n, ((is_near, lo), out) in enumerate(zip(what, outs)):
        plane = 1 - c if is_near else c
        rows = pl.ds(lo, out.shape[1])
        copies.append(pltpu.make_async_copy(warm.at[:, plane, rows], out, sems.at[n]))
        copies[-1].start()
    for copy in copies:
        copy.wait()


def setup_body(where, phi, cot, gain, gain_kt, own):
    c = where[0]
    for i in range(2):
        plane = c if i == 0 else 1 - c
        for r in blocks(phi.shape[1]):
            rows = slice(r, r + BLOCK)
            v = phi[plane, rows]
            k = 3.0 * v * v - 1.0 + 6.0 * GRADIENT_ENERGY
            g = DAMPING / (1.0 + 6.0 * TIME_STEP * k)
            s0, s1 = cot[0, plane, rows], cot[1, plane, rows]
            gain[i, rows] = g
            gain_kt[i, rows] = g * k * TIME_STEP
            own[i, 0, rows] = g * (s0 + k * s1)
            own[i, 1, rows] = g * (s1 - 6.0 * TIME_STEP * s0)


def coarse_setup_body(phi, pair, gain, gain_kt, both):
    for r in blocks(phi.shape[1]):
        rows = slice(r, r + BLOCK)
        a, b = phi[0, rows], phi[1, rows]
        put_rows(both, rows, (3.0 * a * a - 1.0) + (3.0 * b * b - 1.0))
    k = pair_cols(pair_rows(both), pair[...]) / 8.0 + 6.0 * COARSE_ENERGY
    g = DAMPING / (1.0 + 6.0 * COARSE_STEP * k)
    gain[...] = g
    gain_kt[...] = g * k * COARSE_STEP


def gather_rows(chunks, whole):
    lo = 0
    for chunk in chunks:
        n = chunk.shape[1]
        for r in blocks(n):
            for f in range(2):
                whole[f, slice(lo + r, lo + r + BLOCK)] = chunk[f, slice(r, r + BLOCK)]
        lo += n


def part_body(count, *refs):
    chunks, (near, gain, gain_kt, own, far_out, near_out, far) = refs[:count], refs[count:]
    gather_rows(chunks, far)
    rows_all = far.shape[1]
    for i, (mine, other, out) in enumerate(((far, near, far_out), (near, far, near_out))):
        for r in blocks(rows_all):
            rows = slice(r, r + BLOCK)
            p, nb_p = around(reader(mine, 0), r, rows_all)
            m, nb_m = around(reader(mine, 1), r, rows_all)
            out[0, rows], out[1, rows] = add_terms(
                KEEP * p + own[i, 0, rows],
                KEEP * m + own[i, 1, rows],
                gain[i, rows],
                gain_kt[i, rows],
                nb_p + other[0, rows],
                nb_m + other[1, rows],
                GRADIENT_ENERGY,
                TIME_STEP,
            )


def finish_body(i, lo, keep, part, halo, gain, gain_kt, out):
    for r in blocks(halo.shape[1]):
        rows, whole = slice(r, r + BLOCK), slice(lo + r, lo + r + BLOCK)
        hp, hm = halo[0, rows], halo[1, rows]
        if i == 0:
            hp, hm = hp * keep[0], hm * keep[0]
        out[0, rows], out[1, rows] = add_terms(
            part[0, whole], part[1, whole], gain[i, whole], gain_kt[i, whole], hp, hm, GRADIENT_ENERGY, TIME_STEP
        )


def finish_pool_body(i, lo, keep, part, halo, gain, gain_kt, pair, *refs):
    before, (pool, out, tile) = refs[:-3], refs[-3:]
    finish_body(i, lo, keep, part, halo, gain, gain_kt, out)
    for f in range(2):
        for r in blocks(out.shape[1]):
            rows = slice(r, r + BLOCK)
            put_rows(tile, rows, out[f, rows])
        for ref in before:
            pool[f, : lo // 2] = ref[f]
        pool[f, lo // 2 if before else 0 :] = pair_cols(pair_rows(tile), pair[...])


def three_body(count, *refs):
    chunks, (even_col, odd_col, first, second, third, tile) = refs[:count], refs[count:]
    for f in range(2):
        lo = 0
        for chunk in chunks:
            for r in blocks(chunk.shape[1]):
                put_rows(tile, slice(lo + r, lo + r + BLOCK), chunk[f, slice(r, r + BLOCK)])
            lo += chunk.shape[1]
        even, odd = even_odd(tile)
        top, bottom = get_rows(tile, even), get_rows(tile, odd)
        first[f] = pair_cols(top, even_col[...])
        second[f] = pair_cols(top, odd_col[...])
        third[f] = pair_cols(bottom, even_col[...])


def defect_body(count, where, *refs):
    chunks, (near, phi, cot, pair, out, far, total, tile) = refs[:count], refs[count:]
    gather_rows(chunks, far)
    c = where[0]
    rows_all = far.shape[1]
    for i, (mine, other) in enumerate(((far, near), (near, far))):
        plane = c if i == 0 else 1 - c
        for r in blocks(rows_all):
            rows = slice(r, r + BLOCK)
            p, nb_p = around(reader(mine, 0), r, rows_all)
            m, nb_m = around(reader(mine, 1), r, rows_all)
            v = phi[plane, rows]
            lap_p = nb_p + other[0, rows] - 6.0 * p
            lap_m = nb_m + other[1, rows] - 6.0 * m
            r0 = cot[0, plane, rows] - (p - (3.0 * v * v - 1.0) * m + GRADIENT_ENERGY * lap_m)
            r1 = cot[1, plane, rows] - (m - TIME_STEP * lap_p)
            total[0, rows] = r0 if i == 0 else total[0, rows] + r0
            total[1, rows] = r1 if i == 0 else total[1, rows] + r1
    for f in range(2):
        for r in blocks(rows_all):
            rows = slice(r, r + BLOCK)
            put_rows(tile, rows, total[f, rows])
        out[f] = pair_cols(pair_rows(tile), pair[...]) / 8.0


def coarse_first_body(keep, local, far, near, gain, gain_kt, out):
    for r in blocks(local.shape[1]):
        rows = slice(r, r + BLOCK)
        s0 = local[0, rows] - (GRADIENT_ENERGY / 8.0) * (far[1, rows] * keep[0] + near[1, rows])
        s1 = local[1, rows] + (TIME_STEP / 8.0) * (far[0, rows] * keep[0] + near[0, rows])
        g = gain[rows]
        out[0, rows] = g * s0 + (gain_kt[rows] / COARSE_STEP) * s1
        out[1, rows] = g * (s1 - 6.0 * COARSE_STEP * s0)


def coarse_part_body(fix, own, gain, gain_kt, out):
    rows_all = fix.shape[1]
    for r in blocks(rows_all):
        rows = slice(r, r + BLOCK)
        p, nb_p = around(reader(fix, 0), r, rows_all)
        m, nb_m = around(reader(fix, 1), r, rows_all)
        out[0, rows], out[1, rows] = add_terms(
            KEEP * p + own[0, rows],
            KEEP * m + own[1, rows],
            gain[rows],
            gain_kt[rows],
            nb_p,
            nb_m,
            COARSE_ENERGY,
            COARSE_STEP,
        )


def coarse_finish_body(keep, part, far, near, gain, gain_kt, out):
    for r in blocks(part.shape[1]):
        rows = slice(r, r + BLOCK)
        out[0, rows], out[1, rows] = add_terms(
            part[0, rows],
            part[1, rows],
            gain[rows],
            gain_kt[rows],
            far[0, rows] * keep[0] + near[0, rows],
            far[1, rows] * keep[0] + near[1, rows],
            COARSE_ENERGY,
            COARSE_STEP,
        )


def spread_into(tile, fix, pair):
    wide = copy_cols(fix, pair)
    for rows in even_odd(tile):
        put_rows(tile, rows, wide)


def third_body(count, keep, *refs):
    chunks, refs = refs[:count], refs[count:]
    near, fix, near_halo, sums, first, second, third, pair, even_col, odd_col, gain, gain_kt, own = refs[:13]
    far_out, near_out, far_fixed, near_fixed, tile, phase, chem = refs[13:]
    rows_all = near.shape[1]
    gather_rows(chunks, far_fixed)
    for f, halo in enumerate((phase, chem)):
        spread_into(tile, fix[f], pair[...])
        for r in blocks(rows_all):
            rows = slice(r, r + BLOCK)
            wide = get_rows(tile, rows)
            far_fixed[f, rows] = far_fixed[f, rows] + wide
            near_fixed[f, rows] = near[f, rows] + wide
        even, odd = even_odd(halo)
        a, b, c = first[f], second[f], third[f]
        d = sums[f] - ((a + b) + c)
        put_rows(halo, even, copy_cols(a, even_col[...]) + copy_cols(b, odd_col[...]))
        put_rows(halo, odd, copy_cols(c, even_col[...]) + copy_cols(d, odd_col[...]))
    for i, (mine, other, out) in enumerate(((far_fixed, near_fixed, far_out), (near_fixed, far_fixed, near_out))):
        for r in blocks(rows_all):
            rows = slice(r, r + BLOCK)
            p, nb_p = around(reader(mine, 0), r, rows_all)
            m, nb_m = around(reader(mine, 1), r, rows_all)
            if i == 0:
                hp, hm = get_rows(phase, rows) * keep[0], get_rows(chem, rows) * keep[0]
            else:
                hp, hm = near_halo[0, rows], near_halo[1, rows]
            out[0, rows], out[1, rows] = add_terms(
                KEEP * p + own[i, 0, rows],
                KEEP * m + own[i, 1, rows],
                gain[i, rows],
                gain_kt[i, rows],
                nb_p + other[0, rows] + hp,
                nb_m + other[1, rows] + hm,
                GRADIENT_ENERGY,
                TIME_STEP,
            )


def finish_fix_body(i, lo, keep, part, halo, pair, gain, gain_kt, out, phase, chem):
    n = out.shape[1]
    coarse = slice(lo // 2, (lo + n) // 2)
    spread_into(phase, halo[0, coarse], pair[...])
    spread_into(chem, halo[1, coarse], pair[...])
    for r in blocks(n):
        rows, whole = slice(r, r + BLOCK), slice(lo + r, lo + r + BLOCK)
        hp, hm = get_rows(phase, rows), get_rows(chem, rows)
        if i == 0:
            hp, hm = hp * keep[0], hm * keep[0]
        out[0, rows], out[1, rows] = add_terms(
            part[0, whole], part[1, whole], gain[i, whole], gain_kt[i, whole], hp, hm, GRADIENT_ENERGY, TIME_STEP
        )


def final_body(i, lo, where, keep, part, halo, gain, gain_kt, phi, psi, *refs):
    adjoint, design, plane_out, grad_out, sems = refs[-5:]
    c = where[0]
    plane = c if i == 0 else 1 - c
    rows_all = halo.shape[1]
    step = rows_all // 2
    copies = []
    for n, start in enumerate(range(0, rows_all, step)):
        for r in range(start, start + step, BLOCK):
            rows, whole = slice(r, r + BLOCK), slice(lo + r, lo + r + BLOCK)
            hp, hm = halo[0, rows], halo[1, rows]
            if i == 0:
                hp, hm = hp * keep[0], hm * keep[0]
            p, m = add_terms(
                part[0, whole], part[1, whole], gain[i, whole], gain_kt[i, whole], hp, hm, GRADIENT_ENERGY, TIME_STEP
            )
            plane_out[0, rows] = p
            plane_out[1, rows] = m
            grad_out[rows] = 6.0 * phi[plane, whole] * psi[plane, whole] * m
        here, there = pl.ds(start, step), pl.ds(lo + start, step)
        copies.append(pltpu.make_async_copy(plane_out.at[:, here], adjoint.at[:, plane, there], sems.at[2 * n]))
        copies.append(pltpu.make_async_copy(grad_out.at[here], design.at[plane, there], sems.at[2 * n + 1]))
        copies[-2].start()
        copies[-1].start()
    for copy in copies:
        copy.wait()


def on_device(phase_lin, phase_state, cotangent, warm_start):
    groups, count = lax.axis_size("grp"), lax.axis_size("gx")
    me = lax.axis_index("gx")
    where = jnp.reshape(me % 2, (1,)).astype(jnp.int32)
    keep = jnp.reshape(((me > 0) & (me < count - 1)).astype(F32), (1,))
    across, on_chip = cross_pairs(groups, count), chip_pairs(count)
    rows, cols = phase_lin.shape[1:]
    full, half = (2, rows, cols), (2, rows // 2, cols // 2)
    sizes = chunk_sizes(rows)
    starts = [sum(sizes[:n]) for n in range(len(sizes))]
    chunked = [(2, n, cols) for n in sizes]

    cell = lax.broadcasted_iota(jnp.int32, (cols, cols // 2), 0)
    pairs = 2 * lax.broadcasted_iota(jnp.int32, (cols, cols // 2), 1)
    even_col, odd_col = (cell == pairs).astype(jnp.bfloat16), (cell == pairs + 1).astype(jnp.bfloat16)
    pair = ((cell == pairs) | (cell == pairs + 1)).astype(jnp.bfloat16)

    def swap_far(x):
        return lax.ppermute(x, ("grp", "gx"), across)

    def swap_near(x):
        return lax.ppermute(x, "gx", on_chip)

    def run(body, name, outs, args, statics=(), smem=0, **kw):
        specs = [SMEM] * smem + [VMEM] * (len(args) - smem)
        return call(functools.partial(body, *statics), name, outs, args, specs, **kw)

    def take(what, name):
        outs = [(2, n, cols) for _, _, n in what]
        body = functools.partial(take_body, [(is_near, lo) for is_near, lo, _ in what])
        scratch = [pltpu.SemaphoreType.DMA((len(what),))]
        return call(body, name, outs, (where, warm_start), [SMEM, HBM], scratch=scratch, work=0)

    far = take([(False, starts[0], sizes[0])], "take_first")
    *rest, near = take([(False, lo, n) for lo, n in zip(starts[1:], sizes[1:])] + [(True, 0, rows)], "take_rest")
    far = list(far) + rest
    far_halo, near_halo = [swap_far(v) for v in far], swap_near(near)
    gain, gain_kt, own = run(setup_body, "setup", [full, full, (2, 2, rows, cols)], (where, phase_lin, cotangent), smem=1)
    coefs = (gain, gain_kt)

    def part_of(far, near):
        args = (*far, near, gain, gain_kt, own)
        return run(part_body, "part", [full, full], args, (len(far),), scratch=[pltpu.VMEM(full, F32)])

    def finish(i, lo, part, halo):
        shape = (2, halo.shape[1], cols)
        return run(finish_body, "finish", [shape], (keep, part, halo, *coefs), (i, lo), smem=1, work=8)[0]

    far_part, near_part = part_of(far, near)
    near = finish(1, 0, near_part, near_halo)
    far = [finish(0, lo, far_part, halo) for lo, halo in zip(starts, far_halo)]

    far_halo, near_halo = [swap_far(v) for v in far], swap_near(near)
    far_part, near_part = part_of(far, near)
    coarse = run(coarse_setup_body, "coarse_setup", [half[1:], half[1:]], (phase_lin, pair), scratch=[tiles(rows, cols)])

    def finish_pool(i, lo, part, halo, before=()):
        n = halo.shape[1]
        pool = (2, (n + (lo if before else 0)) // 2, cols // 2)
        args = (keep, part, halo, *coefs, pair, *before)
        outs, scratch = [pool, (2, n, cols)], [tiles(n, cols)]
        return run(finish_pool_body, "finish_pool", outs, args, (i, lo), smem=1, scratch=scratch, work=8)

    near_pool, near = finish_pool(1, 0, near_part, near_halo)
    far, before = [], ()
    for lo, halo in zip(starts, far_halo):
        far_pool, chunk = finish_pool(0, lo, far_part, halo, before)
        far.append(chunk)
        before = (far_pool,)

    far_sums, near_sums = swap_far(far_pool), swap_near(near_pool)
    plane_sums = far_sums
    near_halo = swap_near(near)
    args = (*far, even_col, odd_col)
    pieces = run(three_body, "three", [half] * 3, args, (len(far),), scratch=[tiles(rows, cols)])
    arrived = [swap_far(pieces[0])]
    args = (where, *far, near, phase_lin, cotangent, pair)
    scratch = [pltpu.VMEM(full, F32), pltpu.VMEM(full, F32), tiles(rows, cols)]
    local = run(defect_body, "defect", [half], args, (len(far),), smem=1, scratch=scratch)[0]
    fix = run(coarse_first_body, "coarse_first", [half], (keep, local, far_sums, near_sums, *coarse), smem=1, work=8)[0]
    first = fix
    for sweep_index in range(COARSE_SWEEPS - 1):
        far_sums, near_sums = swap_far(fix), swap_near(fix)
        if len(arrived) < len(pieces):
            fix, held = lax.optimization_barrier((fix, pieces[len(arrived)]))
            arrived.append(swap_far(held))
        part = run(coarse_part_body, "coarse_part", [half], (fix, first, *coarse))[0]
        part, arrived[sweep_index] = lax.optimization_barrier((part, arrived[sweep_index]))
        args = (keep, part, far_sums, near_sums, *coarse)
        fix = run(coarse_finish_body, "coarse_finish", [half], args, smem=1, work=8)[0]

    far_sums, near_sums = swap_far(fix), swap_near(fix)
    args = (keep, *far, near, fix, near_halo, plane_sums, *arrived, pair, even_col, odd_col, *coefs, own)
    scratch = [pltpu.VMEM(full, F32)] * 2 + [tiles(rows, cols)] * 3
    far_part, near_part = run(third_body, "third", [full, full], args, (len(far),), smem=1, scratch=scratch)

    def finish_fix(i, lo, n, part, halo):
        args, scratch = (keep, part, halo, pair, *coefs), [tiles(n, cols)] * 2
        return run(finish_fix_body, "finish_fix", [(2, n, cols)], args, (i, lo), smem=1, scratch=scratch, work=8)[0]

    far = [finish_fix(0, lo, n, far_part, far_sums) for lo, n in zip(starts, sizes)]
    near_sums, far[-1] = lax.optimization_barrier((near_sums, far[-1]))
    near = finish_fix(1, 0, rows, near_part, near_sums)

    far_halo, near_halo = [swap_far(v) for v in far], swap_near(near)
    far_part, near_part = part_of(far, near)
    outs = [(2, 2, rows, cols), full]

    def final(i, lo, part, halo, done):
        n = halo.shape[1]
        args = (where, keep, part, halo, *coefs, phase_lin, phase_state, *done)
        in_specs = [SMEM, SMEM] + [VMEM] * 6 + [ANY] * len(done)
        scratch = [pltpu.VMEM((2, n, cols), F32), pltpu.VMEM((n, cols), F32), pltpu.SemaphoreType.DMA((4,))]
        body = functools.partial(final_body, i, lo)
        aliases = {8: 0, 9: 1} if done else None
        return call(body, "final", outs, args, in_specs, [ANY, ANY], scratch, aliases, work=10)

    done = final(1, 0, near_part, near_halo, ())
    for lo, halo in zip(starts, far_halo):
        done = final(0, lo, far_part, halo, done)
    return tuple(done)


def solution(mesh):
    in_specs = (
        P(("grp", "gx"), None, None),
        P(("grp", "gx"), None, None),
        P(None, ("grp", "gx"), None, None),
        P(None, ("grp", "gx"), None, None),
    )
    out_specs = (P(None, ("grp", "gx"), None, None), P(("grp", "gx"), None, None))
    return jax.shard_map(
        on_device, mesh=mesh, in_specs=in_specs, out_specs=out_specs, check_vma=False
    )
```

```python
import functools

import jax
import jax.numpy as jnp
from jax import lax
from jax.experimental import pallas as pl
from jax.experimental.pallas import tpu as pltpu
from jax.sharding import PartitionSpec as P

SWEEPS = 2
COARSE_SWEEPS = 4

GRADIENT_ENERGY = 1.0
TIME_STEP = 0.02
DAMPING = 0.8
KEEP = 1.0 - DAMPING
COARSE_ENERGY = GRADIENT_ENERGY / 4.0
COARSE_STEP = TIME_STEP / 4.0


VMEM = pl.BlockSpec(memory_space=pltpu.VMEM)
SMEM = pl.BlockSpec(memory_space=pltpu.SMEM)
ANY = pl.BlockSpec(memory_space=pl.ANY)
HBM = pl.BlockSpec(memory_space=pltpu.HBM)
BLOCK = 16
F32 = jnp.float32


def chip_pairs(count):
    return [(i, i ^ 1) for i in range(count)]


def cross_pairs(groups, count):
    pairs = []
    for g in range(groups):
        pairs += [(g * count + i, g * count + i + 1) for i in range(1, count - 1, 2)]
    for g in range(0, groups - 1, 2):
        pairs += [(g * count + i, (g + 1) * count + i) for i in (0, count - 1)]
    swaps = pairs + [(b, a) for a, b in pairs]
    if groups % 2 == 1:
        swaps += [((groups - 1) * count + i,) * 2 for i in (0, count - 1)]
    return swaps


def early_chunks(rows):
    return [rows // 2, rows // 2]


def late_chunks(rows):
    return [rows]


def call(body, name, outs, args, in_specs=None, out_specs=None, scratch=(), aliases=None, work=30, dtype=F32):
    shapes = [jax.ShapeDtypeStruct(s, dtype) for s in outs]
    size = sum(int(a.size) for a in args)
    made = sum(s.size for s in shapes)
    return pl.pallas_call(
        body,
        out_shape=shapes,
        in_specs=in_specs or [VMEM] * len(args),
        out_specs=out_specs or [VMEM] * len(outs),
        scratch_shapes=list(scratch),
        input_output_aliases=aliases or {},
        name=name,
        cost_estimate=pl.CostEstimate(flops=0, bytes_accessed=4 * (size + made), transcendentals=0),
        compiler_params=pltpu.CompilerParams(vmem_limit_bytes=12 * 1024 * 1024),
    )(*args)


def blocks(rows):
    return range(0, rows, BLOCK)


def around(read, r, rows):
    x = read(r, r + BLOCK)
    cols = x.shape[-1]
    row = lax.broadcasted_iota(jnp.int32, x.shape, 0)
    col = lax.broadcasted_iota(jnp.int32, x.shape, 1)
    up = read(r - 1, r - 1 + BLOCK) if r > 0 else jnp.where(row == 0, 0.0, pltpu.roll(x, 1, 0))
    if r + BLOCK < rows:
        down = read(r + 1, r + 1 + BLOCK)
    else:
        down = jnp.where(row == BLOCK - 1, 0.0, pltpu.roll(x, BLOCK - 1, 0))
    left = jnp.where(col == 0, 0.0, pltpu.roll(x, 1, 1))
    right = jnp.where(col == cols - 1, 0.0, pltpu.roll(x, cols - 1, 1))
    return x, (up + down) + (left + right)


def reader(ref, *lead):
    return lambda lo, hi: ref[(*lead, slice(lo, hi))]


def add_terms(base_p, base_m, gain, nb_p, nb_m, energy, step):
    gain_kt = (DAMPING - gain) * (1.0 / 6.0)
    new_p = base_p - gain * (energy * nb_m) + gain_kt * nb_p
    new_m = base_m + gain * (step * nb_p + (6.0 * step * energy) * nb_m)
    return new_p, new_m


def parts3(x):
    high = x.astype(jnp.bfloat16)
    rest = x - high.astype(F32)
    middle = rest.astype(jnp.bfloat16)
    low = (rest - middle.astype(F32)).astype(jnp.bfloat16)
    return high, middle, low


def times(xs, matrix):
    n, width = xs[0].shape[0], matrix.shape[0]
    pieces = [x[:, j : j + width] for x in xs for j in range(0, x.shape[1], width)]
    stacked = jnp.concatenate([v for piece in pieces for v in parts3(piece)], axis=0)
    out = jnp.dot(stacked, matrix, preferred_element_type=F32)
    sums = [out[j : j + n] + out[j + n : j + 2 * n] + out[j + 2 * n : j + 3 * n] for j in range(0, out.shape[0], 3 * n)]
    each = len(sums) // len(xs)
    return [jnp.concatenate(sums[j : j + each], axis=1) for j in range(0, len(sums), each)]


LANES = 128


def tiles(rows, cols):
    return pltpu.VMEM((cols // LANES, rows, LANES), F32)


def put_rows(ref, rows, x):
    for j in range(ref.shape[0]):
        ref[j, rows] = x[:, j * LANES : (j + 1) * LANES]


def get_rows(ref, rows):
    return jnp.concatenate([ref[j, rows] for j in range(ref.shape[0])], axis=1)


def even_odd(ref):
    half = ref.shape[1] // 2
    return pl.ds(0, half, stride=2), pl.ds(1, half, stride=2)


def pair_rows(ref):
    even, odd = even_odd(ref)
    return get_rows(ref, even) + get_rows(ref, odd)


def take_body(what, where, warm, *refs):
    outs, sems = refs[:-1], refs[-1]
    c = where[0]
    copies = []
    for n, ((is_near, lo), out) in enumerate(zip(what, outs)):
        plane = 1 - c if is_near else c
        rows = pl.ds(lo, out.shape[1])
        copies.append(pltpu.make_async_copy(warm.at[:, plane, rows], out, sems.at[n]))
        copies[-1].start()
    for copy in copies:
        copy.wait()


def matrices_body(where, pair, even_col, odd_col, pair_t, even_t, odd_t):
    for dim, (both, even, odd) in enumerate(((pair, even_col, odd_col), (pair_t, even_t, odd_t))):
        cell = lax.broadcasted_iota(jnp.int32, both.shape, dim)
        coarse = 2 * lax.broadcasted_iota(jnp.int32, both.shape, 1 - dim)
        is_even = jnp.where(cell == coarse, 1.0, 0.0)
        is_odd = jnp.where(cell == coarse + 1, 1.0, 0.0)
        even[...] = is_even.astype(jnp.bfloat16)
        odd[...] = is_odd.astype(jnp.bfloat16)
        both[...] = (is_even + is_odd).astype(jnp.bfloat16)


def setup_body(where, phi, cot, gain, own):
    c = where[0]
    for i in range(2):
        plane = c if i == 0 else 1 - c
        for r in blocks(phi.shape[1]):
            rows = slice(r, r + BLOCK)
            v = phi[plane, rows]
            k = 3.0 * v * v - 1.0 + 6.0 * GRADIENT_ENERGY
            g = DAMPING / (1.0 + 6.0 * TIME_STEP * k)
            s0, s1 = cot[0, plane, rows], cot[1, plane, rows]
            gain[i, rows] = g
            own[i, 0, rows] = g * (s0 + k * s1)
            own[i, 1, rows] = g * (s1 - 6.0 * TIME_STEP * s0)


def coarse_setup_body(phi, pair, gain, both):
    for r in blocks(phi.shape[1]):
        rows = slice(r, r + BLOCK)
        a, b = phi[0, rows], phi[1, rows]
        put_rows(both, rows, (3.0 * a * a - 1.0) + (3.0 * b * b - 1.0))
    k = times([pair_rows(both)], pair[...])[0] / 8.0 + 6.0 * COARSE_ENERGY
    gain[...] = DAMPING / (1.0 + 6.0 * COARSE_STEP * k)


def gather_rows(chunks, whole):
    lo = 0
    for chunk in chunks:
        n = chunk.shape[1]
        for r in blocks(n):
            for f in range(2):
                whole[f, slice(lo + r, lo + r + BLOCK)] = chunk[f, slice(r, r + BLOCK)]
        lo += n


def part_body(count, *refs):
    chunks, (near, gain, own, far_out, near_out, far) = refs[:count], refs[count:]
    gather_rows(chunks, far)
    rows_all = far.shape[1]
    for i, (mine, other, out) in enumerate(((far, near, far_out), (near, far, near_out))):
        for r in blocks(rows_all):
            rows = slice(r, r + BLOCK)
            p, nb_p = around(reader(mine, 0), r, rows_all)
            m, nb_m = around(reader(mine, 1), r, rows_all)
            out[0, rows], out[1, rows] = add_terms(
                KEEP * p + own[i, 0, rows],
                KEEP * m + own[i, 1, rows],
                gain[i, rows],
                nb_p + other[0, rows],
                nb_m + other[1, rows],
                GRADIENT_ENERGY,
                TIME_STEP,
            )


def finish_body(i, lo, keep, part, halo, gain, out):
    for r in blocks(halo.shape[1]):
        rows, whole = slice(r, r + BLOCK), slice(lo + r, lo + r + BLOCK)
        hp, hm = halo[0, rows], halo[1, rows]
        if i == 0:
            hp, hm = hp * keep[0], hm * keep[0]
        out[0, rows], out[1, rows] = add_terms(
            part[0, whole], part[1, whole], gain[i, whole], hp, hm, GRADIENT_ENERGY, TIME_STEP
        )


def finish_pool_body(i, lo, keep, part, halo, gain, pair, *refs):
    before, (pool, out, phase, chem) = refs[:-4], refs[-4:]
    for r in blocks(halo.shape[1]):
        rows, whole = slice(r, r + BLOCK), slice(lo + r, lo + r + BLOCK)
        hp, hm = halo[0, rows], halo[1, rows]
        if i == 0:
            hp, hm = hp * keep[0], hm * keep[0]
        p, m = add_terms(
            part[0, whole], part[1, whole], gain[i, whole], hp, hm, GRADIENT_ENERGY, TIME_STEP
        )
        out[0, rows] = p
        out[1, rows] = m
        put_rows(phase, rows, p)
        put_rows(chem, rows, m)
    sums = times([pair_rows(phase), pair_rows(chem)], pair[...])
    for f in range(2):
        for ref in before:
            pool[f, : lo // 2] = ref[f]
        pool[f, lo // 2 if before else 0 :] = sums[f]


def three_body(count, *refs):
    chunks, (even_col, odd_col), outs, tile = refs[:count], refs[count : count + 2], refs[count + 2 : -1], refs[-1]
    for f in range(2):
        lo = 0
        for chunk in chunks:
            for r in blocks(chunk.shape[1]):
                put_rows(tile, slice(lo + r, lo + r + BLOCK), chunk[f, slice(r, r + BLOCK)])
            lo += chunk.shape[1]
        even, odd = even_odd(tile)
        top, bottom = get_rows(tile, even), get_rows(tile, odd)
        first, third = times([top, bottom], even_col[...])
        second = times([top], odd_col[...])[0]
        values = jnp.concatenate([first, second, third], axis=0)
        n = values.shape[0] // len(outs)
        for j, out in enumerate(outs):
            out[f] = values[j * n : (j + 1) * n]


def part_defect_body(count, *refs):
    chunks, (near, gain, own, pair, far_out, near_out, out, far, phase, chem) = refs[:count], refs[count:]
    part_body(count, *chunks, near, gain, own, far_out, near_out, far)
    for r in blocks(near.shape[1]):
        rows = slice(r, r + BLOCK)
        r0, r1 = 0.0, 0.0
        for i, (mine, new) in enumerate(((far, far_out), (near, near_out))):
            dp, dm = new[0, rows] - mine[0, rows], new[1, rows] - mine[1, rows]
            k = (DAMPING - gain[i, rows]) / (6.0 * TIME_STEP * gain[i, rows])
            r0 = r0 + (dp - k * dm)
            r1 = r1 + (dm + 6.0 * TIME_STEP * dp)
        put_rows(phase, rows, r0)
        put_rows(chem, rows, r1)
    sums = times([pair_rows(phase), pair_rows(chem)], pair[...])
    for f in range(2):
        out[f] = sums[f] * (1.0 / (8.0 * DAMPING))


def coarse_first_body(keep, local, far, near, gain, out):
    for r in blocks(local.shape[1]):
        rows = slice(r, r + BLOCK)
        s0 = local[0, rows] - (GRADIENT_ENERGY / 8.0) * (far[1, rows] * keep[0] + near[1, rows])
        s1 = local[1, rows] + (TIME_STEP / 8.0) * (far[0, rows] * keep[0] + near[0, rows])
        g = gain[rows]
        out[0, rows] = g * s0 + ((DAMPING - g) * (1.0 / (6.0 * COARSE_STEP))) * s1
        out[1, rows] = g * (s1 - 6.0 * COARSE_STEP * s0)


def coarse_part_body(fix, own, gain, out):
    rows_all = fix.shape[1]
    for r in blocks(rows_all):
        rows = slice(r, r + BLOCK)
        p, nb_p = around(reader(fix, 0), r, rows_all)
        m, nb_m = around(reader(fix, 1), r, rows_all)
        out[0, rows], out[1, rows] = add_terms(
            KEEP * p + own[0, rows],
            KEEP * m + own[1, rows],
            gain[rows],
            nb_p,
            nb_m,
            COARSE_ENERGY,
            COARSE_STEP,
        )


def coarse_finish_body(keep, part, far, near, gain, out):
    for r in blocks(part.shape[1]):
        rows = slice(r, r + BLOCK)
        out[0, rows], out[1, rows] = add_terms(
            part[0, rows],
            part[1, rows],
            gain[rows],
            far[0, rows] * keep[0] + near[0, rows],
            far[1, rows] * keep[0] + near[1, rows],
            COARSE_ENERGY,
            COARSE_STEP,
        )


def spread_into(tile_a, tile_b, fix_a, fix_b, pair_t):
    for tile, wide in zip((tile_a, tile_b), times([fix_a, fix_b], pair_t)):
        for rows in even_odd(tile):
            put_rows(tile, rows, wide)


def third_body(count, keep, *refs):
    far, near, fix, near_halo, sums = refs[:5]
    pieces, refs = refs[5 : 5 + count], refs[5 + count :]
    pair_t, even_t, odd_t, gain, far_out, near_out, fix_p, fix_m, halo_p, halo_m, wide_p, wide_m = refs
    rows_all = near.shape[1]
    half = rows_all // 2
    spread_into(fix_p, fix_m, fix[0], fix[1], pair_t[...])
    for f, tile in enumerate((halo_p, halo_m)):
        values = jnp.concatenate([piece[f] for piece in pieces], axis=0)
        a, b, c = values[:half], values[half : 2 * half], values[2 * half :]
        d = sums[f] - ((a + b) + c)
        even, odd = even_odd(tile)
        (a, c), (b, d) = times([a, c], even_t[...]), times([b, d], odd_t[...])
        put_rows(tile, even, a + b)
        put_rows(tile, odd, c + d)
    for r in blocks(rows_all):
        rows = slice(r, r + BLOCK)
        wide_p[rows], wide_m[rows] = get_rows(fix_p, rows), get_rows(fix_m, rows)
    for r in blocks(rows_all):
        rows = slice(r, r + BLOCK)
        p, nb_p = around(lambda lo, hi: wide_p[lo:hi], r, rows_all)
        m, nb_m = around(lambda lo, hi: wide_m[lo:hi], r, rows_all)
        nb_p, nb_m = nb_p + p, nb_m + m
        hp, hm = get_rows(halo_p, rows) * keep[0], get_rows(halo_m, rows) * keep[0]
        for i, (part, out, xp, xm) in enumerate(
            ((far, far_out, hp, hm), (near, near_out, near_halo[0, rows], near_halo[1, rows]))
        ):
            out[0, rows], out[1, rows] = add_terms(
                part[0, rows] + KEEP * p,
                part[1, rows] + KEEP * m,
                gain[i, rows],
                nb_p + xp,
                nb_m + xm,
                GRADIENT_ENERGY,
                TIME_STEP,
            )


def finish_fix_rows(i, lo, keep, part, halo, pair_t, gain, out, phase, chem):
    n = out.shape[1]
    coarse = slice(lo // 2, (lo + n) // 2)
    spread_into(phase, chem, halo[0, coarse], halo[1, coarse], pair_t[...])
    for r in blocks(n):
        rows, whole = slice(r, r + BLOCK), slice(lo + r, lo + r + BLOCK)
        hp, hm = get_rows(phase, rows), get_rows(chem, rows)
        if i == 0:
            hp, hm = hp * keep[0], hm * keep[0]
        out[0, rows], out[1, rows] = add_terms(
            part[0, whole], part[1, whole], gain[i, whole], hp, hm, GRADIENT_ENERGY, TIME_STEP
        )


def fix_body(starts, keep, far_part, near_part, far_halo, near_halo, pair_t, gain, *refs):
    count = len(starts)
    outs, scratch = refs[: count + 1], refs[count + 1 :]
    for n, (lo, out) in enumerate(zip(starts, outs)):
        finish_fix_rows(0, lo, keep, far_part, far_halo, pair_t, gain, out, *scratch[2 * n : 2 * n + 2])
    finish_fix_rows(1, 0, keep, near_part, near_halo, pair_t, gain, outs[-1], *scratch[-2:])


def final_rows(i, lo, where, keep, part, halo, gain, phi, psi, adjoint, design, plane_out, grad_out, sems):
    c = where[0]
    plane = c if i == 0 else 1 - c
    rows_all = halo.shape[1]
    step = rows_all // 2
    copies = []
    for n, start in enumerate(range(0, rows_all, step)):
        for r in range(start, start + step, BLOCK):
            rows, whole = slice(r, r + BLOCK), slice(lo + r, lo + r + BLOCK)
            hp, hm = halo[0, rows], halo[1, rows]
            if i == 0:
                hp, hm = hp * keep[0], hm * keep[0]
            p, m = add_terms(
                part[0, whole], part[1, whole], gain[i, whole], hp, hm, GRADIENT_ENERGY, TIME_STEP
            )
            plane_out[0, rows] = p
            plane_out[1, rows] = m
            grad_out[rows] = 6.0 * phi[plane, whole] * psi[plane, whole] * m
        here, there = pl.ds(start, step), pl.ds(lo + start, step)
        copies.append(pltpu.make_async_copy(plane_out.at[:, here], adjoint.at[:, plane, there], sems.at[2 * n]))
        copies.append(pltpu.make_async_copy(grad_out.at[here], design.at[plane, there], sems.at[2 * n + 1]))
        copies[-2].start()
        copies[-1].start()
    return copies


def final_body(which, where, keep, gain, phi, psi, *refs):
    count = len(which)
    halos, refs = refs[: 2 * count], refs[2 * count :]
    scratch = refs[-3 * count :]
    adjoint, design = refs[-3 * count - 2 : -3 * count]
    copies = []
    for n, (i, lo) in enumerate(which):
        part, halo = halos[2 * n : 2 * n + 2]
        copies += final_rows(
            i, lo, where, keep, part, halo, gain, phi, psi, adjoint, design, *scratch[3 * n : 3 * n + 3]
        )
    for copy in copies:
        copy.wait()


def on_device(phase_lin, phase_state, cotangent, warm_start):
    groups, count = lax.axis_size("grp"), lax.axis_size("gx")
    me = lax.axis_index("gx")
    where = jnp.reshape(me % 2, (1,)).astype(jnp.int32)
    keep = jnp.reshape(((me > 0) & (me < count - 1)).astype(F32), (1,))
    across, on_chip = cross_pairs(groups, count), chip_pairs(count)
    rows, cols = phase_lin.shape[1:]
    full, half = (2, rows, cols), (2, rows // 2, cols // 2)
    sizes = early_chunks(rows)
    starts = [sum(sizes[:n]) for n in range(len(sizes))]

    def swap_far(x):
        return lax.ppermute(x, ("grp", "gx"), across)

    def swap_near(x):
        return lax.ppermute(x, "gx", on_chip)

    def after(x, y):
        return lax.optimization_barrier((x, y))

    whole, tile = pltpu.VMEM(full, F32), tiles(rows, cols)

    def run(body, name, outs, args, statics=(), smem=0, **kw):
        specs = [SMEM] * smem + [VMEM] * (len(args) - smem)
        return call(functools.partial(body, *statics), name, outs, args, specs, **kw)

    def take(what, name):
        outs = [(2, n, cols) for _, _, n in what]
        body = functools.partial(take_body, [(is_near, lo) for is_near, lo, _ in what])
        scratch = [pltpu.SemaphoreType.DMA((len(what),))]
        source = pltpu.with_memory_space_constraint(warm_start, pltpu.HBM)
        return call(body, name, outs, (where, source), [SMEM, HBM], scratch=scratch, work=0)

    *far, near = take([(False, lo, n) for lo, n in zip(starts, sizes)] + [(True, 0, rows)], "take")
    far_halo = [swap_far(v) for v in far]
    near_halo = swap_near(near)
    gain, own = run(setup_body, "setup", [full, (2, 2, rows, cols)], (where, phase_lin, cotangent), smem=1)
    coefs = (gain,)
    far_part, near_part = run(part_body, "part", [full] * 2, (*far, near, *coefs, own), (len(far),), scratch=[whole])
    def finish(i, lo, part, halo):
        shape = (2, halo.shape[1], cols)
        return run(finish_body, "finish", [shape], (keep, part, halo, *coefs), (i, lo), smem=1, work=8)[0]

    far = [finish(0, lo, far_part, halo) for lo, halo in zip(starts, far_halo)]
    near_halo, far[-1] = after(near_halo, far[-1])
    near = finish(1, 0, near_part, near_halo)
    later, far[-1] = after(where, far[-1])
    shapes = [(2 * LANES, LANES)] * 3 + [(LANES, 2 * LANES)] * 3
    matrices = run(matrices_body, "matrices", shapes, (later,), smem=1, dtype=jnp.bfloat16)
    pair, even_col, odd_col, pair_t, even_t, odd_t = matrices
    coarse = run(coarse_setup_body, "coarse_setup", [half[1:]], (phase_lin, pair), scratch=[tile])

    far_halo = [swap_far(v) for v in far]
    near_halo = swap_near(near)
    far_part, near_part = run(part_body, "part", [full] * 2, (*far, near, *coefs, own), (len(far),), scratch=[whole])

    def finish_pool(i, lo, part, halo, before=()):
        n = halo.shape[1]
        pool = (2, (n + (lo if before else 0)) // 2, cols // 2)
        args = (keep, part, halo, *coefs, pair, *before)
        outs, scratch = [pool, (2, n, cols)], [tiles(n, cols)] * 2
        return run(finish_pool_body, "finish_pool", outs, args, (i, lo), smem=1, scratch=scratch, work=8)

    far, before = [], ()
    for lo, halo in zip(starts, far_halo):
        far_pool, chunk = finish_pool(0, lo, far_part, halo, before)
        far.append(chunk)
        before = (far_pool,)
    near_pool, near = finish_pool(1, 0, near_part, near_halo)
    near_pool, far_pool = after(near_pool, far_pool)

    far_sums, near_sums = swap_far(far_pool), swap_near(near_pool)
    plane_sums = far_sums
    many = COARSE_SWEEPS - 1
    pieces = [(2, 3 * rows // 2 // many, cols // 2)] * many
    pieces = run(three_body, "three", pieces, (*far, even_col, odd_col), (len(far),), scratch=[tile])
    arrived = [swap_far(pieces[0])]
    near_halo = swap_near(near)
    args, scratch = (*far, near, *coefs, own, pair), [whole, tile, tile]
    far_part, near_part, local = run(
        part_defect_body, "part_defect", [full, full, half], args, (len(far),), scratch=scratch
    )
    fix = run(coarse_first_body, "coarse_first", [half], (keep, local, far_sums, near_sums, *coarse), smem=1, work=8)[0]
    first = fix
    for sweep_index in range(COARSE_SWEEPS - 1):
        far_sums, near_sums = swap_far(fix), swap_near(fix)
        if len(arrived) < len(pieces):
            fix, held = lax.optimization_barrier((fix, pieces[len(arrived)]))
            arrived.append(swap_far(held))
        part = run(coarse_part_body, "coarse_part", [half], (fix, first, *coarse))[0]
        part, arrived[sweep_index] = after(part, arrived[sweep_index])
        args = (keep, part, far_sums, near_sums, *coarse)
        fix = run(coarse_finish_body, "coarse_finish", [half], args, smem=1, work=8)[0]

    far_sums, near_sums = swap_far(fix), swap_near(fix)
    args = (keep, far_part, near_part, fix, near_halo, plane_sums, *arrived, pair_t, even_t, odd_t, *coefs)
    scratch = [tile] * 4 + [pltpu.VMEM((rows, cols), F32)] * 2
    far_part, near_part = run(third_body, "third", [full, full], args, (len(arrived),), smem=1, scratch=scratch)
    sizes = late_chunks(rows)
    starts = [sum(sizes[:n]) for n in range(len(sizes))]
    args, shapes = (keep, far_part, near_part, far_sums, near_sums, pair_t, *coefs), [(2, n, cols) for n in sizes]
    scratch = [v for n in [*sizes, rows] for v in [tiles(n, cols)] * 2]
    *far, near = run(fix_body, "fix", [*shapes, full], args, (starts,), smem=1, scratch=scratch, work=8)

    far_halo, near_halo = [swap_far(v) for v in far], swap_near(near)
    far_part, near_part = run(part_body, "part", [full] * 2, (*far, near, *coefs, own), (len(far),), scratch=[whole])
    outs = [(2, 2, rows, cols), full]

    def final(which, fields, done):
        args = (where, keep, *coefs, phase_lin, phase_state, *fields, *done)
        in_specs = [SMEM, SMEM] + [VMEM] * (len(args) - len(done) - 2) + [ANY] * len(done)
        scratch = []
        for halo in fields[1::2]:
            n = halo.shape[1]
            scratch += [pltpu.VMEM((2, n, cols), F32), pltpu.VMEM((n, cols), F32), pltpu.SemaphoreType.DMA((4,))]
        body = functools.partial(final_body, which)
        aliases = {len(args) - 2: 0, len(args) - 1: 1} if done else None
        return call(body, "final", outs, args, in_specs, [ANY, ANY], scratch, aliases, work=10)

    done = ()
    for lo, halo in zip(starts[:-1], far_halo[:-1]):
        done = final([(0, lo)], (far_part, halo), done)
    done = final([(1, 0)], (near_part, near_halo), done)
    done = final([(0, starts[-1])], (far_part, far_halo[-1]), done)
    return tuple(done)


def solution(mesh):
    in_specs = (
        P(("grp", "gx"), None, None),
        P(("grp", "gx"), None, None),
        P(None, ("grp", "gx"), None, None),
        P(None, ("grp", "gx"), None, None),
    )
    out_specs = (P(None, ("grp", "gx"), None, None), P(("grp", "gx"), None, None))
    return jax.shard_map(
        on_device, mesh=mesh, in_specs=in_specs, out_specs=out_specs, check_vma=False
    )
```

```python
import functools

import jax
import jax.numpy as jnp
from jax import lax
from jax.experimental import pallas as pl
from jax.experimental.pallas import tpu as pltpu
from jax.sharding import PartitionSpec as P

SWEEPS = 2
COARSE_SWEEPS = 4

GRADIENT_ENERGY = 1.0
TIME_STEP = 0.02
DAMPING = 0.8
KEEP = 1.0 - DAMPING
COARSE_ENERGY = GRADIENT_ENERGY / 4.0
COARSE_STEP = TIME_STEP / 4.0


VMEM = pl.BlockSpec(memory_space=pltpu.VMEM)
SMEM = pl.BlockSpec(memory_space=pltpu.SMEM)
ANY = pl.BlockSpec(memory_space=pl.ANY)
HBM = pl.BlockSpec(memory_space=pltpu.HBM)
BLOCK = 16
F32 = jnp.float32


def chip_pairs(count):
    return [(i, i ^ 1) for i in range(count)]


def cross_pairs(groups, count):
    pairs = []
    for g in range(groups):
        pairs += [(g * count + i, g * count + i + 1) for i in range(1, count - 1, 2)]
    for g in range(0, groups - 1, 2):
        pairs += [(g * count + i, (g + 1) * count + i) for i in (0, count - 1)]
    swaps = pairs + [(b, a) for a, b in pairs]
    if groups % 2 == 1:
        swaps += [((groups - 1) * count + i,) * 2 for i in (0, count - 1)]
    return swaps


def early_chunks(rows):
    return [rows // 2, rows // 2]


def late_chunks(rows):
    return [rows]


def call(body, name, outs, args, in_specs=None, out_specs=None, scratch=(), aliases=None, work=30, dtype=F32):
    shapes = [jax.ShapeDtypeStruct(s, dtype) for s in outs]
    size = sum(int(a.size) for a in args)
    made = sum(s.size for s in shapes)
    return pl.pallas_call(
        body,
        out_shape=shapes,
        in_specs=in_specs or [VMEM] * len(args),
        out_specs=out_specs or [VMEM] * len(outs),
        scratch_shapes=list(scratch),
        input_output_aliases=aliases or {},
        name=name,
        cost_estimate=pl.CostEstimate(flops=0, bytes_accessed=4 * (size + made), transcendentals=0),
        compiler_params=pltpu.CompilerParams(vmem_limit_bytes=12 * 1024 * 1024),
    )(*args)


def blocks(rows):
    return range(0, rows, BLOCK)


def around(read, r, rows):
    x = read(r, r + BLOCK)
    cols = x.shape[-1]
    row = lax.broadcasted_iota(jnp.int32, x.shape, 0)
    col = lax.broadcasted_iota(jnp.int32, x.shape, 1)
    up = read(r - 1, r - 1 + BLOCK) if r > 0 else jnp.where(row == 0, 0.0, pltpu.roll(x, 1, 0))
    if r + BLOCK < rows:
        down = read(r + 1, r + 1 + BLOCK)
    else:
        down = jnp.where(row == BLOCK - 1, 0.0, pltpu.roll(x, BLOCK - 1, 0))
    left = jnp.where(col == 0, 0.0, pltpu.roll(x, 1, 1))
    right = jnp.where(col == cols - 1, 0.0, pltpu.roll(x, cols - 1, 1))
    return x, (up + down) + (left + right)


def reader(ref, *lead):
    return lambda lo, hi: ref[(*lead, slice(lo, hi))]


def add_terms(base_p, base_m, gain, nb_p, nb_m, energy, step):
    gain_kt = (DAMPING - gain) * (1.0 / 6.0)
    new_p = base_p - gain * (energy * nb_m) + gain_kt * nb_p
    new_m = base_m + gain * (step * nb_p + (6.0 * step * energy) * nb_m)
    return new_p, new_m


def parts3(x):
    high = x.astype(jnp.bfloat16)
    rest = x - high.astype(F32)
    middle = rest.astype(jnp.bfloat16)
    low = (rest - middle.astype(F32)).astype(jnp.bfloat16)
    return high, middle, low


def times(xs, matrix):
    n, width = xs[0].shape[0], matrix.shape[0]
    pieces = [x[:, j : j + width] for x in xs for j in range(0, x.shape[1], width)]
    stacked = jnp.concatenate([v for piece in pieces for v in parts3(piece)], axis=0)
    out = jnp.dot(stacked, matrix, preferred_element_type=F32)
    sums = [out[j : j + n] + out[j + n : j + 2 * n] + out[j + 2 * n : j + 3 * n] for j in range(0, out.shape[0], 3 * n)]
    each = len(sums) // len(xs)
    return [jnp.concatenate(sums[j : j + each], axis=1) for j in range(0, len(sums), each)]


LANES = 128


def tiles(rows, cols):
    return pltpu.VMEM((cols // LANES, rows, LANES), F32)


def put_rows(ref, rows, x):
    for j in range(ref.shape[0]):
        ref[j, rows] = x[:, j * LANES : (j + 1) * LANES]


def get_rows(ref, rows):
    return jnp.concatenate([ref[j, rows] for j in range(ref.shape[0])], axis=1)


def even_odd(ref):
    half = ref.shape[1] // 2
    return pl.ds(0, half, stride=2), pl.ds(1, half, stride=2)


def pair_rows(ref):
    even, odd = even_odd(ref)
    return get_rows(ref, even) + get_rows(ref, odd)


def take_body(what, where, warm, *refs):
    outs, sems = refs[:-1], refs[-1]
    c = where[0]
    copies = []
    for n, ((is_near, lo), out) in enumerate(zip(what, outs)):
        plane = 1 - c if is_near else c
        rows = pl.ds(lo, out.shape[1])
        copies.append(pltpu.make_async_copy(warm.at[:, plane, rows], out, sems.at[n]))
        copies[-1].start()
    for copy in copies:
        copy.wait()


def matrices_body(where, pair, even_col, odd_col, pair_t, even_t, odd_t):
    for dim, (both, even, odd) in enumerate(((pair, even_col, odd_col), (pair_t, even_t, odd_t))):
        cell = lax.broadcasted_iota(jnp.int32, both.shape, dim)
        coarse = 2 * lax.broadcasted_iota(jnp.int32, both.shape, 1 - dim)
        is_even = jnp.where(cell == coarse, 1.0, 0.0)
        is_odd = jnp.where(cell == coarse + 1, 1.0, 0.0)
        even[...] = is_even.astype(jnp.bfloat16)
        odd[...] = is_odd.astype(jnp.bfloat16)
        both[...] = (is_even + is_odd).astype(jnp.bfloat16)


def setup_body(where, phi, cot, gain, own):
    c = where[0]
    for i in range(2):
        plane = c if i == 0 else 1 - c
        for r in blocks(phi.shape[1]):
            rows = slice(r, r + BLOCK)
            v = phi[plane, rows]
            k = 3.0 * v * v - 1.0 + 6.0 * GRADIENT_ENERGY
            g = DAMPING / (1.0 + 6.0 * TIME_STEP * k)
            s0, s1 = cot[0, plane, rows], cot[1, plane, rows]
            gain[i, rows] = g
            own[i, 0, rows] = g * (s0 + k * s1)
            own[i, 1, rows] = g * (s1 - 6.0 * TIME_STEP * s0)


def coarse_setup_body(phi, pair, gain, both):
    for r in blocks(phi.shape[1]):
        rows = slice(r, r + BLOCK)
        a, b = phi[0, rows], phi[1, rows]
        put_rows(both, rows, (3.0 * a * a - 1.0) + (3.0 * b * b - 1.0))
    k = times([pair_rows(both)], pair[...])[0] / 8.0 + 6.0 * COARSE_ENERGY
    gain[...] = DAMPING / (1.0 + 6.0 * COARSE_STEP * k)


def gather_rows(chunks, whole):
    lo = 0
    for chunk in chunks:
        n = chunk.shape[1]
        for r in blocks(n):
            for f in range(2):
                whole[f, slice(lo + r, lo + r + BLOCK)] = chunk[f, slice(r, r + BLOCK)]
        lo += n


def part_body(count, *refs):
    chunks, (near, gain, own, far_out, near_out, far) = refs[:count], refs[count:]
    gather_rows(chunks, far)
    rows_all = far.shape[1]
    for i, (mine, other, out) in enumerate(((far, near, far_out), (near, far, near_out))):
        for r in blocks(rows_all):
            rows = slice(r, r + BLOCK)
            p, nb_p = around(reader(mine, 0), r, rows_all)
            m, nb_m = around(reader(mine, 1), r, rows_all)
            out[0, rows], out[1, rows] = add_terms(
                KEEP * p + own[i, 0, rows],
                KEEP * m + own[i, 1, rows],
                gain[i, rows],
                nb_p + other[0, rows],
                nb_m + other[1, rows],
                GRADIENT_ENERGY,
                TIME_STEP,
            )


def finish_body(i, lo, keep, part, halo, gain, out):
    for r in blocks(halo.shape[1]):
        rows, whole = slice(r, r + BLOCK), slice(lo + r, lo + r + BLOCK)
        hp, hm = halo[0, rows], halo[1, rows]
        if i == 0:
            hp, hm = hp * keep[0], hm * keep[0]
        out[0, rows], out[1, rows] = add_terms(
            part[0, whole], part[1, whole], gain[i, whole], hp, hm, GRADIENT_ENERGY, TIME_STEP
        )


def finish_pool_body(i, lo, keep, part, halo, gain, pair, *refs):
    before, (pool, out, phase, chem) = refs[:-4], refs[-4:]
    for r in blocks(halo.shape[1]):
        rows, whole = slice(r, r + BLOCK), slice(lo + r, lo + r + BLOCK)
        hp, hm = halo[0, rows], halo[1, rows]
        if i == 0:
            hp, hm = hp * keep[0], hm * keep[0]
        p, m = add_terms(
            part[0, whole], part[1, whole], gain[i, whole], hp, hm, GRADIENT_ENERGY, TIME_STEP
        )
        out[0, rows] = p
        out[1, rows] = m
        put_rows(phase, rows, p)
        put_rows(chem, rows, m)
    sums = times([pair_rows(phase), pair_rows(chem)], pair[...])
    for f in range(2):
        for ref in before:
            pool[f, : lo // 2] = ref[f]
        pool[f, lo // 2 if before else 0 :] = sums[f]


def three_body(count, *refs):
    chunks, (even_col, odd_col), outs, tile = refs[:count], refs[count : count + 2], refs[count + 2 : -1], refs[-1]
    for f in range(2):
        lo = 0
        for chunk in chunks:
            for r in blocks(chunk.shape[1]):
                put_rows(tile, slice(lo + r, lo + r + BLOCK), chunk[f, slice(r, r + BLOCK)])
            lo += chunk.shape[1]
        even, odd = even_odd(tile)
        top, bottom = get_rows(tile, even), get_rows(tile, odd)
        first, third = times([top, bottom], even_col[...])
        second = times([top], odd_col[...])[0]
        values = jnp.concatenate([first, second, third], axis=0)
        n = values.shape[0] // len(outs)
        for j, out in enumerate(outs):
            out[f] = values[j * n : (j + 1) * n]


def part_defect_body(count, *refs):
    chunks, (near, gain, own, pair, far_out, near_out, out, far, phase, chem) = refs[:count], refs[count:]
    part_body(count, *chunks, near, gain, own, far_out, near_out, far)
    for r in blocks(near.shape[1]):
        rows = slice(r, r + BLOCK)
        r0, r1 = 0.0, 0.0
        for i, (mine, new) in enumerate(((far, far_out), (near, near_out))):
            dp, dm = new[0, rows] - mine[0, rows], new[1, rows] - mine[1, rows]
            k = (DAMPING - gain[i, rows]) / (6.0 * TIME_STEP * gain[i, rows])
            r0 = r0 + (dp - k * dm)
            r1 = r1 + (dm + 6.0 * TIME_STEP * dp)
        put_rows(phase, rows, r0)
        put_rows(chem, rows, r1)
    sums = times([pair_rows(phase), pair_rows(chem)], pair[...])
    for f in range(2):
        out[f] = sums[f] * (1.0 / (8.0 * DAMPING))


def coarse_first_body(keep, local, far, near, gain, out):
    for r in blocks(local.shape[1]):
        rows = slice(r, r + BLOCK)
        s0 = local[0, rows] - (GRADIENT_ENERGY / 8.0) * (far[1, rows] * keep[0] + near[1, rows])
        s1 = local[1, rows] + (TIME_STEP / 8.0) * (far[0, rows] * keep[0] + near[0, rows])
        g = gain[rows]
        out[0, rows] = g * s0 + ((DAMPING - g) * (1.0 / (6.0 * COARSE_STEP))) * s1
        out[1, rows] = g * (s1 - 6.0 * COARSE_STEP * s0)


def coarse_part_body(fix, own, gain, out):
    rows_all = fix.shape[1]
    for r in blocks(rows_all):
        rows = slice(r, r + BLOCK)
        p, nb_p = around(reader(fix, 0), r, rows_all)
        m, nb_m = around(reader(fix, 1), r, rows_all)
        out[0, rows], out[1, rows] = add_terms(
            KEEP * p + own[0, rows],
            KEEP * m + own[1, rows],
            gain[rows],
            nb_p,
            nb_m,
            COARSE_ENERGY,
            COARSE_STEP,
        )


def coarse_finish_body(keep, part, far, near, gain, out):
    for r in blocks(part.shape[1]):
        rows = slice(r, r + BLOCK)
        out[0, rows], out[1, rows] = add_terms(
            part[0, rows],
            part[1, rows],
            gain[rows],
            far[0, rows] * keep[0] + near[0, rows],
            far[1, rows] * keep[0] + near[1, rows],
            COARSE_ENERGY,
            COARSE_STEP,
        )


def spread_into(tile_a, tile_b, fix_a, fix_b, pair_t):
    for tile, wide in zip((tile_a, tile_b), times([fix_a, fix_b], pair_t)):
        for rows in even_odd(tile):
            put_rows(tile, rows, wide)


def third_body(far, near, fix, near_halo, pair_t, gain, far_out, near_out, fix_p, fix_m, wide_p, wide_m):
    rows_all = near.shape[1]
    spread_into(fix_p, fix_m, fix[0], fix[1], pair_t[...])
    for r in blocks(rows_all):
        rows = slice(r, r + BLOCK)
        wide_p[rows], wide_m[rows] = get_rows(fix_p, rows), get_rows(fix_m, rows)
    for r in blocks(rows_all):
        rows = slice(r, r + BLOCK)
        p, nb_p = around(lambda lo, hi: wide_p[lo:hi], r, rows_all)
        m, nb_m = around(lambda lo, hi: wide_m[lo:hi], r, rows_all)
        nb_p, nb_m = nb_p + p, nb_m + m
        for i, (part, out) in enumerate(((far, far_out), (near, near_out))):
            xp, xm = (near_halo[0, rows], near_halo[1, rows]) if i == 1 else (0.0, 0.0)
            out[0, rows], out[1, rows] = add_terms(
                part[0, rows] + KEEP * p,
                part[1, rows] + KEEP * m,
                gain[i, rows],
                nb_p + xp,
                nb_m + xm,
                GRADIENT_ENERGY,
                TIME_STEP,
            )


def rebuild_body(sums, *refs):
    pieces, (even_t, odd_t, out, halo_p, halo_m) = refs[:-5], refs[-5:]
    half = sums.shape[1]
    for f, tile in enumerate((halo_p, halo_m)):
        values = jnp.concatenate([piece[f] for piece in pieces], axis=0)
        a, b, c = values[:half], values[half : 2 * half], values[2 * half :]
        d = sums[f] - ((a + b) + c)
        even, odd = even_odd(tile)
        (a, c), (b, d) = times([a, c], even_t[...]), times([b, d], odd_t[...])
        put_rows(tile, even, a + b)
        put_rows(tile, odd, c + d)
        for r in blocks(2 * half):
            rows = slice(r, r + BLOCK)
            out[f, rows] = get_rows(tile, rows)


def finish_fix_rows(i, lo, keep, part, halo, pair_t, gain, out, phase, chem, state_nb=None):
    n = out.shape[1]
    coarse = slice(lo // 2, (lo + n) // 2)
    spread_into(phase, chem, halo[0, coarse], halo[1, coarse], pair_t[...])
    for r in blocks(n):
        rows, whole = slice(r, r + BLOCK), slice(lo + r, lo + r + BLOCK)
        hp, hm = get_rows(phase, rows), get_rows(chem, rows)
        if i == 0:
            hp, hm = (hp + state_nb[0, whole]) * keep[0], (hm + state_nb[1, whole]) * keep[0]
        out[0, rows], out[1, rows] = add_terms(
            part[0, whole], part[1, whole], gain[i, whole], hp, hm, GRADIENT_ENERGY, TIME_STEP
        )


def fix_body(starts, keep, far_part, near_part, far_halo, near_halo, state_nb, pair_t, gain, *refs):
    count = len(starts)
    outs, scratch = refs[: count + 1], refs[count + 1 :]
    for n, (lo, out) in enumerate(zip(starts, outs)):
        finish_fix_rows(0, lo, keep, far_part, far_halo, pair_t, gain, out, *scratch[2 * n : 2 * n + 2], state_nb)
    finish_fix_rows(1, 0, keep, near_part, near_halo, pair_t, gain, outs[-1], *scratch[-2:])


def final_rows(i, lo, where, keep, part, halo, gain, phi, psi, adjoint, design, plane_out, grad_out, sems):
    c = where[0]
    plane = c if i == 0 else 1 - c
    rows_all = halo.shape[1]
    step = rows_all // 2
    copies = []
    for n, start in enumerate(range(0, rows_all, step)):
        for r in range(start, start + step, BLOCK):
            rows, whole = slice(r, r + BLOCK), slice(lo + r, lo + r + BLOCK)
            hp, hm = halo[0, rows], halo[1, rows]
            if i == 0:
                hp, hm = hp * keep[0], hm * keep[0]
            p, m = add_terms(
                part[0, whole], part[1, whole], gain[i, whole], hp, hm, GRADIENT_ENERGY, TIME_STEP
            )
            plane_out[0, rows] = p
            plane_out[1, rows] = m
            grad_out[rows] = 6.0 * phi[plane, whole] * psi[plane, whole] * m
        here, there = pl.ds(start, step), pl.ds(lo + start, step)
        copies.append(pltpu.make_async_copy(plane_out.at[:, here], adjoint.at[:, plane, there], sems.at[2 * n]))
        copies.append(pltpu.make_async_copy(grad_out.at[here], design.at[plane, there], sems.at[2 * n + 1]))
        copies[-2].start()
        copies[-1].start()
    return copies


def final_body(which, where, keep, gain, phi, psi, *refs):
    count = len(which)
    halos, refs = refs[: 2 * count], refs[2 * count :]
    scratch = refs[-3 * count :]
    adjoint, design = refs[-3 * count - 2 : -3 * count]
    copies = []
    for n, (i, lo) in enumerate(which):
        part, halo = halos[2 * n : 2 * n + 2]
        copies += final_rows(
            i, lo, where, keep, part, halo, gain, phi, psi, adjoint, design, *scratch[3 * n : 3 * n + 3]
        )
    for copy in copies:
        copy.wait()


def on_device(phase_lin, phase_state, cotangent, warm_start):
    groups, count = lax.axis_size("grp"), lax.axis_size("gx")
    me = lax.axis_index("gx")
    where = jnp.reshape(me % 2, (1,)).astype(jnp.int32)
    keep = jnp.reshape(((me > 0) & (me < count - 1)).astype(F32), (1,))
    across, on_chip = cross_pairs(groups, count), chip_pairs(count)
    rows, cols = phase_lin.shape[1:]
    full, half = (2, rows, cols), (2, rows // 2, cols // 2)
    sizes = early_chunks(rows)
    starts = [sum(sizes[:n]) for n in range(len(sizes))]

    def swap_far(x):
        return lax.ppermute(x, ("grp", "gx"), across)

    def swap_near(x):
        return lax.ppermute(x, "gx", on_chip)

    def after(x, y):
        return lax.optimization_barrier((x, y))

    whole, tile = pltpu.VMEM(full, F32), tiles(rows, cols)

    def run(body, name, outs, args, statics=(), smem=0, **kw):
        specs = [SMEM] * smem + [VMEM] * (len(args) - smem)
        return call(functools.partial(body, *statics), name, outs, args, specs, **kw)

    def take(what, name):
        outs = [(2, n, cols) for _, _, n in what]
        body = functools.partial(take_body, [(is_near, lo) for is_near, lo, _ in what])
        scratch = [pltpu.SemaphoreType.DMA((len(what),))]
        source = pltpu.with_memory_space_constraint(warm_start, pltpu.HBM)
        return call(body, name, outs, (where, source), [SMEM, HBM], scratch=scratch, work=0)

    *far, near = take([(False, lo, n) for lo, n in zip(starts, sizes)] + [(True, 0, rows)], "take")
    far_halo = [swap_far(v) for v in far]
    near_halo = swap_near(near)
    gain, own = run(setup_body, "setup", [full, (2, 2, rows, cols)], (where, phase_lin, cotangent), smem=1)
    coefs = (gain,)
    far_part, near_part = run(part_body, "part", [full] * 2, (*far, near, *coefs, own), (len(far),), scratch=[whole])
    def finish(i, lo, part, halo):
        shape = (2, halo.shape[1], cols)
        return run(finish_body, "finish", [shape], (keep, part, halo, *coefs), (i, lo), smem=1, work=8)[0]

    far = [finish(0, lo, far_part, halo) for lo, halo in zip(starts, far_halo)]
    near_halo, far[-1] = after(near_halo, far[-1])
    near = finish(1, 0, near_part, near_halo)
    later, far[-1] = after(where, far[-1])
    shapes = [(2 * LANES, LANES)] * 3 + [(LANES, 2 * LANES)] * 3
    matrices = run(matrices_body, "matrices", shapes, (later,), smem=1, dtype=jnp.bfloat16)
    pair, even_col, odd_col, pair_t, even_t, odd_t = matrices
    coarse = run(coarse_setup_body, "coarse_setup", [half[1:]], (phase_lin, pair), scratch=[tile])

    far_halo = [swap_far(v) for v in far]
    near_halo = swap_near(near)
    far_part, near_part = run(part_body, "part", [full] * 2, (*far, near, *coefs, own), (len(far),), scratch=[whole])

    def finish_pool(i, lo, part, halo, before=()):
        n = halo.shape[1]
        pool = (2, (n + (lo if before else 0)) // 2, cols // 2)
        args = (keep, part, halo, *coefs, pair, *before)
        outs, scratch = [pool, (2, n, cols)], [tiles(n, cols)] * 2
        return run(finish_pool_body, "finish_pool", outs, args, (i, lo), smem=1, scratch=scratch, work=8)

    far, before = [], ()
    for lo, halo in zip(starts, far_halo):
        far_pool, chunk = finish_pool(0, lo, far_part, halo, before)
        far.append(chunk)
        before = (far_pool,)
    near_pool, near = finish_pool(1, 0, near_part, near_halo)

    far_sums, near_sums = swap_far(far_pool), swap_near(near_pool)
    plane_sums = far_sums
    many = COARSE_SWEEPS - 1
    pieces = [(2, 3 * rows // 2 // many, cols // 2)] * many
    pieces = run(three_body, "three", pieces, (*far, even_col, odd_col), (len(far),), scratch=[tile])
    arrived = [swap_far(pieces[0])]
    near_halo = swap_near(near)
    args, scratch = (*far, near, *coefs, own, pair), [whole, tile, tile]
    far_part, near_part, local = run(
        part_defect_body, "part_defect", [full, full, half], args, (len(far),), scratch=scratch
    )
    fix = run(coarse_first_body, "coarse_first", [half], (keep, local, far_sums, near_sums, *coarse), smem=1, work=8)[0]
    first = fix
    for sweep_index in range(COARSE_SWEEPS - 1):
        far_sums, near_sums = swap_far(fix), swap_near(fix)
        if len(arrived) < len(pieces):
            fix, held = lax.optimization_barrier((fix, pieces[len(arrived)]))
            arrived.append(swap_far(held))
        part = run(coarse_part_body, "coarse_part", [half], (fix, first, *coarse))[0]
        if sweep_index:
            part, arrived[sweep_index - 1] = after(part, arrived[sweep_index - 1])
        args = (keep, part, far_sums, near_sums, *coarse)
        fix = run(coarse_finish_body, "coarse_finish", [half], args, smem=1, work=8)[0]

    far_sums, near_sums = swap_far(fix), swap_near(fix)
    args = (far_part, near_part, fix, near_halo, pair_t, *coefs)
    scratch = [tile] * 2 + [pltpu.VMEM((rows, cols), F32)] * 2
    far_part, near_part = run(third_body, "third", [full, full], args, scratch=scratch)
    plane_sums, far_part = after(plane_sums, far_part)
    state_nb = run(rebuild_body, "rebuild", [full], (plane_sums, *arrived, even_t, odd_t), scratch=[tile] * 2)[0]
    sizes = late_chunks(rows)
    starts = [sum(sizes[:n]) for n in range(len(sizes))]
    args = (keep, far_part, near_part, far_sums, near_sums, state_nb, pair_t, *coefs)
    shapes = [(2, n, cols) for n in sizes]
    scratch = [v for n in [*sizes, rows] for v in [tiles(n, cols)] * 2]
    *far, near = run(fix_body, "fix", [*shapes, full], args, (starts,), smem=1, scratch=scratch, work=8)

    far_halo, near_halo = [swap_far(v) for v in far], swap_near(near)
    far_part, near_part = run(part_body, "part", [full] * 2, (*far, near, *coefs, own), (len(far),), scratch=[whole])
    outs = [(2, 2, rows, cols), full]

    def final(which, fields, done):
        args = (where, keep, *coefs, phase_lin, phase_state, *fields, *done)
        in_specs = [SMEM, SMEM] + [VMEM] * (len(args) - len(done) - 2) + [ANY] * len(done)
        scratch = []
        for halo in fields[1::2]:
            n = halo.shape[1]
            scratch += [pltpu.VMEM((2, n, cols), F32), pltpu.VMEM((n, cols), F32), pltpu.SemaphoreType.DMA((4,))]
        body = functools.partial(final_body, which)
        aliases = {len(args) - 2: 0, len(args) - 1: 1} if done else None
        return call(body, "final", outs, args, in_specs, [ANY, ANY], scratch, aliases, work=10)

    done = ()
    for lo, halo in zip(starts[:-1], far_halo[:-1]):
        done = final([(0, lo)], (far_part, halo), done)
    done = final([(1, 0)], (near_part, near_halo), done)
    done = final([(0, starts[-1])], (far_part, far_halo[-1]), done)
    return tuple(done)


def solution(mesh):
    in_specs = (
        P(("grp", "gx"), None, None),
        P(("grp", "gx"), None, None),
        P(None, ("grp", "gx"), None, None),
        P(None, ("grp", "gx"), None, None),
    )
    out_specs = (P(None, ("grp", "gx"), None, None), P(("grp", "gx"), None, None))
    return jax.shard_map(
        on_device, mesh=mesh, in_specs=in_specs, out_specs=out_specs, check_vma=False
    )
```

```python
import functools

import jax
import jax.numpy as jnp
from jax import lax
from jax.experimental import pallas as pl
from jax.experimental.pallas import tpu as pltpu
from jax.sharding import PartitionSpec as P

SWEEPS = 2
COARSE_SWEEPS = 4

GRADIENT_ENERGY = 1.0
TIME_STEP = 0.02
DAMPING = 0.8
KEEP = 1.0 - DAMPING
COARSE_ENERGY = GRADIENT_ENERGY / 4.0
COARSE_STEP = TIME_STEP / 4.0


VMEM = pl.BlockSpec(memory_space=pltpu.VMEM)
SMEM = pl.BlockSpec(memory_space=pltpu.SMEM)
ANY = pl.BlockSpec(memory_space=pl.ANY)
HBM = pl.BlockSpec(memory_space=pltpu.HBM)
BLOCK = 16
F32 = jnp.float32


def chip_pairs(count):
    return [(i, i ^ 1) for i in range(count)]


def cross_pairs(groups, count):
    pairs = []
    for g in range(groups):
        pairs += [(g * count + i, g * count + i + 1) for i in range(1, count - 1, 2)]
    for g in range(0, groups - 1, 2):
        pairs += [(g * count + i, (g + 1) * count + i) for i in (0, count - 1)]
    swaps = pairs + [(b, a) for a, b in pairs]
    if groups % 2 == 1:
        swaps += [((groups - 1) * count + i,) * 2 for i in (0, count - 1)]
    return swaps


def early_chunks(rows):
    return [5 * rows // 8, 3 * rows // 8]


def late_chunks(rows):
    return [rows]


def call(body, name, outs, args, in_specs=None, out_specs=None, scratch=(), aliases=None, work=30, dtype=F32):
    shapes = [jax.ShapeDtypeStruct(s, dtype) for s in outs]
    size = sum(int(a.size) for a in args)
    made = sum(s.size for s in shapes)
    return pl.pallas_call(
        body,
        out_shape=shapes,
        in_specs=in_specs or [VMEM] * len(args),
        out_specs=out_specs or [VMEM] * len(outs),
        scratch_shapes=list(scratch),
        input_output_aliases=aliases or {},
        name=name,
        cost_estimate=pl.CostEstimate(flops=0, bytes_accessed=4 * (size + made), transcendentals=0),
        compiler_params=pltpu.CompilerParams(vmem_limit_bytes=12 * 1024 * 1024),
    )(*args)


def blocks(rows):
    return range(0, rows, BLOCK)


def around(read, r, rows):
    x = read(r, r + BLOCK)
    cols = x.shape[-1]
    row = lax.broadcasted_iota(jnp.int32, x.shape, 0)
    col = lax.broadcasted_iota(jnp.int32, x.shape, 1)
    up = read(r - 1, r - 1 + BLOCK) if r > 0 else jnp.where(row == 0, 0.0, pltpu.roll(x, 1, 0))
    if r + BLOCK < rows:
        down = read(r + 1, r + 1 + BLOCK)
    else:
        down = jnp.where(row == BLOCK - 1, 0.0, pltpu.roll(x, BLOCK - 1, 0))
    left = jnp.where(col == 0, 0.0, pltpu.roll(x, 1, 1))
    right = jnp.where(col == cols - 1, 0.0, pltpu.roll(x, cols - 1, 1))
    return x, (up + down) + (left + right)


def reader(ref, *lead):
    return lambda lo, hi: ref[(*lead, slice(lo, hi))]


def add_terms(base_p, base_m, gain, nb_p, nb_m, energy, step):
    gain_kt = (DAMPING - gain) * (1.0 / 6.0)
    new_p = base_p - gain * (energy * nb_m) + gain_kt * nb_p
    new_m = base_m + gain * (step * nb_p + (6.0 * step * energy) * nb_m)
    return new_p, new_m


def parts3(x):
    high = x.astype(jnp.bfloat16)
    rest = x - high.astype(F32)
    middle = rest.astype(jnp.bfloat16)
    low = (rest - middle.astype(F32)).astype(jnp.bfloat16)
    return high, middle, low


def times(xs, matrix):
    n, width = xs[0].shape[0], matrix.shape[0]
    pieces = [x[:, j : j + width] for x in xs for j in range(0, x.shape[1], width)]
    stacked = jnp.concatenate([v for piece in pieces for v in parts3(piece)], axis=0)
    out = jnp.dot(stacked, matrix, preferred_element_type=F32)
    sums = [out[j : j + n] + out[j + n : j + 2 * n] + out[j + 2 * n : j + 3 * n] for j in range(0, out.shape[0], 3 * n)]
    each = len(sums) // len(xs)
    return [jnp.concatenate(sums[j : j + each], axis=1) for j in range(0, len(sums), each)]


LANES = 128


def tiles(rows, cols):
    return pltpu.VMEM((cols // LANES, rows, LANES), F32)


def put_rows(ref, rows, x):
    for j in range(ref.shape[0]):
        ref[j, rows] = x[:, j * LANES : (j + 1) * LANES]


def get_rows(ref, rows):
    return jnp.concatenate([ref[j, rows] for j in range(ref.shape[0])], axis=1)


def even_odd(ref):
    half = ref.shape[1] // 2
    return pl.ds(0, half, stride=2), pl.ds(1, half, stride=2)


def pair_rows(ref):
    even, odd = even_odd(ref)
    return get_rows(ref, even) + get_rows(ref, odd)


def take_body(what, where, warm, *refs):
    outs, sems = refs[:-1], refs[-1]
    c = where[0]
    copies = []
    for n, ((is_near, lo), out) in enumerate(zip(what, outs)):
        plane = 1 - c if is_near else c
        rows = pl.ds(lo, out.shape[1])
        copies.append(pltpu.make_async_copy(warm.at[:, plane, rows], out, sems.at[n]))
        copies[-1].start()
    for copy in copies:
        copy.wait()


def matrices_body(where, pair, even_col, odd_col, pair_t, even_t, odd_t):
    for dim, (both, even, odd) in enumerate(((pair, even_col, odd_col), (pair_t, even_t, odd_t))):
        cell = lax.broadcasted_iota(jnp.int32, both.shape, dim)
        coarse = 2 * lax.broadcasted_iota(jnp.int32, both.shape, 1 - dim)
        is_even = jnp.where(cell == coarse, 1.0, 0.0)
        is_odd = jnp.where(cell == coarse + 1, 1.0, 0.0)
        even[...] = is_even.astype(jnp.bfloat16)
        odd[...] = is_odd.astype(jnp.bfloat16)
        both[...] = (is_even + is_odd).astype(jnp.bfloat16)


def setup_body(where, phi, cot, gain, own):
    c = where[0]
    for i in range(2):
        plane = c if i == 0 else 1 - c
        for r in blocks(phi.shape[1]):
            rows = slice(r, r + BLOCK)
            v = phi[plane, rows]
            k = 3.0 * v * v - 1.0 + 6.0 * GRADIENT_ENERGY
            g = DAMPING / (1.0 + 6.0 * TIME_STEP * k)
            s0, s1 = cot[0, plane, rows], cot[1, plane, rows]
            gain[i, rows] = g
            own[i, 0, rows] = g * (s0 + k * s1)
            own[i, 1, rows] = g * (s1 - 6.0 * TIME_STEP * s0)


def coarse_setup_body(phi, pair, gain, both):
    for r in blocks(phi.shape[1]):
        rows = slice(r, r + BLOCK)
        a, b = phi[0, rows], phi[1, rows]
        put_rows(both, rows, (3.0 * a * a - 1.0) + (3.0 * b * b - 1.0))
    k = times([pair_rows(both)], pair[...])[0] / 8.0 + 6.0 * COARSE_ENERGY
    gain[...] = DAMPING / (1.0 + 6.0 * COARSE_STEP * k)


def gather_rows(chunks, whole):
    lo = 0
    for chunk in chunks:
        n = chunk.shape[1]
        for r in blocks(n):
            for f in range(2):
                whole[f, slice(lo + r, lo + r + BLOCK)] = chunk[f, slice(r, r + BLOCK)]
        lo += n


def part_body(count, *refs):
    chunks, (near, gain, own, far_out, near_out, far) = refs[:count], refs[count:]
    gather_rows(chunks, far)
    rows_all = far.shape[1]
    for i, (mine, other, out) in enumerate(((far, near, far_out), (near, far, near_out))):
        for r in blocks(rows_all):
            rows = slice(r, r + BLOCK)
            p, nb_p = around(reader(mine, 0), r, rows_all)
            m, nb_m = around(reader(mine, 1), r, rows_all)
            out[0, rows], out[1, rows] = add_terms(
                KEEP * p + own[i, 0, rows],
                KEEP * m + own[i, 1, rows],
                gain[i, rows],
                nb_p + other[0, rows],
                nb_m + other[1, rows],
                GRADIENT_ENERGY,
                TIME_STEP,
            )


def finish_body(i, lo, keep, part, halo, gain, out):
    for r in blocks(halo.shape[1]):
        rows, whole = slice(r, r + BLOCK), slice(lo + r, lo + r + BLOCK)
        hp, hm = halo[0, rows], halo[1, rows]
        if i == 0:
            hp, hm = hp * keep[0], hm * keep[0]
        out[0, rows], out[1, rows] = add_terms(
            part[0, whole], part[1, whole], gain[i, whole], hp, hm, GRADIENT_ENERGY, TIME_STEP
        )


def finish_pool_body(i, lo, keep, part, halo, gain, pair, *refs):
    before, (pool, out, phase, chem) = refs[:-4], refs[-4:]
    for r in blocks(halo.shape[1]):
        rows, whole = slice(r, r + BLOCK), slice(lo + r, lo + r + BLOCK)
        hp, hm = halo[0, rows], halo[1, rows]
        if i == 0:
            hp, hm = hp * keep[0], hm * keep[0]
        p, m = add_terms(
            part[0, whole], part[1, whole], gain[i, whole], hp, hm, GRADIENT_ENERGY, TIME_STEP
        )
        out[0, rows] = p
        out[1, rows] = m
        put_rows(phase, rows, p)
        put_rows(chem, rows, m)
    sums = times([pair_rows(phase), pair_rows(chem)], pair[...])
    for f in range(2):
        for ref in before:
            pool[f, : lo // 2] = ref[f]
        pool[f, lo // 2 if before else 0 :] = sums[f]


def three_body(count, *refs):
    chunks, (even_col, odd_col), outs, tile = refs[:count], refs[count : count + 2], refs[count + 2 : -1], refs[-1]
    for f in range(2):
        lo = 0
        for chunk in chunks:
            for r in blocks(chunk.shape[1]):
                put_rows(tile, slice(lo + r, lo + r + BLOCK), chunk[f, slice(r, r + BLOCK)])
            lo += chunk.shape[1]
        even, odd = even_odd(tile)
        top, bottom = get_rows(tile, even), get_rows(tile, odd)
        first, third = times([top, bottom], even_col[...])
        second = times([top], odd_col[...])[0]
        values = jnp.concatenate([first, second, third], axis=0)
        n = values.shape[0] // len(outs)
        for j, out in enumerate(outs):
            out[f] = values[j * n : (j + 1) * n]


def part_defect_body(count, *refs):
    chunks, (near, gain, own, pair, far_out, near_out, out, far, phase, chem) = refs[:count], refs[count:]
    part_body(count, *chunks, near, gain, own, far_out, near_out, far)
    for r in blocks(near.shape[1]):
        rows = slice(r, r + BLOCK)
        r0, r1 = 0.0, 0.0
        for i, (mine, new) in enumerate(((far, far_out), (near, near_out))):
            dp, dm = new[0, rows] - mine[0, rows], new[1, rows] - mine[1, rows]
            k = (DAMPING - gain[i, rows]) / (6.0 * TIME_STEP * gain[i, rows])
            r0 = r0 + (dp - k * dm)
            r1 = r1 + (dm + 6.0 * TIME_STEP * dp)
        put_rows(phase, rows, r0)
        put_rows(chem, rows, r1)
    sums = times([pair_rows(phase), pair_rows(chem)], pair[...])
    for f in range(2):
        out[f] = sums[f] * (1.0 / (8.0 * DAMPING))


def coarse_first_body(keep, local, far, near, gain, out):
    for r in blocks(local.shape[1]):
        rows = slice(r, r + BLOCK)
        s0 = local[0, rows] - (GRADIENT_ENERGY / 8.0) * (far[1, rows] * keep[0] + near[1, rows])
        s1 = local[1, rows] + (TIME_STEP / 8.0) * (far[0, rows] * keep[0] + near[0, rows])
        g = gain[rows]
        out[0, rows] = g * s0 + ((DAMPING - g) * (1.0 / (6.0 * COARSE_STEP))) * s1
        out[1, rows] = g * (s1 - 6.0 * COARSE_STEP * s0)


def coarse_part_body(fix, own, gain, out):
    rows_all = fix.shape[1]
    for r in blocks(rows_all):
        rows = slice(r, r + BLOCK)
        p, nb_p = around(reader(fix, 0), r, rows_all)
        m, nb_m = around(reader(fix, 1), r, rows_all)
        out[0, rows], out[1, rows] = add_terms(
            KEEP * p + own[0, rows],
            KEEP * m + own[1, rows],
            gain[rows],
            nb_p,
            nb_m,
            COARSE_ENERGY,
            COARSE_STEP,
        )


def coarse_finish_body(keep, part, far, near, gain, out):
    for r in blocks(part.shape[1]):
        rows = slice(r, r + BLOCK)
        out[0, rows], out[1, rows] = add_terms(
            part[0, rows],
            part[1, rows],
            gain[rows],
            far[0, rows] * keep[0] + near[0, rows],
            far[1, rows] * keep[0] + near[1, rows],
            COARSE_ENERGY,
            COARSE_STEP,
        )


def spread_into(tile_a, tile_b, fix_a, fix_b, pair_t):
    for tile, wide in zip((tile_a, tile_b), times([fix_a, fix_b], pair_t)):
        for rows in even_odd(tile):
            put_rows(tile, rows, wide)


def third_body(far, near, fix, near_halo, pair_t, gain, far_out, near_out, fix_p, fix_m, wide_p, wide_m):
    rows_all = near.shape[1]
    spread_into(fix_p, fix_m, fix[0], fix[1], pair_t[...])
    for r in blocks(rows_all):
        rows = slice(r, r + BLOCK)
        wide_p[rows], wide_m[rows] = get_rows(fix_p, rows), get_rows(fix_m, rows)
    for r in blocks(rows_all):
        rows = slice(r, r + BLOCK)
        p, nb_p = around(lambda lo, hi: wide_p[lo:hi], r, rows_all)
        m, nb_m = around(lambda lo, hi: wide_m[lo:hi], r, rows_all)
        nb_p, nb_m = nb_p + p, nb_m + m
        for i, (part, out) in enumerate(((far, far_out), (near, near_out))):
            xp, xm = (near_halo[0, rows], near_halo[1, rows]) if i == 1 else (0.0, 0.0)
            out[0, rows], out[1, rows] = add_terms(
                part[0, rows] + KEEP * p,
                part[1, rows] + KEEP * m,
                gain[i, rows],
                nb_p + xp,
                nb_m + xm,
                GRADIENT_ENERGY,
                TIME_STEP,
            )


def rebuild_body(sums, *refs):
    pieces, (even_t, odd_t, out, halo_p, halo_m) = refs[:-5], refs[-5:]
    half = sums.shape[1]
    for f, tile in enumerate((halo_p, halo_m)):
        values = jnp.concatenate([piece[f] for piece in pieces], axis=0)
        a, b, c = values[:half], values[half : 2 * half], values[2 * half :]
        d = sums[f] - ((a + b) + c)
        even, odd = even_odd(tile)
        (a, c), (b, d) = times([a, c], even_t[...]), times([b, d], odd_t[...])
        put_rows(tile, even, a + b)
        put_rows(tile, odd, c + d)
        for r in blocks(2 * half):
            rows = slice(r, r + BLOCK)
            out[f, rows] = get_rows(tile, rows)


def finish_fix_rows(i, lo, keep, part, halo, pair_t, gain, out, phase, chem, state_nb=None):
    n = out.shape[1]
    coarse = slice(lo // 2, (lo + n) // 2)
    spread_into(phase, chem, halo[0, coarse], halo[1, coarse], pair_t[...])
    for r in blocks(n):
        rows, whole = slice(r, r + BLOCK), slice(lo + r, lo + r + BLOCK)
        hp, hm = get_rows(phase, rows), get_rows(chem, rows)
        if i == 0:
            hp, hm = (hp + state_nb[0, whole]) * keep[0], (hm + state_nb[1, whole]) * keep[0]
        out[0, rows], out[1, rows] = add_terms(
            part[0, whole], part[1, whole], gain[i, whole], hp, hm, GRADIENT_ENERGY, TIME_STEP
        )


def fix_body(starts, keep, far_part, near_part, far_halo, near_halo, state_nb, pair_t, gain, *refs):
    count = len(starts)
    outs, scratch = refs[: count + 1], refs[count + 1 :]
    for n, (lo, out) in enumerate(zip(starts, outs)):
        finish_fix_rows(0, lo, keep, far_part, far_halo, pair_t, gain, out, *scratch[2 * n : 2 * n + 2], state_nb)
    finish_fix_rows(1, 0, keep, near_part, near_halo, pair_t, gain, outs[-1], *scratch[-2:])


def final_rows(i, lo, where, keep, part, halo, gain, phi, psi, adjoint, design, plane_out, grad_out, sems):
    c = where[0]
    plane = c if i == 0 else 1 - c
    rows_all = halo.shape[1]
    step = rows_all // 2
    copies = []
    for n, start in enumerate(range(0, rows_all, step)):
        for r in range(start, start + step, BLOCK):
            rows, whole = slice(r, r + BLOCK), slice(lo + r, lo + r + BLOCK)
            hp, hm = halo[0, rows], halo[1, rows]
            if i == 0:
                hp, hm = hp * keep[0], hm * keep[0]
            p, m = add_terms(
                part[0, whole], part[1, whole], gain[i, whole], hp, hm, GRADIENT_ENERGY, TIME_STEP
            )
            plane_out[0, rows] = p
            plane_out[1, rows] = m
            grad_out[rows] = 6.0 * phi[plane, whole] * psi[plane, whole] * m
        here, there = pl.ds(start, step), pl.ds(lo + start, step)
        copies.append(pltpu.make_async_copy(plane_out.at[:, here], adjoint.at[:, plane, there], sems.at[2 * n]))
        copies.append(pltpu.make_async_copy(grad_out.at[here], design.at[plane, there], sems.at[2 * n + 1]))
        copies[-2].start()
        copies[-1].start()
    return copies


def final_body(which, where, keep, gain, phi, psi, *refs):
    count = len(which)
    halos, refs = refs[: 2 * count], refs[2 * count :]
    scratch = refs[-3 * count :]
    adjoint, design = refs[-3 * count - 2 : -3 * count]
    copies = []
    for n, (i, lo) in enumerate(which):
        part, halo = halos[2 * n : 2 * n + 2]
        copies += final_rows(
            i, lo, where, keep, part, halo, gain, phi, psi, adjoint, design, *scratch[3 * n : 3 * n + 3]
        )
    for copy in copies:
        copy.wait()


def on_device(phase_lin, phase_state, cotangent, warm_start):
    groups, count = lax.axis_size("grp"), lax.axis_size("gx")
    me = lax.axis_index("gx")
    where = jnp.reshape(me % 2, (1,)).astype(jnp.int32)
    keep = jnp.reshape(((me > 0) & (me < count - 1)).astype(F32), (1,))
    across, on_chip = cross_pairs(groups, count), chip_pairs(count)
    rows, cols = phase_lin.shape[1:]
    full, half = (2, rows, cols), (2, rows // 2, cols // 2)
    sizes = early_chunks(rows)
    starts = [sum(sizes[:n]) for n in range(len(sizes))]

    def swap_far(x):
        return lax.ppermute(x, ("grp", "gx"), across)

    def swap_near(x):
        return lax.ppermute(x, "gx", on_chip)

    def after(x, y):
        return lax.optimization_barrier((x, y))

    whole, tile = pltpu.VMEM(full, F32), tiles(rows, cols)

    def run(body, name, outs, args, statics=(), smem=0, **kw):
        specs = [SMEM] * smem + [VMEM] * (len(args) - smem)
        return call(functools.partial(body, *statics), name, outs, args, specs, **kw)

    def take(what, name):
        outs = [(2, n, cols) for _, _, n in what]
        body = functools.partial(take_body, [(is_near, lo) for is_near, lo, _ in what])
        scratch = [pltpu.SemaphoreType.DMA((len(what),))]
        source = pltpu.with_memory_space_constraint(warm_start, pltpu.HBM)
        return call(body, name, outs, (where, source), [SMEM, HBM], scratch=scratch, work=0)

    *far, near = take([(False, lo, n) for lo, n in zip(starts, sizes)] + [(True, 0, rows)], "take")
    far_halo = [swap_far(v) for v in far]
    near_halo = swap_near(near)
    gain, own = run(setup_body, "setup", [full, (2, 2, rows, cols)], (where, phase_lin, cotangent), smem=1)
    coefs = (gain,)
    far_part, near_part = run(part_body, "part", [full] * 2, (*far, near, *coefs, own), (len(far),), scratch=[whole])
    def finish(i, lo, part, halo):
        shape = (2, halo.shape[1], cols)
        return run(finish_body, "finish", [shape], (keep, part, halo, *coefs), (i, lo), smem=1, work=8)[0]

    far = [finish(0, lo, far_part, halo) for lo, halo in zip(starts, far_halo)]
    near_halo, far[-1] = after(near_halo, far[-1])
    near = finish(1, 0, near_part, near_halo)
    later, far[-1] = after(where, far[-1])
    shapes = [(2 * LANES, LANES)] * 3 + [(LANES, 2 * LANES)] * 3
    matrices = run(matrices_body, "matrices", shapes, (later,), smem=1, dtype=jnp.bfloat16)
    pair, even_col, odd_col, pair_t, even_t, odd_t = matrices
    coarse = run(coarse_setup_body, "coarse_setup", [half[1:]], (phase_lin, pair), scratch=[tile])

    far_halo = [swap_far(v) for v in far]
    near_halo = swap_near(near)
    far_part, near_part = run(part_body, "part", [full] * 2, (*far, near, *coefs, own), (len(far),), scratch=[whole])

    def finish_pool(i, lo, part, halo, before=()):
        n = halo.shape[1]
        pool = (2, (n + (lo if before else 0)) // 2, cols // 2)
        args = (keep, part, halo, *coefs, pair, *before)
        outs, scratch = [pool, (2, n, cols)], [tiles(n, cols)] * 2
        return run(finish_pool_body, "finish_pool", outs, args, (i, lo), smem=1, scratch=scratch, work=8)

    far, before = [], ()
    for lo, halo in zip(starts, far_halo):
        far_pool, chunk = finish_pool(0, lo, far_part, halo, before)
        far.append(chunk)
        before = (far_pool,)
    near_pool, near = finish_pool(1, 0, near_part, near_halo)

    far_sums, near_sums = swap_far(far_pool), swap_near(near_pool)
    plane_sums = far_sums
    many = COARSE_SWEEPS - 1
    pieces = [(2, 3 * rows // 2 // many, cols // 2)] * many
    pieces = run(three_body, "three", pieces, (*far, even_col, odd_col), (len(far),), scratch=[tile])
    arrived = [swap_far(pieces[0])]
    near_halo = swap_near(near)
    args, scratch = (*far, near, *coefs, own, pair), [whole, tile, tile]
    far_part, near_part, local = run(
        part_defect_body, "part_defect", [full, full, half], args, (len(far),), scratch=scratch
    )
    fix = run(coarse_first_body, "coarse_first", [half], (keep, local, far_sums, near_sums, *coarse), smem=1, work=8)[0]
    first = fix
    for sweep_index in range(COARSE_SWEEPS - 1):
        far_sums, near_sums = swap_far(fix), swap_near(fix)
        if len(arrived) < len(pieces):
            fix, held = lax.optimization_barrier((fix, pieces[len(arrived)]))
            arrived.append(swap_far(held))
        part = run(coarse_part_body, "coarse_part", [half], (fix, first, *coarse))[0]
        if sweep_index:
            part, arrived[sweep_index - 1] = after(part, arrived[sweep_index - 1])
        args = (keep, part, far_sums, near_sums, *coarse)
        fix = run(coarse_finish_body, "coarse_finish", [half], args, smem=1, work=8)[0]

    far_sums, near_sums = swap_far(fix), swap_near(fix)
    args = (far_part, near_part, fix, near_halo, pair_t, *coefs)
    scratch = [tile] * 2 + [pltpu.VMEM((rows, cols), F32)] * 2
    far_part, near_part = run(third_body, "third", [full, full], args, scratch=scratch)
    plane_sums, far_part = after(plane_sums, far_part)
    state_nb = run(rebuild_body, "rebuild", [full], (plane_sums, *arrived, even_t, odd_t), scratch=[tile] * 2)[0]
    sizes = late_chunks(rows)
    starts = [sum(sizes[:n]) for n in range(len(sizes))]
    args = (keep, far_part, near_part, far_sums, near_sums, state_nb, pair_t, *coefs)
    shapes = [(2, n, cols) for n in sizes]
    scratch = [v for n in [*sizes, rows] for v in [tiles(n, cols)] * 2]
    *far, near = run(fix_body, "fix", [*shapes, full], args, (starts,), smem=1, scratch=scratch, work=8)

    far_halo, near_halo = [swap_far(v) for v in far], swap_near(near)
    far_part, near_part = run(part_body, "part", [full] * 2, (*far, near, *coefs, own), (len(far),), scratch=[whole])
    outs = [(2, 2, rows, cols), full]

    def final(which, fields, done):
        args = (where, keep, *coefs, phase_lin, phase_state, *fields, *done)
        in_specs = [SMEM, SMEM] + [VMEM] * (len(args) - len(done) - 2) + [ANY] * len(done)
        scratch = []
        for halo in fields[1::2]:
            n = halo.shape[1]
            scratch += [pltpu.VMEM((2, n, cols), F32), pltpu.VMEM((n, cols), F32), pltpu.SemaphoreType.DMA((4,))]
        body = functools.partial(final_body, which)
        aliases = {len(args) - 2: 0, len(args) - 1: 1} if done else None
        return call(body, "final", outs, args, in_specs, [ANY, ANY], scratch, aliases, work=10)

    done = ()
    for lo, halo in zip(starts[:-1], far_halo[:-1]):
        done = final([(0, lo)], (far_part, halo), done)
    done = final([(1, 0)], (near_part, near_halo), done)
    done = final([(0, starts[-1])], (far_part, far_halo[-1]), done)
    return tuple(done)


def solution(mesh):
    in_specs = (
        P(("grp", "gx"), None, None),
        P(("grp", "gx"), None, None),
        P(None, ("grp", "gx"), None, None),
        P(None, ("grp", "gx"), None, None),
    )
    out_specs = (P(None, ("grp", "gx"), None, None), P(("grp", "gx"), None, None))
    return jax.shard_map(
        on_device, mesh=mesh, in_specs=in_specs, out_specs=out_specs, check_vma=False
    )
```

```python
import functools

import jax
import jax.numpy as jnp
from jax import lax
from jax.experimental import pallas as pl
from jax.experimental.pallas import tpu as pltpu
from jax.sharding import PartitionSpec as P

SWEEPS = 2
COARSE_SWEEPS = 4

GRADIENT_ENERGY = 1.0
TIME_STEP = 0.02
DAMPING = 0.8
KEEP = 1.0 - DAMPING
COARSE_ENERGY = GRADIENT_ENERGY / 4.0
COARSE_STEP = TIME_STEP / 4.0


VMEM = pl.BlockSpec(memory_space=pltpu.VMEM)
SMEM = pl.BlockSpec(memory_space=pltpu.SMEM)
ANY = pl.BlockSpec(memory_space=pl.ANY)
HBM = pl.BlockSpec(memory_space=pltpu.HBM)
BLOCK = 16
F32 = jnp.float32


def chip_pairs(count):
    return [(i, i ^ 1) for i in range(count)]


def cross_pairs(groups, count):
    pairs = []
    for g in range(groups):
        pairs += [(g * count + i, g * count + i + 1) for i in range(1, count - 1, 2)]
    for g in range(0, groups - 1, 2):
        pairs += [(g * count + i, (g + 1) * count + i) for i in (0, count - 1)]
    swaps = pairs + [(b, a) for a, b in pairs]
    if groups % 2 == 1:
        swaps += [((groups - 1) * count + i,) * 2 for i in (0, count - 1)]
    return swaps


def early_chunks(rows):
    return [5 * rows // 8, 3 * rows // 8]


def call(body, name, outs, args, in_specs=None, out_specs=None, scratch=(), aliases=None, work=30, dtype=F32):
    shapes = [jax.ShapeDtypeStruct(s, dtype) for s in outs]
    size = sum(int(a.size) for a in args)
    made = sum(s.size for s in shapes)
    return pl.pallas_call(
        body,
        out_shape=shapes,
        in_specs=in_specs or [VMEM] * len(args),
        out_specs=out_specs or [VMEM] * len(outs),
        scratch_shapes=list(scratch),
        input_output_aliases=aliases or {},
        name=name,
        cost_estimate=pl.CostEstimate(flops=0, bytes_accessed=4 * (size + made), transcendentals=0),
        compiler_params=pltpu.CompilerParams(vmem_limit_bytes=12 * 1024 * 1024),
    )(*args)


def blocks(rows):
    return range(0, rows, BLOCK)


def around(read, r, rows):
    x = read(r, r + BLOCK)
    cols = x.shape[-1]
    row = lax.broadcasted_iota(jnp.int32, x.shape, 0)
    col = lax.broadcasted_iota(jnp.int32, x.shape, 1)
    up = read(r - 1, r - 1 + BLOCK) if r > 0 else jnp.where(row == 0, 0.0, pltpu.roll(x, 1, 0))
    if r + BLOCK < rows:
        down = read(r + 1, r + 1 + BLOCK)
    else:
        down = jnp.where(row == BLOCK - 1, 0.0, pltpu.roll(x, BLOCK - 1, 0))
    left = jnp.where(col == 0, 0.0, pltpu.roll(x, 1, 1))
    right = jnp.where(col == cols - 1, 0.0, pltpu.roll(x, cols - 1, 1))
    return x, (up + down) + (left + right)


def reader(ref, *lead):
    return lambda lo, hi: ref[(*lead, slice(lo, hi))]


def add_terms(base_p, base_m, gain, nb_p, nb_m, energy, step):
    gain_kt = (DAMPING - gain) * (1.0 / 6.0)
    new_p = base_p - gain * (energy * nb_m) + gain_kt * nb_p
    new_m = base_m + gain * (step * nb_p + (6.0 * step * energy) * nb_m)
    return new_p, new_m


def parts3(x):
    high = x.astype(jnp.bfloat16)
    rest = x - high.astype(F32)
    middle = rest.astype(jnp.bfloat16)
    low = (rest - middle.astype(F32)).astype(jnp.bfloat16)
    return high, middle, low


def times(xs, matrix):
    n, width = xs[0].shape[0], matrix.shape[0]
    pieces = [x[:, j : j + width] for x in xs for j in range(0, x.shape[1], width)]
    stacked = jnp.concatenate([v for piece in pieces for v in parts3(piece)], axis=0)
    out = jnp.dot(stacked, matrix, preferred_element_type=F32)
    sums = [out[j : j + n] + out[j + n : j + 2 * n] + out[j + 2 * n : j + 3 * n] for j in range(0, out.shape[0], 3 * n)]
    each = len(sums) // len(xs)
    return [jnp.concatenate(sums[j : j + each], axis=1) for j in range(0, len(sums), each)]


LANES = 128


def tiles(rows, cols):
    return pltpu.VMEM((cols // LANES, rows, LANES), F32)


def put_rows(ref, rows, x):
    for j in range(ref.shape[0]):
        ref[j, rows] = x[:, j * LANES : (j + 1) * LANES]


def get_rows(ref, rows):
    return jnp.concatenate([ref[j, rows] for j in range(ref.shape[0])], axis=1)


def even_odd(ref):
    half = ref.shape[1] // 2
    return pl.ds(0, half, stride=2), pl.ds(1, half, stride=2)


def pair_rows(ref):
    even, odd = even_odd(ref)
    return get_rows(ref, even) + get_rows(ref, odd)


def take_body(what, where, warm, *refs):
    outs, sems = refs[:-1], refs[-1]
    c = where[0]
    copies = []
    for n, ((is_near, lo), out) in enumerate(zip(what, outs)):
        plane = 1 - c if is_near else c
        rows = pl.ds(lo, out.shape[1])
        copies.append(pltpu.make_async_copy(warm.at[:, plane, rows], out, sems.at[n]))
        copies[-1].start()
    for copy in copies:
        copy.wait()


def matrices_body(where, pair, even_col, odd_col, pair_t, even_t, odd_t):
    for dim, (both, even, odd) in enumerate(((pair, even_col, odd_col), (pair_t, even_t, odd_t))):
        cell = lax.broadcasted_iota(jnp.int32, both.shape, dim)
        coarse = 2 * lax.broadcasted_iota(jnp.int32, both.shape, 1 - dim)
        is_even = jnp.where(cell == coarse, 1.0, 0.0)
        is_odd = jnp.where(cell == coarse + 1, 1.0, 0.0)
        even[...] = is_even.astype(jnp.bfloat16)
        odd[...] = is_odd.astype(jnp.bfloat16)
        both[...] = (is_even + is_odd).astype(jnp.bfloat16)


def setup_body(where, phi, cot, gain, own):
    c = where[0]
    for i in range(2):
        plane = c if i == 0 else 1 - c
        for r in blocks(phi.shape[1]):
            rows = slice(r, r + BLOCK)
            v = phi[plane, rows]
            k = 3.0 * v * v - 1.0 + 6.0 * GRADIENT_ENERGY
            g = DAMPING / (1.0 + 6.0 * TIME_STEP * k)
            s0, s1 = cot[0, plane, rows], cot[1, plane, rows]
            gain[i, rows] = g
            own[i, 0, rows] = g * (s0 + k * s1)
            own[i, 1, rows] = g * (s1 - 6.0 * TIME_STEP * s0)


def coarse_setup_body(phi, pair, gain, both):
    for r in blocks(phi.shape[1]):
        rows = slice(r, r + BLOCK)
        a, b = phi[0, rows], phi[1, rows]
        put_rows(both, rows, (3.0 * a * a - 1.0) + (3.0 * b * b - 1.0))
    k = times([pair_rows(both)], pair[...])[0] / 8.0 + 6.0 * COARSE_ENERGY
    gain[...] = DAMPING / (1.0 + 6.0 * COARSE_STEP * k)


def gather_rows(chunks, whole):
    lo = 0
    for chunk in chunks:
        n = chunk.shape[1]
        for r in blocks(n):
            for f in range(2):
                whole[f, slice(lo + r, lo + r + BLOCK)] = chunk[f, slice(r, r + BLOCK)]
        lo += n


def part_body(count, *refs):
    chunks, (near, gain, own, far_out, near_out, far) = refs[:count], refs[count:]
    gather_rows(chunks, far)
    rows_all = far.shape[1]
    for i, (mine, other, out) in enumerate(((far, near, far_out), (near, far, near_out))):
        for r in blocks(rows_all):
            rows = slice(r, r + BLOCK)
            p, nb_p = around(reader(mine, 0), r, rows_all)
            m, nb_m = around(reader(mine, 1), r, rows_all)
            out[0, rows], out[1, rows] = add_terms(
                KEEP * p + own[i, 0, rows],
                KEEP * m + own[i, 1, rows],
                gain[i, rows],
                nb_p + other[0, rows],
                nb_m + other[1, rows],
                GRADIENT_ENERGY,
                TIME_STEP,
            )


def finish_body(i, lo, keep, part, halo, gain, out):
    for r in blocks(halo.shape[1]):
        rows, whole = slice(r, r + BLOCK), slice(lo + r, lo + r + BLOCK)
        hp, hm = halo[0, rows], halo[1, rows]
        if i == 0:
            hp, hm = hp * keep[0], hm * keep[0]
        out[0, rows], out[1, rows] = add_terms(
            part[0, whole], part[1, whole], gain[i, whole], hp, hm, GRADIENT_ENERGY, TIME_STEP
        )


def finish_pool_body(i, lo, keep, part, halo, gain, pair, *refs):
    before, (pool, out, phase, chem) = refs[:-4], refs[-4:]
    for r in blocks(halo.shape[1]):
        rows, whole = slice(r, r + BLOCK), slice(lo + r, lo + r + BLOCK)
        hp, hm = halo[0, rows], halo[1, rows]
        if i == 0:
            hp, hm = hp * keep[0], hm * keep[0]
        p, m = add_terms(
            part[0, whole], part[1, whole], gain[i, whole], hp, hm, GRADIENT_ENERGY, TIME_STEP
        )
        out[0, rows] = p
        out[1, rows] = m
        put_rows(phase, rows, p)
        put_rows(chem, rows, m)
    sums = times([pair_rows(phase), pair_rows(chem)], pair[...])
    for f in range(2):
        for ref in before:
            pool[f, : lo // 2] = ref[f]
        pool[f, lo // 2 if before else 0 :] = sums[f]


def three_body(count, *refs):
    chunks, (even_col, odd_col), outs, tile = refs[:count], refs[count : count + 2], refs[count + 2 : -1], refs[-1]
    for f in range(2):
        lo = 0
        for chunk in chunks:
            for r in blocks(chunk.shape[1]):
                put_rows(tile, slice(lo + r, lo + r + BLOCK), chunk[f, slice(r, r + BLOCK)])
            lo += chunk.shape[1]
        even, odd = even_odd(tile)
        top, bottom = get_rows(tile, even), get_rows(tile, odd)
        first, third = times([top, bottom], even_col[...])
        second = times([top], odd_col[...])[0]
        values = jnp.concatenate([first, second, third], axis=0)
        n = values.shape[0] // len(outs)
        for j, out in enumerate(outs):
            out[f] = values[j * n : (j + 1) * n]


def part_defect_body(count, *refs):
    chunks, (near, gain, own, pair, far_out, near_out, out, far, phase, chem) = refs[:count], refs[count:]
    part_body(count, *chunks, near, gain, own, far_out, near_out, far)
    for r in blocks(near.shape[1]):
        rows = slice(r, r + BLOCK)
        r0, r1 = 0.0, 0.0
        for i, (mine, new) in enumerate(((far, far_out), (near, near_out))):
            dp, dm = new[0, rows] - mine[0, rows], new[1, rows] - mine[1, rows]
            k = (DAMPING - gain[i, rows]) / (6.0 * TIME_STEP * gain[i, rows])
            r0 = r0 + (dp - k * dm)
            r1 = r1 + (dm + 6.0 * TIME_STEP * dp)
        put_rows(phase, rows, r0)
        put_rows(chem, rows, r1)
    sums = times([pair_rows(phase), pair_rows(chem)], pair[...])
    for f in range(2):
        out[f] = sums[f] * (1.0 / (8.0 * DAMPING))


def coarse_first_body(keep, local, far, near, gain, out):
    for r in blocks(local.shape[1]):
        rows = slice(r, r + BLOCK)
        s0 = local[0, rows] - (GRADIENT_ENERGY / 8.0) * (far[1, rows] * keep[0] + near[1, rows])
        s1 = local[1, rows] + (TIME_STEP / 8.0) * (far[0, rows] * keep[0] + near[0, rows])
        g = gain[rows]
        out[0, rows] = g * s0 + ((DAMPING - g) * (1.0 / (6.0 * COARSE_STEP))) * s1
        out[1, rows] = g * (s1 - 6.0 * COARSE_STEP * s0)


def coarse_part_body(fix, own, gain, out):
    rows_all = fix.shape[1]
    for r in blocks(rows_all):
        rows = slice(r, r + BLOCK)
        p, nb_p = around(reader(fix, 0), r, rows_all)
        m, nb_m = around(reader(fix, 1), r, rows_all)
        out[0, rows], out[1, rows] = add_terms(
            KEEP * p + own[0, rows],
            KEEP * m + own[1, rows],
            gain[rows],
            nb_p,
            nb_m,
            COARSE_ENERGY,
            COARSE_STEP,
        )


def coarse_finish_body(keep, part, far, near, gain, out):
    for r in blocks(part.shape[1]):
        rows = slice(r, r + BLOCK)
        out[0, rows], out[1, rows] = add_terms(
            part[0, rows],
            part[1, rows],
            gain[rows],
            far[0, rows] * keep[0] + near[0, rows],
            far[1, rows] * keep[0] + near[1, rows],
            COARSE_ENERGY,
            COARSE_STEP,
        )


def spread_into(tile_a, tile_b, fix_a, fix_b, pair_t):
    for tile, wide in zip((tile_a, tile_b), times([fix_a, fix_b], pair_t)):
        for rows in even_odd(tile):
            put_rows(tile, rows, wide)


def third_body(far, near, fix, near_halo, pair_t, gain, far_out, near_out, fix_p, fix_m, wide_p, wide_m):
    rows_all = near.shape[1]
    spread_into(fix_p, fix_m, fix[0], fix[1], pair_t[...])
    for r in blocks(rows_all):
        rows = slice(r, r + BLOCK)
        wide_p[rows], wide_m[rows] = get_rows(fix_p, rows), get_rows(fix_m, rows)
    for r in blocks(rows_all):
        rows = slice(r, r + BLOCK)
        p, nb_p = around(lambda lo, hi: wide_p[lo:hi], r, rows_all)
        m, nb_m = around(lambda lo, hi: wide_m[lo:hi], r, rows_all)
        nb_p, nb_m = nb_p + p, nb_m + m
        for i, (part, out) in enumerate(((far, far_out), (near, near_out))):
            xp, xm = (near_halo[0, rows], near_halo[1, rows]) if i == 1 else (0.0, 0.0)
            out[0, rows], out[1, rows] = add_terms(
                part[0, rows] + KEEP * p,
                part[1, rows] + KEEP * m,
                gain[i, rows],
                nb_p + xp,
                nb_m + xm,
                GRADIENT_ENERGY,
                TIME_STEP,
            )


def rebuild_body(sums, *refs):
    pieces, (even_t, odd_t, out, halo_p, halo_m) = refs[:-5], refs[-5:]
    half = sums.shape[1]
    for f, tile in enumerate((halo_p, halo_m)):
        values = jnp.concatenate([piece[f] for piece in pieces], axis=0)
        a, b, c = values[:half], values[half : 2 * half], values[2 * half :]
        d = sums[f] - ((a + b) + c)
        even, odd = even_odd(tile)
        (a, c), (b, d) = times([a, c], even_t[...]), times([b, d], odd_t[...])
        put_rows(tile, even, a + b)
        put_rows(tile, odd, c + d)
        for r in blocks(2 * half):
            rows = slice(r, r + BLOCK)
            out[f, rows] = get_rows(tile, rows)


def finish_fix_rows(i, lo, keep, part, halo, pair_t, gain, out, phase, chem, state_nb=None):
    n = out.shape[1]
    coarse = slice(lo // 2, (lo + n) // 2)
    spread_into(phase, chem, halo[0, coarse], halo[1, coarse], pair_t[...])
    for r in blocks(n):
        rows, whole = slice(r, r + BLOCK), slice(lo + r, lo + r + BLOCK)
        hp, hm = get_rows(phase, rows), get_rows(chem, rows)
        if i == 0:
            hp, hm = (hp + state_nb[0, whole]) * keep[0], (hm + state_nb[1, whole]) * keep[0]
        out[0, rows], out[1, rows] = add_terms(
            part[0, whole], part[1, whole], gain[i, whole], hp, hm, GRADIENT_ENERGY, TIME_STEP
        )


def fix_far_body(keep, part, halo, state_nb, pair_t, gain, out, phase, chem):
    finish_fix_rows(0, 0, keep, part, halo, pair_t, gain, out, phase, chem, state_nb)


def fix_near_body(part, halo, pair_t, gain, out, top, bottom, phase, chem):
    finish_fix_rows(1, 0, None, part, halo, pair_t, gain, out, phase, chem)
    n = top.shape[1]
    for f in range(2):
        for r in blocks(n):
            rows = slice(r, r + BLOCK)
            top[f, rows] = out[f, rows]
            bottom[f, rows] = out[f, slice(n + r, n + r + BLOCK)]


def final_rows(i, lo, where, keep, part, halo, gain, phi, psi, adjoint, design, plane_out, grad_out, sems):
    c = where[0]
    plane = c if i == 0 else 1 - c
    rows_all = halo.shape[1]
    step = rows_all // 2
    copies = []
    for n, start in enumerate(range(0, rows_all, step)):
        for r in range(start, start + step, BLOCK):
            rows, whole = slice(r, r + BLOCK), slice(lo + r, lo + r + BLOCK)
            hp, hm = halo[0, rows], halo[1, rows]
            if i == 0:
                hp, hm = hp * keep[0], hm * keep[0]
            p, m = add_terms(
                part[0, whole], part[1, whole], gain[i, whole], hp, hm, GRADIENT_ENERGY, TIME_STEP
            )
            plane_out[0, rows] = p
            plane_out[1, rows] = m
            grad_out[rows] = 6.0 * phi[plane, whole] * psi[plane, whole] * m
        here, there = pl.ds(start, step), pl.ds(lo + start, step)
        copies.append(pltpu.make_async_copy(plane_out.at[:, here], adjoint.at[:, plane, there], sems.at[2 * n]))
        copies.append(pltpu.make_async_copy(grad_out.at[here], design.at[plane, there], sems.at[2 * n + 1]))
        copies[-2].start()
        copies[-1].start()
    return copies


def final_body(which, where, keep, gain, phi, psi, *refs):
    count = len(which)
    halos, refs = refs[: 2 * count], refs[2 * count :]
    scratch = refs[-3 * count :]
    adjoint, design = refs[-3 * count - 2 : -3 * count]
    copies = []
    for n, (i, lo) in enumerate(which):
        part, halo = halos[2 * n : 2 * n + 2]
        copies += final_rows(
            i, lo, where, keep, part, halo, gain, phi, psi, adjoint, design, *scratch[3 * n : 3 * n + 3]
        )
    for copy in copies:
        copy.wait()


def on_device(phase_lin, phase_state, cotangent, warm_start):
    groups, count = lax.axis_size("grp"), lax.axis_size("gx")
    me = lax.axis_index("gx")
    where = jnp.reshape(me % 2, (1,)).astype(jnp.int32)
    keep = jnp.reshape(((me > 0) & (me < count - 1)).astype(F32), (1,))
    across, on_chip = cross_pairs(groups, count), chip_pairs(count)
    rows, cols = phase_lin.shape[1:]
    full, half = (2, rows, cols), (2, rows // 2, cols // 2)
    sizes = early_chunks(rows)
    starts = [sum(sizes[:n]) for n in range(len(sizes))]

    def swap_far(x):
        return lax.ppermute(x, ("grp", "gx"), across)

    def swap_near(x):
        return lax.ppermute(x, "gx", on_chip)

    def after(x, y):
        return lax.optimization_barrier((x, y))

    whole, tile = pltpu.VMEM(full, F32), tiles(rows, cols)

    def run(body, name, outs, args, statics=(), smem=0, **kw):
        specs = [SMEM] * smem + [VMEM] * (len(args) - smem)
        return call(functools.partial(body, *statics), name, outs, args, specs, **kw)

    def take(what, name):
        outs = [(2, n, cols) for _, _, n in what]
        body = functools.partial(take_body, [(is_near, lo) for is_near, lo, _ in what])
        scratch = [pltpu.SemaphoreType.DMA((len(what),))]
        source = pltpu.with_memory_space_constraint(warm_start, pltpu.HBM)
        return call(body, name, outs, (where, source), [SMEM, HBM], scratch=scratch, work=0)

    *far, near = take([(False, lo, n) for lo, n in zip(starts, sizes)] + [(True, 0, rows)], "take")
    far_halo = [swap_far(v) for v in far]
    near_halo = swap_near(near)
    gain, own = run(setup_body, "setup", [full, (2, 2, rows, cols)], (where, phase_lin, cotangent), smem=1)
    coefs = (gain,)
    far_part, near_part = run(part_body, "part", [full] * 2, (*far, near, *coefs, own), (len(far),), scratch=[whole])
    def finish(i, lo, part, halo):
        shape = (2, halo.shape[1], cols)
        return run(finish_body, "finish", [shape], (keep, part, halo, *coefs), (i, lo), smem=1, work=8)[0]

    far = [finish(0, lo, far_part, halo) for lo, halo in zip(starts, far_halo)]
    near_halo, far[-1] = after(near_halo, far[-1])
    near = finish(1, 0, near_part, near_halo)
    later, far[-1] = after(where, far[-1])
    shapes = [(2 * LANES, LANES)] * 3 + [(LANES, 2 * LANES)] * 3
    matrices = run(matrices_body, "matrices", shapes, (later,), smem=1, dtype=jnp.bfloat16)
    pair, even_col, odd_col, pair_t, even_t, odd_t = matrices
    coarse = run(coarse_setup_body, "coarse_setup", [half[1:]], (phase_lin, pair), scratch=[tile])

    far_halo = [swap_far(v) for v in far]
    near_halo = swap_near(near)
    far_part, near_part = run(part_body, "part", [full] * 2, (*far, near, *coefs, own), (len(far),), scratch=[whole])

    def finish_pool(i, lo, part, halo, before=()):
        n = halo.shape[1]
        pool = (2, (n + (lo if before else 0)) // 2, cols // 2)
        args = (keep, part, halo, *coefs, pair, *before)
        outs, scratch = [pool, (2, n, cols)], [tiles(n, cols)] * 2
        return run(finish_pool_body, "finish_pool", outs, args, (i, lo), smem=1, scratch=scratch, work=8)

    far, before = [], ()
    for lo, halo in zip(starts, far_halo):
        far_pool, chunk = finish_pool(0, lo, far_part, halo, before)
        far.append(chunk)
        before = (far_pool,)
    near_pool, near = finish_pool(1, 0, near_part, near_halo)

    far_sums, near_sums = swap_far(far_pool), swap_near(near_pool)
    plane_sums = far_sums
    many = COARSE_SWEEPS - 1
    pieces = [(2, 3 * rows // 2 // many, cols // 2)] * many
    pieces = run(three_body, "three", pieces, (*far, even_col, odd_col), (len(far),), scratch=[tile])
    arrived = [swap_far(pieces[0])]
    near_halo = swap_near(near)
    args, scratch = (*far, near, *coefs, own, pair), [whole, tile, tile]
    far_part, near_part, local = run(
        part_defect_body, "part_defect", [full, full, half], args, (len(far),), scratch=scratch
    )
    fix = run(coarse_first_body, "coarse_first", [half], (keep, local, far_sums, near_sums, *coarse), smem=1, work=8)[0]
    first = fix
    for sweep_index in range(COARSE_SWEEPS - 1):
        far_sums, near_sums = swap_far(fix), swap_near(fix)
        if len(arrived) < len(pieces):
            fix, held = lax.optimization_barrier((fix, pieces[len(arrived)]))
            arrived.append(swap_far(held))
        part = run(coarse_part_body, "coarse_part", [half], (fix, first, *coarse))[0]
        if sweep_index:
            part, arrived[sweep_index - 1] = after(part, arrived[sweep_index - 1])
        args = (keep, part, far_sums, near_sums, *coarse)
        fix = run(coarse_finish_body, "coarse_finish", [half], args, smem=1, work=8)[0]

    far_sums, near_sums = swap_far(fix), swap_near(fix)
    args = (far_part, near_part, fix, near_halo, pair_t, *coefs)
    scratch = [tile] * 2 + [pltpu.VMEM((rows, cols), F32)] * 2
    far_part, near_part = run(third_body, "third", [full, full], args, scratch=scratch)
    plane_sums, far_part = after(plane_sums, far_part)
    state_nb = run(rebuild_body, "rebuild", [full], (plane_sums, *arrived, even_t, odd_t), scratch=[tile] * 2)[0]
    args = (keep, far_part, far_sums, state_nb, pair_t, *coefs)
    far = run(fix_far_body, "fix_far", [full], args, smem=1, scratch=[tile] * 2, work=8)
    starts = [0]
    top = (2, rows // 2, cols)
    args = (near_part, near_sums, pair_t, *coefs)
    near, *near_chunks = run(fix_near_body, "fix_near", [full, top, top], args, scratch=[tile] * 2, work=8)

    far_halo, near_halos = [swap_far(v) for v in far], [swap_near(v) for v in near_chunks]
    far_part, near_part = run(part_body, "part", [full] * 2, (*far, near, *coefs, own), (len(far),), scratch=[whole])
    outs = [(2, 2, rows, cols), full]

    def final(which, fields, done):
        args = (where, keep, *coefs, phase_lin, phase_state, *fields, *done)
        in_specs = [SMEM, SMEM] + [VMEM] * (len(args) - len(done) - 2) + [ANY] * len(done)
        scratch = []
        for halo in fields[1::2]:
            n = halo.shape[1]
            scratch += [pltpu.VMEM((2, n, cols), F32), pltpu.VMEM((n, cols), F32), pltpu.SemaphoreType.DMA((4,))]
        body = functools.partial(final_body, which)
        aliases = {len(args) - 2: 0, len(args) - 1: 1} if done else None
        return call(body, "final", outs, args, in_specs, [ANY, ANY], scratch, aliases, work=10)

    done = ()
    for lo, halo in zip(starts[:-1], far_halo[:-1]):
        done = final([(0, lo)], (far_part, halo), done)
    fields = (near_part, near_halos[0], near_part, near_halos[1])
    done = final([(1, 0), (1, rows // 2)], fields, done)
    done = final([(0, starts[-1])], (far_part, far_halo[-1]), done)
    return tuple(done)


def solution(mesh):
    in_specs = (
        P(("grp", "gx"), None, None),
        P(("grp", "gx"), None, None),
        P(None, ("grp", "gx"), None, None),
        P(None, ("grp", "gx"), None, None),
    )
    out_specs = (P(None, ("grp", "gx"), None, None), P(("grp", "gx"), None, None))
    return jax.shard_map(
        on_device, mesh=mesh, in_specs=in_specs, out_specs=out_specs, check_vma=False
    )
```

```python
import functools

import jax
import jax.numpy as jnp
from jax import lax
from jax.experimental import pallas as pl
from jax.experimental.pallas import tpu as pltpu
from jax.sharding import PartitionSpec as P

SWEEPS = 2
COARSE_SWEEPS = 4

GRADIENT_ENERGY = 1.0
TIME_STEP = 0.02
DAMPING = 0.8
KEEP = 1.0 - DAMPING
COARSE_ENERGY = GRADIENT_ENERGY / 4.0
COARSE_STEP = TIME_STEP / 4.0


VMEM = pl.BlockSpec(memory_space=pltpu.VMEM)
SMEM = pl.BlockSpec(memory_space=pltpu.SMEM)
ANY = pl.BlockSpec(memory_space=pl.ANY)
HBM = pl.BlockSpec(memory_space=pltpu.HBM)
BLOCK = 16
F32 = jnp.float32


def chip_pairs(count):
    return [(i, i ^ 1) for i in range(count)]


def cross_pairs(groups, count):
    pairs = []
    for g in range(groups):
        pairs += [(g * count + i, g * count + i + 1) for i in range(1, count - 1, 2)]
    for g in range(0, groups - 1, 2):
        pairs += [(g * count + i, (g + 1) * count + i) for i in (0, count - 1)]
    swaps = pairs + [(b, a) for a, b in pairs]
    if groups % 2 == 1:
        swaps += [((groups - 1) * count + i,) * 2 for i in (0, count - 1)]
    return swaps


def early_chunks(rows):
    return [5 * rows // 8, 3 * rows // 8]


def call(body, name, outs, args, in_specs=None, out_specs=None, scratch=(), aliases=None, work=30, dtype=F32):
    shapes = [jax.ShapeDtypeStruct(s, dtype) for s in outs]
    size = sum(int(a.size) for a in args)
    made = sum(s.size for s in shapes)
    return pl.pallas_call(
        body,
        out_shape=shapes,
        in_specs=in_specs or [VMEM] * len(args),
        out_specs=out_specs or [VMEM] * len(outs),
        scratch_shapes=list(scratch),
        input_output_aliases=aliases or {},
        name=name,
        cost_estimate=pl.CostEstimate(flops=0, bytes_accessed=4 * (size + made), transcendentals=0),
        compiler_params=pltpu.CompilerParams(vmem_limit_bytes=12 * 1024 * 1024),
    )(*args)


def blocks(rows):
    return range(0, rows, BLOCK)


def around(read, r, rows):
    x = read(r, r + BLOCK)
    cols = x.shape[-1]
    row = lax.broadcasted_iota(jnp.int32, x.shape, 0)
    col = lax.broadcasted_iota(jnp.int32, x.shape, 1)
    up = read(r - 1, r - 1 + BLOCK) if r > 0 else jnp.where(row == 0, 0.0, pltpu.roll(x, 1, 0))
    if r + BLOCK < rows:
        down = read(r + 1, r + 1 + BLOCK)
    else:
        down = jnp.where(row == BLOCK - 1, 0.0, pltpu.roll(x, BLOCK - 1, 0))
    left = jnp.where(col == 0, 0.0, pltpu.roll(x, 1, 1))
    right = jnp.where(col == cols - 1, 0.0, pltpu.roll(x, cols - 1, 1))
    return x, (up + down) + (left + right)


def reader(ref, *lead):
    return lambda lo, hi: ref[(*lead, slice(lo, hi))]


def add_terms(base_p, base_m, gain, nb_p, nb_m, energy, step):
    gain_kt = (DAMPING - gain) * (1.0 / 6.0)
    new_p = base_p - gain * (energy * nb_m) + gain_kt * nb_p
    new_m = base_m + gain * (step * nb_p + (6.0 * step * energy) * nb_m)
    return new_p, new_m


def parts3(x):
    high = x.astype(jnp.bfloat16)
    rest = x - high.astype(F32)
    middle = rest.astype(jnp.bfloat16)
    low = (rest - middle.astype(F32)).astype(jnp.bfloat16)
    return high, middle, low


def times(xs, matrix):
    n, width = xs[0].shape[0], matrix.shape[0]
    pieces = [x[:, j : j + width] for x in xs for j in range(0, x.shape[1], width)]
    stacked = jnp.concatenate([v for piece in pieces for v in parts3(piece)], axis=0)
    out = jnp.dot(stacked, matrix, preferred_element_type=F32)
    sums = [out[j : j + n] + out[j + n : j + 2 * n] + out[j + 2 * n : j + 3 * n] for j in range(0, out.shape[0], 3 * n)]
    each = len(sums) // len(xs)
    return [jnp.concatenate(sums[j : j + each], axis=1) for j in range(0, len(sums), each)]


LANES = 128


def tiles(rows, cols):
    return pltpu.VMEM((cols // LANES, rows, LANES), F32)


def put_rows(ref, rows, x):
    for j in range(ref.shape[0]):
        ref[j, rows] = x[:, j * LANES : (j + 1) * LANES]


def get_rows(ref, rows):
    return jnp.concatenate([ref[j, rows] for j in range(ref.shape[0])], axis=1)


def even_odd(ref):
    half = ref.shape[1] // 2
    return pl.ds(0, half, stride=2), pl.ds(1, half, stride=2)


def pair_rows(ref):
    even, odd = even_odd(ref)
    return get_rows(ref, even) + get_rows(ref, odd)


def take_body(what, where, warm, *refs):
    outs, sems = refs[:-1], refs[-1]
    c = where[0]
    copies = []
    for n, ((is_near, lo), out) in enumerate(zip(what, outs)):
        plane = 1 - c if is_near else c
        rows = pl.ds(lo, out.shape[1])
        copies.append(pltpu.make_async_copy(warm.at[:, plane, rows], out, sems.at[n]))
        copies[-1].start()
    for copy in copies:
        copy.wait()


def matrices_body(where, pair, even_col, odd_col, pair_t, even_t, odd_t):
    for dim, (both, even, odd) in enumerate(((pair, even_col, odd_col), (pair_t, even_t, odd_t))):
        cell = lax.broadcasted_iota(jnp.int32, both.shape, dim)
        coarse = 2 * lax.broadcasted_iota(jnp.int32, both.shape, 1 - dim)
        is_even = jnp.where(cell == coarse, 1.0, 0.0)
        is_odd = jnp.where(cell == coarse + 1, 1.0, 0.0)
        even[...] = is_even.astype(jnp.bfloat16)
        odd[...] = is_odd.astype(jnp.bfloat16)
        both[...] = (is_even + is_odd).astype(jnp.bfloat16)


def setup_body(where, phi, cot, gain, own):
    c = where[0]
    for i in range(2):
        plane = c if i == 0 else 1 - c
        for r in blocks(phi.shape[1]):
            rows = slice(r, r + BLOCK)
            v = phi[plane, rows]
            k = 3.0 * v * v - 1.0 + 6.0 * GRADIENT_ENERGY
            g = DAMPING / (1.0 + 6.0 * TIME_STEP * k)
            s0, s1 = cot[0, plane, rows], cot[1, plane, rows]
            gain[i, rows] = g
            own[i, 0, rows] = g * (s0 + k * s1)
            own[i, 1, rows] = g * (s1 - 6.0 * TIME_STEP * s0)


def coarse_setup_body(phi, pair, gain, both):
    for r in blocks(phi.shape[1]):
        rows = slice(r, r + BLOCK)
        a, b = phi[0, rows], phi[1, rows]
        put_rows(both, rows, (3.0 * a * a - 1.0) + (3.0 * b * b - 1.0))
    k = times([pair_rows(both)], pair[...])[0] / 8.0 + 6.0 * COARSE_ENERGY
    gain[...] = DAMPING / (1.0 + 6.0 * COARSE_STEP * k)


def gather_rows(chunks, whole):
    lo = 0
    for chunk in chunks:
        n = chunk.shape[1]
        for r in blocks(n):
            for f in range(2):
                whole[f, slice(lo + r, lo + r + BLOCK)] = chunk[f, slice(r, r + BLOCK)]
        lo += n


def part_body(count, *refs):
    chunks, (near, gain, own, far_out, near_out, far) = refs[:count], refs[count:]
    gather_rows(chunks, far)
    rows_all = far.shape[1]
    for i, (mine, other, out) in enumerate(((far, near, far_out), (near, far, near_out))):
        for r in blocks(rows_all):
            rows = slice(r, r + BLOCK)
            p, nb_p = around(reader(mine, 0), r, rows_all)
            m, nb_m = around(reader(mine, 1), r, rows_all)
            out[0, rows], out[1, rows] = add_terms(
                KEEP * p + own[i, 0, rows],
                KEEP * m + own[i, 1, rows],
                gain[i, rows],
                nb_p + other[0, rows],
                nb_m + other[1, rows],
                GRADIENT_ENERGY,
                TIME_STEP,
            )


def finish_body(i, lo, keep, part, halo, gain, out):
    for r in blocks(halo.shape[1]):
        rows, whole = slice(r, r + BLOCK), slice(lo + r, lo + r + BLOCK)
        hp, hm = halo[0, rows], halo[1, rows]
        if i == 0:
            hp, hm = hp * keep[0], hm * keep[0]
        out[0, rows], out[1, rows] = add_terms(
            part[0, whole], part[1, whole], gain[i, whole], hp, hm, GRADIENT_ENERGY, TIME_STEP
        )


def finish_pool_body(i, lo, keep, part, halo, gain, pair, *refs):
    before, (pool, out, phase, chem) = refs[:-4], refs[-4:]
    for r in blocks(halo.shape[1]):
        rows, whole = slice(r, r + BLOCK), slice(lo + r, lo + r + BLOCK)
        hp, hm = halo[0, rows], halo[1, rows]
        if i == 0:
            hp, hm = hp * keep[0], hm * keep[0]
        p, m = add_terms(
            part[0, whole], part[1, whole], gain[i, whole], hp, hm, GRADIENT_ENERGY, TIME_STEP
        )
        out[0, rows] = p
        out[1, rows] = m
        put_rows(phase, rows, p)
        put_rows(chem, rows, m)
    sums = times([pair_rows(phase), pair_rows(chem)], pair[...])
    for f in range(2):
        for ref in before:
            pool[f, : lo // 2] = ref[f]
        pool[f, lo // 2 if before else 0 :] = sums[f]


def three_body(count, *refs):
    chunks, (even_col, odd_col), outs, tile = refs[:count], refs[count : count + 2], refs[count + 2 : -1], refs[-1]
    for f in range(2):
        lo = 0
        for chunk in chunks:
            for r in blocks(chunk.shape[1]):
                put_rows(tile, slice(lo + r, lo + r + BLOCK), chunk[f, slice(r, r + BLOCK)])
            lo += chunk.shape[1]
        even, odd = even_odd(tile)
        top, bottom = get_rows(tile, even), get_rows(tile, odd)
        first, third = times([top, bottom], even_col[...])
        second = times([top], odd_col[...])[0]
        values = jnp.concatenate([first, second, third], axis=0)
        n = values.shape[0] // len(outs)
        for j, out in enumerate(outs):
            out[f] = values[j * n : (j + 1) * n]


def part_defect_body(count, *refs):
    chunks, (near, gain, own, pair, far_out, near_out, out, far, phase, chem) = refs[:count], refs[count:]
    part_body(count, *chunks, near, gain, own, far_out, near_out, far)
    for r in blocks(near.shape[1]):
        rows = slice(r, r + BLOCK)
        r0, r1 = 0.0, 0.0
        for i, (mine, new) in enumerate(((far, far_out), (near, near_out))):
            dp, dm = new[0, rows] - mine[0, rows], new[1, rows] - mine[1, rows]
            k = (DAMPING - gain[i, rows]) / (6.0 * TIME_STEP * gain[i, rows])
            r0 = r0 + (dp - k * dm)
            r1 = r1 + (dm + 6.0 * TIME_STEP * dp)
        put_rows(phase, rows, r0)
        put_rows(chem, rows, r1)
    sums = times([pair_rows(phase), pair_rows(chem)], pair[...])
    for f in range(2):
        out[f] = sums[f] * (1.0 / (8.0 * DAMPING))


def coarse_first_body(keep, local, far, near, gain, out):
    for r in blocks(local.shape[1]):
        rows = slice(r, r + BLOCK)
        s0 = local[0, rows] - (GRADIENT_ENERGY / 8.0) * (far[1, rows] * keep[0] + near[1, rows])
        s1 = local[1, rows] + (TIME_STEP / 8.0) * (far[0, rows] * keep[0] + near[0, rows])
        g = gain[rows]
        out[0, rows] = g * s0 + ((DAMPING - g) * (1.0 / (6.0 * COARSE_STEP))) * s1
        out[1, rows] = g * (s1 - 6.0 * COARSE_STEP * s0)


def coarse_part_body(fix, own, gain, out):
    rows_all = fix.shape[1]
    for r in blocks(rows_all):
        rows = slice(r, r + BLOCK)
        p, nb_p = around(reader(fix, 0), r, rows_all)
        m, nb_m = around(reader(fix, 1), r, rows_all)
        out[0, rows], out[1, rows] = add_terms(
            KEEP * p + own[0, rows],
            KEEP * m + own[1, rows],
            gain[rows],
            nb_p,
            nb_m,
            COARSE_ENERGY,
            COARSE_STEP,
        )


def coarse_finish_body(keep, part, far, near, gain, out):
    for r in blocks(part.shape[1]):
        rows = slice(r, r + BLOCK)
        out[0, rows], out[1, rows] = add_terms(
            part[0, rows],
            part[1, rows],
            gain[rows],
            far[0, rows] * keep[0] + near[0, rows],
            far[1, rows] * keep[0] + near[1, rows],
            COARSE_ENERGY,
            COARSE_STEP,
        )


def spread_into(tile_a, tile_b, fix_a, fix_b, pair_t):
    for tile, wide in zip((tile_a, tile_b), times([fix_a, fix_b], pair_t)):
        for rows in even_odd(tile):
            put_rows(tile, rows, wide)


def third_body(far, near, fix, near_halo, pair_t, gain, far_out, near_out, fix_p, fix_m, wide_p, wide_m):
    rows_all = near.shape[1]
    spread_into(fix_p, fix_m, fix[0], fix[1], pair_t[...])
    for r in blocks(rows_all):
        rows = slice(r, r + BLOCK)
        wide_p[rows], wide_m[rows] = get_rows(fix_p, rows), get_rows(fix_m, rows)
    for r in blocks(rows_all):
        rows = slice(r, r + BLOCK)
        p, nb_p = around(lambda lo, hi: wide_p[lo:hi], r, rows_all)
        m, nb_m = around(lambda lo, hi: wide_m[lo:hi], r, rows_all)
        nb_p, nb_m = nb_p + p, nb_m + m
        for i, (part, out) in enumerate(((far, far_out), (near, near_out))):
            xp, xm = (near_halo[0, rows], near_halo[1, rows]) if i == 1 else (0.0, 0.0)
            out[0, rows], out[1, rows] = add_terms(
                part[0, rows] + KEEP * p,
                part[1, rows] + KEEP * m,
                gain[i, rows],
                nb_p + xp,
                nb_m + xm,
                GRADIENT_ENERGY,
                TIME_STEP,
            )


def rebuild_body(sums, *refs):
    pieces, (even_t, odd_t, out, halo_p, halo_m) = refs[:-5], refs[-5:]
    half = sums.shape[1]
    for f, tile in enumerate((halo_p, halo_m)):
        values = jnp.concatenate([piece[f] for piece in pieces], axis=0)
        a, b, c = values[:half], values[half : 2 * half], values[2 * half :]
        d = sums[f] - ((a + b) + c)
        even, odd = even_odd(tile)
        (a, c), (b, d) = times([a, c], even_t[...]), times([b, d], odd_t[...])
        put_rows(tile, even, a + b)
        put_rows(tile, odd, c + d)
        for r in blocks(2 * half):
            rows = slice(r, r + BLOCK)
            out[f, rows] = get_rows(tile, rows)


def finish_fix_rows(i, lo, keep, part, halo, pair_t, gain, out, phase, chem, state_nb=None):
    n = out.shape[1]
    coarse = slice(lo // 2, (lo + n) // 2)
    spread_into(phase, chem, halo[0, coarse], halo[1, coarse], pair_t[...])
    for r in blocks(n):
        rows, whole = slice(r, r + BLOCK), slice(lo + r, lo + r + BLOCK)
        hp, hm = get_rows(phase, rows), get_rows(chem, rows)
        if i == 0:
            hp, hm = (hp + state_nb[0, whole]) * keep[0], (hm + state_nb[1, whole]) * keep[0]
        out[0, rows], out[1, rows] = add_terms(
            part[0, whole], part[1, whole], gain[i, whole], hp, hm, GRADIENT_ENERGY, TIME_STEP
        )


def fix_far_body(keep, part, halo, state_nb, pair_t, gain, out, phase, chem):
    finish_fix_rows(0, 0, keep, part, halo, pair_t, gain, out, phase, chem, state_nb)


def fix_near_body(part, halo, pair_t, gain, out, top, bottom, phase, chem):
    finish_fix_rows(1, 0, None, part, halo, pair_t, gain, out, phase, chem)
    n = top.shape[1]
    for f in range(2):
        for r in blocks(n):
            rows = slice(r, r + BLOCK)
            top[f, rows] = out[f, rows]
            bottom[f, rows] = out[f, slice(n + r, n + r + BLOCK)]


def final_rows(i, lo, where, keep, part, halo, gain, phi, psi, adjoint, design, plane_out, grad_out, sems):
    c = where[0]
    plane = c if i == 0 else 1 - c
    rows_all = halo.shape[1]
    step = rows_all // 2
    copies = []
    for n, start in enumerate(range(0, rows_all, step)):
        for r in range(start, start + step, BLOCK):
            rows, whole = slice(r, r + BLOCK), slice(lo + r, lo + r + BLOCK)
            hp, hm = halo[0, rows], halo[1, rows]
            if i == 0:
                hp, hm = hp * keep[0], hm * keep[0]
            p, m = add_terms(
                part[0, whole], part[1, whole], gain[i, whole], hp, hm, GRADIENT_ENERGY, TIME_STEP
            )
            plane_out[0, rows] = p
            plane_out[1, rows] = m
            grad_out[rows] = 6.0 * phi[plane, whole] * psi[plane, whole] * m
        here, there = pl.ds(start, step), pl.ds(lo + start, step)
        copies.append(pltpu.make_async_copy(plane_out.at[:, here], adjoint.at[:, plane, there], sems.at[2 * n]))
        copies.append(pltpu.make_async_copy(grad_out.at[here], design.at[plane, there], sems.at[2 * n + 1]))
        copies[-2].start()
        copies[-1].start()
    return copies


def final_body(which, where, keep, gain, phi, psi, *refs):
    count = len(which)
    halos, refs = refs[: 2 * count], refs[2 * count :]
    scratch = refs[-3 * count :]
    adjoint, design = refs[-3 * count - 2 : -3 * count]
    copies = []
    for n, (i, lo) in enumerate(which):
        part, halo = halos[2 * n : 2 * n + 2]
        copies += final_rows(
            i, lo, where, keep, part, halo, gain, phi, psi, adjoint, design, *scratch[3 * n : 3 * n + 3]
        )
    for copy in copies:
        copy.wait()


def on_device(phase_lin, phase_state, cotangent, warm_start):
    groups, count = lax.axis_size("grp"), lax.axis_size("gx")
    me = lax.axis_index("gx")
    where = jnp.reshape(me % 2, (1,)).astype(jnp.int32)
    keep = jnp.reshape(((me > 0) & (me < count - 1)).astype(F32), (1,))
    across, on_chip = cross_pairs(groups, count), chip_pairs(count)
    rows, cols = phase_lin.shape[1:]
    full, half = (2, rows, cols), (2, rows // 2, cols // 2)
    sizes = early_chunks(rows)
    starts = [sum(sizes[:n]) for n in range(len(sizes))]

    def swap_far(x):
        return lax.ppermute(x, ("grp", "gx"), across)

    def swap_near(x):
        return lax.ppermute(x, "gx", on_chip)

    def after(x, y):
        return lax.optimization_barrier((x, y))

    whole, tile = pltpu.VMEM(full, F32), tiles(rows, cols)

    def run(body, name, outs, args, statics=(), smem=0, **kw):
        specs = [SMEM] * smem + [VMEM] * (len(args) - smem)
        return call(functools.partial(body, *statics), name, outs, args, specs, **kw)

    def take(what, name):
        outs = [(2, n, cols) for _, _, n in what]
        body = functools.partial(take_body, [(is_near, lo) for is_near, lo, _ in what])
        scratch = [pltpu.SemaphoreType.DMA((len(what),))]
        source = pltpu.with_memory_space_constraint(warm_start, pltpu.HBM)
        return call(body, name, outs, (where, source), [SMEM, HBM], scratch=scratch, work=0)

    *far, near = take([(False, lo, n) for lo, n in zip(starts, sizes)] + [(True, 0, rows)], "take")
    far_halo = [swap_far(v) for v in far]
    near_halo = swap_near(near)
    gain, own = run(setup_body, "setup", [full, (2, 2, rows, cols)], (where, phase_lin, cotangent), smem=1)
    coefs = (gain,)
    far_part, near_part = run(part_body, "part", [full] * 2, (*far, near, *coefs, own), (len(far),), scratch=[whole])
    def finish(i, lo, part, halo):
        shape = (2, halo.shape[1], cols)
        return run(finish_body, "finish", [shape], (keep, part, halo, *coefs), (i, lo), smem=1, work=8)[0]

    far = [finish(0, lo, far_part, halo) for lo, halo in zip(starts, far_halo)]
    near_halo, far[-1] = after(near_halo, far[-1])
    near = finish(1, 0, near_part, near_halo)
    later, far[-1] = after(where, far[-1])
    shapes = [(2 * LANES, LANES)] * 3 + [(LANES, 2 * LANES)] * 3
    matrices = run(matrices_body, "matrices", shapes, (later,), smem=1, dtype=jnp.bfloat16)
    pair, even_col, odd_col, pair_t, even_t, odd_t = matrices
    coarse = run(coarse_setup_body, "coarse_setup", [half[1:]], (phase_lin, pair), scratch=[tile])

    far_halo = [swap_far(v) for v in far]
    near_halo = swap_near(near)
    far_part, near_part = run(part_body, "part", [full] * 2, (*far, near, *coefs, own), (len(far),), scratch=[whole])

    def finish_pool(i, lo, part, halo, before=()):
        n = halo.shape[1]
        pool = (2, (n + (lo if before else 0)) // 2, cols // 2)
        args = (keep, part, halo, *coefs, pair, *before)
        outs, scratch = [pool, (2, n, cols)], [tiles(n, cols)] * 2
        return run(finish_pool_body, "finish_pool", outs, args, (i, lo), smem=1, scratch=scratch, work=8)

    far, before = [], ()
    for lo, halo in zip(starts, far_halo):
        far_pool, chunk = finish_pool(0, lo, far_part, halo, before)
        far.append(chunk)
        before = (far_pool,)
    near_pool, near = finish_pool(1, 0, near_part, near_halo)

    far_sums, near_sums = swap_far(far_pool), swap_near(near_pool)
    plane_sums = far_sums
    many = COARSE_SWEEPS - 1
    pieces = [(2, 3 * rows // 2 // many, cols // 2)] * many
    pieces = run(three_body, "three", pieces, (*far, even_col, odd_col), (len(far),), scratch=[tile])
    arrived = [swap_far(pieces[0])]
    near_halo = swap_near(near)
    args, scratch = (*far, near, *coefs, own, pair), [whole, tile, tile]
    far_part, near_part, local = run(
        part_defect_body, "part_defect", [full, full, half], args, (len(far),), scratch=scratch
    )
    fix = run(coarse_first_body, "coarse_first", [half], (keep, local, far_sums, near_sums, *coarse), smem=1, work=8)[0]
    first = fix
    for sweep_index in range(COARSE_SWEEPS - 1):
        far_sums, near_sums = swap_far(fix), swap_near(fix)
        part = run(coarse_part_body, "coarse_part", [half], (fix, first, *coarse))[0]
        if len(arrived) < len(pieces):
            held, part = after(pieces[len(arrived)], part)
            arrived.append(swap_far(held))
        if sweep_index:
            part, arrived[sweep_index - 1] = after(part, arrived[sweep_index - 1])
        args = (keep, part, far_sums, near_sums, *coarse)
        fix = run(coarse_finish_body, "coarse_finish", [half], args, smem=1, work=8)[0]

    far_sums, near_sums = swap_far(fix), swap_near(fix)
    args = (far_part, near_part, fix, near_halo, pair_t, *coefs)
    scratch = [tile] * 2 + [pltpu.VMEM((rows, cols), F32)] * 2
    far_part, near_part = run(third_body, "third", [full, full], args, scratch=scratch)
    plane_sums, far_part = after(plane_sums, far_part)
    state_nb = run(rebuild_body, "rebuild", [full], (plane_sums, *arrived, even_t, odd_t), scratch=[tile] * 2)[0]
    args = (keep, far_part, far_sums, state_nb, pair_t, *coefs)
    far = run(fix_far_body, "fix_far", [full], args, smem=1, scratch=[tile] * 2, work=8)
    starts = [0]
    top = (2, rows // 2, cols)
    args = (near_part, near_sums, pair_t, *coefs)
    near, *near_chunks = run(fix_near_body, "fix_near", [full, top, top], args, scratch=[tile] * 2, work=8)

    far_halo, near_halos = [swap_far(v) for v in far], [swap_near(v) for v in near_chunks]
    far_part, near_part = run(part_body, "part", [full] * 2, (*far, near, *coefs, own), (len(far),), scratch=[whole])
    outs = [(2, 2, rows, cols), full]

    def final(which, fields, done):
        args = (where, keep, *coefs, phase_lin, phase_state, *fields, *done)
        in_specs = [SMEM, SMEM] + [VMEM] * (len(args) - len(done) - 2) + [ANY] * len(done)
        scratch = []
        for halo in fields[1::2]:
            n = halo.shape[1]
            scratch += [pltpu.VMEM((2, n, cols), F32), pltpu.VMEM((n, cols), F32), pltpu.SemaphoreType.DMA((4,))]
        body = functools.partial(final_body, which)
        aliases = {len(args) - 2: 0, len(args) - 1: 1} if done else None
        return call(body, "final", outs, args, in_specs, [ANY, ANY], scratch, aliases, work=10)

    done = ()
    for lo, halo in zip(starts[:-1], far_halo[:-1]):
        done = final([(0, lo)], (far_part, halo), done)
    fields = (near_part, near_halos[0], near_part, near_halos[1])
    done = final([(1, 0), (1, rows // 2)], fields, done)
    done = final([(0, starts[-1])], (far_part, far_halo[-1]), done)
    return tuple(done)


def solution(mesh):
    in_specs = (
        P(("grp", "gx"), None, None),
        P(("grp", "gx"), None, None),
        P(None, ("grp", "gx"), None, None),
        P(None, ("grp", "gx"), None, None),
    )
    out_specs = (P(None, ("grp", "gx"), None, None), P(("grp", "gx"), None, None))
    return jax.shard_map(
        on_device, mesh=mesh, in_specs=in_specs, out_specs=out_specs, check_vma=False
    )
```

```python
import functools

import jax
import jax.numpy as jnp
from jax import lax
from jax.experimental import pallas as pl
from jax.experimental.pallas import tpu as pltpu
from jax.sharding import PartitionSpec as P

SWEEPS = 2
COARSE_SWEEPS = 4

GRADIENT_ENERGY = 1.0
TIME_STEP = 0.02
DAMPING = 0.8
KEEP = 1.0 - DAMPING
COARSE_ENERGY = GRADIENT_ENERGY / 4.0
COARSE_STEP = TIME_STEP / 4.0


VMEM = pl.BlockSpec(memory_space=pltpu.VMEM)
SMEM = pl.BlockSpec(memory_space=pltpu.SMEM)
ANY = pl.BlockSpec(memory_space=pl.ANY)
HBM = pl.BlockSpec(memory_space=pltpu.HBM)
BLOCK = 16
F32 = jnp.float32


def chip_pairs(count):
    return [(i, i ^ 1) for i in range(count)]


def cross_pairs(groups, count):
    pairs = []
    for g in range(groups):
        pairs += [(g * count + i, g * count + i + 1) for i in range(1, count - 1, 2)]
    for g in range(0, groups - 1, 2):
        pairs += [(g * count + i, (g + 1) * count + i) for i in (0, count - 1)]
    swaps = pairs + [(b, a) for a, b in pairs]
    if groups % 2 == 1:
        swaps += [((groups - 1) * count + i,) * 2 for i in (0, count - 1)]
    return swaps


def early_chunks(rows):
    return [5 * rows // 8, 3 * rows // 8]


def call(body, name, outs, args, in_specs=None, out_specs=None, scratch=(), aliases=None, work=30, dtype=F32):
    shapes = [jax.ShapeDtypeStruct(s, dtype) for s in outs]
    size = sum(int(a.size) for a in args)
    made = sum(s.size for s in shapes)
    return pl.pallas_call(
        body,
        out_shape=shapes,
        in_specs=in_specs or [VMEM] * len(args),
        out_specs=out_specs or [VMEM] * len(outs),
        scratch_shapes=list(scratch),
        input_output_aliases=aliases or {},
        name=name,
        cost_estimate=pl.CostEstimate(flops=0, bytes_accessed=4 * (size + made), transcendentals=0),
        compiler_params=pltpu.CompilerParams(vmem_limit_bytes=12 * 1024 * 1024),
    )(*args)


def blocks(rows):
    return range(0, rows, BLOCK)


def around(read, r, rows):
    x = read(r, r + BLOCK)
    cols = x.shape[-1]
    row = lax.broadcasted_iota(jnp.int32, x.shape, 0)
    col = lax.broadcasted_iota(jnp.int32, x.shape, 1)
    up = read(r - 1, r - 1 + BLOCK) if r > 0 else jnp.where(row == 0, 0.0, pltpu.roll(x, 1, 0))
    if r + BLOCK < rows:
        down = read(r + 1, r + 1 + BLOCK)
    else:
        down = jnp.where(row == BLOCK - 1, 0.0, pltpu.roll(x, BLOCK - 1, 0))
    left = jnp.where(col == 0, 0.0, pltpu.roll(x, 1, 1))
    right = jnp.where(col == cols - 1, 0.0, pltpu.roll(x, cols - 1, 1))
    return x, (up + down) + (left + right)


def reader(ref, *lead):
    return lambda lo, hi: ref[(*lead, slice(lo, hi))]


def add_terms(base_p, base_m, gain, nb_p, nb_m, energy, step):
    gain_kt = (DAMPING - gain) * (1.0 / 6.0)
    new_p = base_p - gain * (energy * nb_m) + gain_kt * nb_p
    new_m = base_m + gain * (step * nb_p + (6.0 * step * energy) * nb_m)
    return new_p, new_m


def parts3(x):
    high = x.astype(jnp.bfloat16)
    rest = x - high.astype(F32)
    middle = rest.astype(jnp.bfloat16)
    low = (rest - middle.astype(F32)).astype(jnp.bfloat16)
    return high, middle, low


def times(xs, matrix):
    n, width = xs[0].shape[0], matrix.shape[0]
    pieces = [x[:, j : j + width] for x in xs for j in range(0, x.shape[1], width)]
    stacked = jnp.concatenate([v for piece in pieces for v in parts3(piece)], axis=0)
    out = jnp.dot(stacked, matrix, preferred_element_type=F32)
    sums = [out[j : j + n] + out[j + n : j + 2 * n] + out[j + 2 * n : j + 3 * n] for j in range(0, out.shape[0], 3 * n)]
    each = len(sums) // len(xs)
    return [jnp.concatenate(sums[j : j + each], axis=1) for j in range(0, len(sums), each)]


LANES = 128


def tiles(rows, cols):
    return pltpu.VMEM((cols // LANES, rows, LANES), F32)


def put_rows(ref, rows, x):
    for j in range(ref.shape[0]):
        ref[j, rows] = x[:, j * LANES : (j + 1) * LANES]


def get_rows(ref, rows):
    return jnp.concatenate([ref[j, rows] for j in range(ref.shape[0])], axis=1)


def even_odd(ref):
    half = ref.shape[1] // 2
    return pl.ds(0, half, stride=2), pl.ds(1, half, stride=2)


def pair_rows(ref):
    even, odd = even_odd(ref)
    return get_rows(ref, even) + get_rows(ref, odd)


def take_body(what, where, warm, *refs):
    outs, sems = refs[:-1], refs[-1]
    c = where[0]
    copies = []
    for n, ((is_near, lo), out) in enumerate(zip(what, outs)):
        plane = 1 - c if is_near else c
        rows = pl.ds(lo, out.shape[1])
        copies.append(pltpu.make_async_copy(warm.at[:, plane, rows], out, sems.at[n]))
        copies[-1].start()
    for copy in copies:
        copy.wait()


def matrices_body(where, pair, even_col, odd_col, pair_t, even_t, odd_t):
    for dim, (both, even, odd) in enumerate(((pair, even_col, odd_col), (pair_t, even_t, odd_t))):
        cell = lax.broadcasted_iota(jnp.int32, both.shape, dim)
        coarse = 2 * lax.broadcasted_iota(jnp.int32, both.shape, 1 - dim)
        is_even = jnp.where(cell == coarse, 1.0, 0.0)
        is_odd = jnp.where(cell == coarse + 1, 1.0, 0.0)
        even[...] = is_even.astype(jnp.bfloat16)
        odd[...] = is_odd.astype(jnp.bfloat16)
        both[...] = (is_even + is_odd).astype(jnp.bfloat16)


def setup_body(where, phi, cot, gain, own):
    c = where[0]
    for i in range(2):
        plane = c if i == 0 else 1 - c
        for r in blocks(phi.shape[1]):
            rows = slice(r, r + BLOCK)
            v = phi[plane, rows]
            k = 3.0 * v * v - 1.0 + 6.0 * GRADIENT_ENERGY
            g = DAMPING / (1.0 + 6.0 * TIME_STEP * k)
            s0, s1 = cot[0, plane, rows], cot[1, plane, rows]
            gain[i, rows] = g
            own[i, 0, rows] = g * (s0 + k * s1)
            own[i, 1, rows] = g * (s1 - 6.0 * TIME_STEP * s0)


def coarse_setup_body(phi, pair, gain, both):
    for r in blocks(phi.shape[1]):
        rows = slice(r, r + BLOCK)
        a, b = phi[0, rows], phi[1, rows]
        put_rows(both, rows, (3.0 * a * a - 1.0) + (3.0 * b * b - 1.0))
    k = times([pair_rows(both)], pair[...])[0] / 8.0 + 6.0 * COARSE_ENERGY
    gain[...] = DAMPING / (1.0 + 6.0 * COARSE_STEP * k)


def gather_rows(chunks, whole):
    lo = 0
    for chunk in chunks:
        n = chunk.shape[1]
        for r in blocks(n):
            for f in range(2):
                whole[f, slice(lo + r, lo + r + BLOCK)] = chunk[f, slice(r, r + BLOCK)]
        lo += n


def part_body(count, *refs):
    chunks, (near, gain, own, far_out, near_out, far) = refs[:count], refs[count:]
    gather_rows(chunks, far)
    rows_all = far.shape[1]
    for i, (mine, other, out) in enumerate(((far, near, far_out), (near, far, near_out))):
        for r in blocks(rows_all):
            rows = slice(r, r + BLOCK)
            p, nb_p = around(reader(mine, 0), r, rows_all)
            m, nb_m = around(reader(mine, 1), r, rows_all)
            out[0, rows], out[1, rows] = add_terms(
                KEEP * p + own[i, 0, rows],
                KEEP * m + own[i, 1, rows],
                gain[i, rows],
                nb_p + other[0, rows],
                nb_m + other[1, rows],
                GRADIENT_ENERGY,
                TIME_STEP,
            )


def finish_body(i, lo, keep, part, halo, gain, out):
    for r in blocks(halo.shape[1]):
        rows, whole = slice(r, r + BLOCK), slice(lo + r, lo + r + BLOCK)
        hp, hm = halo[0, rows], halo[1, rows]
        if i == 0:
            hp, hm = hp * keep[0], hm * keep[0]
        out[0, rows], out[1, rows] = add_terms(
            part[0, whole], part[1, whole], gain[i, whole], hp, hm, GRADIENT_ENERGY, TIME_STEP
        )


def finish_pool_body(i, lo, keep, part, halo, gain, pair, *refs):
    before, (pool, out, phase, chem) = refs[:-4], refs[-4:]
    for r in blocks(halo.shape[1]):
        rows, whole = slice(r, r + BLOCK), slice(lo + r, lo + r + BLOCK)
        hp, hm = halo[0, rows], halo[1, rows]
        if i == 0:
            hp, hm = hp * keep[0], hm * keep[0]
        p, m = add_terms(
            part[0, whole], part[1, whole], gain[i, whole], hp, hm, GRADIENT_ENERGY, TIME_STEP
        )
        out[0, rows] = p
        out[1, rows] = m
        put_rows(phase, rows, p)
        put_rows(chem, rows, m)
    sums = times([pair_rows(phase), pair_rows(chem)], pair[...])
    for f in range(2):
        for ref in before:
            pool[f, : lo // 2] = ref[f]
        pool[f, lo // 2 if before else 0 :] = sums[f]


def three_body(count, *refs):
    chunks, (even_col, odd_col), outs, tile = refs[:count], refs[count : count + 2], refs[count + 2 : -1], refs[-1]
    for f in range(2):
        lo = 0
        for chunk in chunks:
            for r in blocks(chunk.shape[1]):
                put_rows(tile, slice(lo + r, lo + r + BLOCK), chunk[f, slice(r, r + BLOCK)])
            lo += chunk.shape[1]
        even, odd = even_odd(tile)
        top, bottom = get_rows(tile, even), get_rows(tile, odd)
        first, third = times([top, bottom], even_col[...])
        second = times([top], odd_col[...])[0]
        values = jnp.concatenate([first, second, third], axis=0)
        n = values.shape[0] // len(outs)
        for j, out in enumerate(outs):
            out[f] = values[j * n : (j + 1) * n]


def part_defect_body(count, *refs):
    chunks, (near, gain, own, pair, far_out, near_out, out, far, phase, chem) = refs[:count], refs[count:]
    part_body(count, *chunks, near, gain, own, far_out, near_out, far)
    for r in blocks(near.shape[1]):
        rows = slice(r, r + BLOCK)
        r0, r1 = 0.0, 0.0
        for i, (mine, new) in enumerate(((far, far_out), (near, near_out))):
            dp, dm = new[0, rows] - mine[0, rows], new[1, rows] - mine[1, rows]
            k = (DAMPING - gain[i, rows]) / (6.0 * TIME_STEP * gain[i, rows])
            r0 = r0 + (dp - k * dm)
            r1 = r1 + (dm + 6.0 * TIME_STEP * dp)
        put_rows(phase, rows, r0)
        put_rows(chem, rows, r1)
    sums = times([pair_rows(phase), pair_rows(chem)], pair[...])
    for f in range(2):
        out[f] = sums[f] * (1.0 / (8.0 * DAMPING))


def coarse_first_body(keep, local, far, near, gain, out):
    for r in blocks(local.shape[1]):
        rows = slice(r, r + BLOCK)
        s0 = local[0, rows] - (GRADIENT_ENERGY / 8.0) * (far[1, rows] * keep[0] + near[1, rows])
        s1 = local[1, rows] + (TIME_STEP / 8.0) * (far[0, rows] * keep[0] + near[0, rows])
        g = gain[rows]
        out[0, rows] = g * s0 + ((DAMPING - g) * (1.0 / (6.0 * COARSE_STEP))) * s1
        out[1, rows] = g * (s1 - 6.0 * COARSE_STEP * s0)


def coarse_part_body(fix, own, gain, out):
    rows_all = fix.shape[1]
    for r in blocks(rows_all):
        rows = slice(r, r + BLOCK)
        p, nb_p = around(reader(fix, 0), r, rows_all)
        m, nb_m = around(reader(fix, 1), r, rows_all)
        out[0, rows], out[1, rows] = add_terms(
            KEEP * p + own[0, rows],
            KEEP * m + own[1, rows],
            gain[rows],
            nb_p,
            nb_m,
            COARSE_ENERGY,
            COARSE_STEP,
        )


def coarse_finish_body(keep, part, far, near, gain, out):
    for r in blocks(part.shape[1]):
        rows = slice(r, r + BLOCK)
        out[0, rows], out[1, rows] = add_terms(
            part[0, rows],
            part[1, rows],
            gain[rows],
            far[0, rows] * keep[0] + near[0, rows],
            far[1, rows] * keep[0] + near[1, rows],
            COARSE_ENERGY,
            COARSE_STEP,
        )


def spread_into(tile_a, tile_b, fix_a, fix_b, pair_t):
    for tile, wide in zip((tile_a, tile_b), times([fix_a, fix_b], pair_t)):
        for rows in even_odd(tile):
            put_rows(tile, rows, wide)


def third_body(far, near, fix, near_halo, pair_t, gain, far_out, near_out, fix_p, fix_m, wide_p, wide_m):
    rows_all = near.shape[1]
    spread_into(fix_p, fix_m, fix[0], fix[1], pair_t[...])
    for r in blocks(rows_all):
        rows = slice(r, r + BLOCK)
        wide_p[rows], wide_m[rows] = get_rows(fix_p, rows), get_rows(fix_m, rows)
    for r in blocks(rows_all):
        rows = slice(r, r + BLOCK)
        p, nb_p = around(lambda lo, hi: wide_p[lo:hi], r, rows_all)
        m, nb_m = around(lambda lo, hi: wide_m[lo:hi], r, rows_all)
        nb_p, nb_m = nb_p + p, nb_m + m
        for i, (part, out) in enumerate(((far, far_out), (near, near_out))):
            xp, xm = (near_halo[0, rows], near_halo[1, rows]) if i == 1 else (0.0, 0.0)
            out[0, rows], out[1, rows] = add_terms(
                part[0, rows] + KEEP * p,
                part[1, rows] + KEEP * m,
                gain[i, rows],
                nb_p + xp,
                nb_m + xm,
                GRADIENT_ENERGY,
                TIME_STEP,
            )


def rebuild_body(sums, *refs):
    pieces, (even_t, odd_t, out, halo_p, halo_m) = refs[:-5], refs[-5:]
    half = sums.shape[1]
    for f, tile in enumerate((halo_p, halo_m)):
        values = jnp.concatenate([piece[f] for piece in pieces], axis=0)
        a, b, c = values[:half], values[half : 2 * half], values[2 * half :]
        d = sums[f] - ((a + b) + c)
        even, odd = even_odd(tile)
        (a, c), (b, d) = times([a, c], even_t[...]), times([b, d], odd_t[...])
        put_rows(tile, even, a + b)
        put_rows(tile, odd, c + d)
        for r in blocks(2 * half):
            rows = slice(r, r + BLOCK)
            out[f, rows] = get_rows(tile, rows)


def finish_fix_rows(i, lo, keep, part, halo, pair_t, gain, out, phase, chem, state_nb=None):
    n = out.shape[1]
    coarse = slice(lo // 2, (lo + n) // 2)
    spread_into(phase, chem, halo[0, coarse], halo[1, coarse], pair_t[...])
    for r in blocks(n):
        rows, whole = slice(r, r + BLOCK), slice(lo + r, lo + r + BLOCK)
        hp, hm = get_rows(phase, rows), get_rows(chem, rows)
        if i == 0:
            hp, hm = (hp + state_nb[0, whole]) * keep[0], (hm + state_nb[1, whole]) * keep[0]
        out[0, rows], out[1, rows] = add_terms(
            part[0, whole], part[1, whole], gain[i, whole], hp, hm, GRADIENT_ENERGY, TIME_STEP
        )


def fix_far_body(keep, part, halo, state_nb, pair_t, gain, out, phase, chem):
    finish_fix_rows(0, 0, keep, part, halo, pair_t, gain, out, phase, chem, state_nb)


def fix_near_body(part, halo, pair_t, gain, out, top, bottom, phase, chem):
    finish_fix_rows(1, 0, None, part, halo, pair_t, gain, out, phase, chem)
    n = top.shape[1]
    for f in range(2):
        for r in blocks(n):
            rows = slice(r, r + BLOCK)
            top[f, rows] = out[f, rows]
            bottom[f, rows] = out[f, slice(n + r, n + r + BLOCK)]


def final_rows(i, lo, where, keep, part, halo, gain, phi, psi, adjoint, design, plane_out, grad_out, sems):
    c = where[0]
    plane = c if i == 0 else 1 - c
    rows_all = halo.shape[1]
    step = rows_all // 2
    copies = []
    for n, start in enumerate(range(0, rows_all, step)):
        for r in range(start, start + step, BLOCK):
            rows, whole = slice(r, r + BLOCK), slice(lo + r, lo + r + BLOCK)
            hp, hm = halo[0, rows], halo[1, rows]
            if i == 0:
                hp, hm = hp * keep[0], hm * keep[0]
            p, m = add_terms(
                part[0, whole], part[1, whole], gain[i, whole], hp, hm, GRADIENT_ENERGY, TIME_STEP
            )
            plane_out[0, rows] = p
            plane_out[1, rows] = m
            grad_out[rows] = 6.0 * phi[plane, whole] * psi[plane, whole] * m
        here, there = pl.ds(start, step), pl.ds(lo + start, step)
        copies.append(pltpu.make_async_copy(plane_out.at[:, here], adjoint.at[:, plane, there], sems.at[2 * n]))
        copies.append(pltpu.make_async_copy(grad_out.at[here], design.at[plane, there], sems.at[2 * n + 1]))
        copies[-2].start()
        copies[-1].start()
    return copies


def final_body(which, where, keep, gain, phi, psi, *refs):
    count = len(which)
    halos, refs = refs[: 2 * count], refs[2 * count :]
    scratch = refs[-3 * count :]
    adjoint, design = refs[-3 * count - 2 : -3 * count]
    copies = []
    for n, (i, lo) in enumerate(which):
        part, halo = halos[2 * n : 2 * n + 2]
        copies += final_rows(
            i, lo, where, keep, part, halo, gain, phi, psi, adjoint, design, *scratch[3 * n : 3 * n + 3]
        )
    for copy in copies:
        copy.wait()


def on_device(phase_lin, phase_state, cotangent, warm_start):
    groups, count = lax.axis_size("grp"), lax.axis_size("gx")
    me = lax.axis_index("gx")
    where = jnp.reshape(me % 2, (1,)).astype(jnp.int32)
    keep = jnp.reshape(((me > 0) & (me < count - 1)).astype(F32), (1,))
    across, on_chip = cross_pairs(groups, count), chip_pairs(count)
    rows, cols = phase_lin.shape[1:]
    full, half = (2, rows, cols), (2, rows // 2, cols // 2)
    sizes = early_chunks(rows)
    starts = [sum(sizes[:n]) for n in range(len(sizes))]

    def swap_far(x):
        return lax.ppermute(x, ("grp", "gx"), across)

    def swap_near(x):
        return lax.ppermute(x, "gx", on_chip)

    def after(x, y):
        return lax.optimization_barrier((x, y))

    whole, tile = pltpu.VMEM(full, F32), tiles(rows, cols)

    def run(body, name, outs, args, statics=(), smem=0, **kw):
        specs = [SMEM] * smem + [VMEM] * (len(args) - smem)
        return call(functools.partial(body, *statics), name, outs, args, specs, **kw)

    def take(what, name):
        outs = [(2, n, cols) for _, _, n in what]
        body = functools.partial(take_body, [(is_near, lo) for is_near, lo, _ in what])
        scratch = [pltpu.SemaphoreType.DMA((len(what),))]
        source = pltpu.with_memory_space_constraint(warm_start, pltpu.HBM)
        return call(body, name, outs, (where, source), [SMEM, HBM], scratch=scratch, work=0)

    *far, near = take([(False, lo, n) for lo, n in zip(starts, sizes)] + [(True, 0, rows)], "take")
    far_halo = [swap_far(v) for v in far]
    near_halo = swap_near(near)
    gain, own = run(setup_body, "setup", [full, (2, 2, rows, cols)], (where, phase_lin, cotangent), smem=1)
    coefs = (gain,)
    far_part, near_part = run(part_body, "part", [full] * 2, (*far, near, *coefs, own), (len(far),), scratch=[whole])
    def finish(i, lo, part, halo):
        shape = (2, halo.shape[1], cols)
        return run(finish_body, "finish", [shape], (keep, part, halo, *coefs), (i, lo), smem=1, work=8)[0]

    far = [finish(0, lo, far_part, halo) for lo, halo in zip(starts, far_halo)]
    near_halo, far[-1] = after(near_halo, far[-1])
    near = finish(1, 0, near_part, near_halo)
    later, far[-1] = after(where, far[-1])
    shapes = [(2 * LANES, LANES)] * 3 + [(LANES, 2 * LANES)] * 3
    matrices = run(matrices_body, "matrices", shapes, (later,), smem=1, dtype=jnp.bfloat16)
    pair, even_col, odd_col, pair_t, even_t, odd_t = matrices
    coarse = run(coarse_setup_body, "coarse_setup", [half[1:]], (phase_lin, pair), scratch=[tile])

    far_halo = [swap_far(v) for v in far]
    near_halo = swap_near(near)
    far_part, near_part = run(part_body, "part", [full] * 2, (*far, near, *coefs, own), (len(far),), scratch=[whole])
    coarse = list(coarse)
    far_part, coarse[0] = after(far_part, coarse[0])

    def finish_pool(i, lo, part, halo, before=()):
        n = halo.shape[1]
        pool = (2, (n + (lo if before else 0)) // 2, cols // 2)
        args = (keep, part, halo, *coefs, pair, *before)
        outs, scratch = [pool, (2, n, cols)], [tiles(n, cols)] * 2
        return run(finish_pool_body, "finish_pool", outs, args, (i, lo), smem=1, scratch=scratch, work=8)

    far, before = [], ()
    for lo, halo in zip(starts, far_halo):
        far_pool, chunk = finish_pool(0, lo, far_part, halo, before)
        far.append(chunk)
        before = (far_pool,)
    near_pool, near = finish_pool(1, 0, near_part, near_halo)

    far_sums, near_sums = swap_far(far_pool), swap_near(near_pool)
    plane_sums = far_sums
    many = COARSE_SWEEPS - 1
    pieces = [(2, 3 * rows // 2 // many, cols // 2)] * many
    pieces = run(three_body, "three", pieces, (*far, even_col, odd_col), (len(far),), scratch=[tile])
    arrived = [swap_far(pieces[0])]
    near_halo = swap_near(near)
    args, scratch = (*far, near, *coefs, own, pair), [whole, tile, tile]
    far_part, near_part, local = run(
        part_defect_body, "part_defect", [full, full, half], args, (len(far),), scratch=scratch
    )
    fix = run(coarse_first_body, "coarse_first", [half], (keep, local, far_sums, near_sums, *coarse), smem=1, work=8)[0]
    first = fix
    for sweep_index in range(COARSE_SWEEPS - 1):
        far_sums, near_sums = swap_far(fix), swap_near(fix)
        if len(arrived) < len(pieces):
            fix, held = lax.optimization_barrier((fix, pieces[len(arrived)]))
            arrived.append(swap_far(held))
        part = run(coarse_part_body, "coarse_part", [half], (fix, first, *coarse))[0]
        if sweep_index:
            part, arrived[sweep_index - 1] = after(part, arrived[sweep_index - 1])
        args = (keep, part, far_sums, near_sums, *coarse)
        fix = run(coarse_finish_body, "coarse_finish", [half], args, smem=1, work=8)[0]

    far_sums, near_sums = swap_far(fix), swap_near(fix)
    args = (far_part, near_part, fix, near_halo, pair_t, *coefs)
    scratch = [tile] * 2 + [pltpu.VMEM((rows, cols), F32)] * 2
    far_part, near_part = run(third_body, "third", [full, full], args, scratch=scratch)
    plane_sums, far_part = after(plane_sums, far_part)
    state_nb = run(rebuild_body, "rebuild", [full], (plane_sums, *arrived, even_t, odd_t), scratch=[tile] * 2)[0]
    args = (keep, far_part, far_sums, state_nb, pair_t, *coefs)
    far = run(fix_far_body, "fix_far", [full], args, smem=1, scratch=[tile] * 2, work=8)
    starts = [0]
    top = (2, rows // 2, cols)
    args = (near_part, near_sums, pair_t, *coefs)
    near, *near_chunks = run(fix_near_body, "fix_near", [full, top, top], args, scratch=[tile] * 2, work=8)

    far_halo, near_halos = [swap_far(v) for v in far], [swap_near(v) for v in near_chunks]
    far_part, near_part = run(part_body, "part", [full] * 2, (*far, near, *coefs, own), (len(far),), scratch=[whole])
    outs = [(2, 2, rows, cols), full]

    def final(which, fields, done):
        args = (where, keep, *coefs, phase_lin, phase_state, *fields, *done)
        in_specs = [SMEM, SMEM] + [VMEM] * (len(args) - len(done) - 2) + [ANY] * len(done)
        scratch = []
        for halo in fields[1::2]:
            n = halo.shape[1]
            scratch += [pltpu.VMEM((2, n, cols), F32), pltpu.VMEM((n, cols), F32), pltpu.SemaphoreType.DMA((4,))]
        body = functools.partial(final_body, which)
        aliases = {len(args) - 2: 0, len(args) - 1: 1} if done else None
        return call(body, "final", outs, args, in_specs, [ANY, ANY], scratch, aliases, work=10)

    done = ()
    for lo, halo in zip(starts[:-1], far_halo[:-1]):
        done = final([(0, lo)], (far_part, halo), done)
    fields = (near_part, near_halos[0], near_part, near_halos[1])
    done = final([(1, 0), (1, rows // 2)], fields, done)
    done = final([(0, starts[-1])], (far_part, far_halo[-1]), done)
    return tuple(done)


def solution(mesh):
    in_specs = (
        P(("grp", "gx"), None, None),
        P(("grp", "gx"), None, None),
        P(None, ("grp", "gx"), None, None),
        P(None, ("grp", "gx"), None, None),
    )
    out_specs = (P(None, ("grp", "gx"), None, None), P(("grp", "gx"), None, None))
    return jax.shard_map(
        on_device, mesh=mesh, in_specs=in_specs, out_specs=out_specs, check_vma=False
    )
```

```python
import functools

import jax
import jax.numpy as jnp
from jax import lax
from jax.experimental import pallas as pl
from jax.experimental.pallas import tpu as pltpu
from jax.sharding import PartitionSpec as P

SWEEPS = 2
COARSE_SWEEPS = 4

GRADIENT_ENERGY = 1.0
TIME_STEP = 0.02
DAMPING = 0.8
KEEP = 1.0 - DAMPING
COARSE_ENERGY = GRADIENT_ENERGY / 4.0
COARSE_STEP = TIME_STEP / 4.0


VMEM = pl.BlockSpec(memory_space=pltpu.VMEM)
SMEM = pl.BlockSpec(memory_space=pltpu.SMEM)
ANY = pl.BlockSpec(memory_space=pl.ANY)
HBM = pl.BlockSpec(memory_space=pltpu.HBM)
BLOCK = 16
F32 = jnp.float32


def chip_pairs(count):
    return [(i, i ^ 1) for i in range(count)]


def cross_pairs(groups, count):
    pairs = []
    for g in range(groups):
        pairs += [(g * count + i, g * count + i + 1) for i in range(1, count - 1, 2)]
    for g in range(0, groups - 1, 2):
        pairs += [(g * count + i, (g + 1) * count + i) for i in (0, count - 1)]
    swaps = pairs + [(b, a) for a, b in pairs]
    if groups % 2 == 1:
        swaps += [((groups - 1) * count + i,) * 2 for i in (0, count - 1)]
    return swaps


def early_chunks(rows):
    return [5 * rows // 8, 3 * rows // 8]


def call(body, name, outs, args, in_specs=None, out_specs=None, scratch=(), aliases=None, work=30, dtype=F32):
    shapes = [jax.ShapeDtypeStruct(s, dtype) for s in outs]
    size = sum(int(a.size) for a in args)
    made = sum(s.size for s in shapes)
    return pl.pallas_call(
        body,
        out_shape=shapes,
        in_specs=in_specs or [VMEM] * len(args),
        out_specs=out_specs or [VMEM] * len(outs),
        scratch_shapes=list(scratch),
        input_output_aliases=aliases or {},
        name=name,
        cost_estimate=pl.CostEstimate(flops=0, bytes_accessed=4 * (size + made), transcendentals=0),
        compiler_params=pltpu.CompilerParams(vmem_limit_bytes=12 * 1024 * 1024),
    )(*args)


def blocks(rows):
    return range(0, rows, BLOCK)


def around(read, r, rows):
    x = read(r, r + BLOCK)
    cols = x.shape[-1]
    row = lax.broadcasted_iota(jnp.int32, x.shape, 0)
    col = lax.broadcasted_iota(jnp.int32, x.shape, 1)
    up = read(r - 1, r - 1 + BLOCK) if r > 0 else jnp.where(row == 0, 0.0, pltpu.roll(x, 1, 0))
    if r + BLOCK < rows:
        down = read(r + 1, r + 1 + BLOCK)
    else:
        down = jnp.where(row == BLOCK - 1, 0.0, pltpu.roll(x, BLOCK - 1, 0))
    left = jnp.where(col == 0, 0.0, pltpu.roll(x, 1, 1))
    right = jnp.where(col == cols - 1, 0.0, pltpu.roll(x, cols - 1, 1))
    return x, (up + down) + (left + right)


def reader(ref, *lead):
    return lambda lo, hi: ref[(*lead, slice(lo, hi))]


def add_terms(base_p, base_m, gain, nb_p, nb_m, energy, step):
    gain_kt = (DAMPING - gain) * (1.0 / 6.0)
    new_p = base_p - gain * (energy * nb_m) + gain_kt * nb_p
    new_m = base_m + gain * (step * nb_p + (6.0 * step * energy) * nb_m)
    return new_p, new_m


def parts3(x):
    high = x.astype(jnp.bfloat16)
    rest = x - high.astype(F32)
    middle = rest.astype(jnp.bfloat16)
    low = (rest - middle.astype(F32)).astype(jnp.bfloat16)
    return high, middle, low


def times(xs, matrix):
    n, width = xs[0].shape[0], matrix.shape[0]
    pieces = [x[:, j : j + width] for x in xs for j in range(0, x.shape[1], width)]
    stacked = jnp.concatenate([v for piece in pieces for v in parts3(piece)], axis=0)
    out = jnp.dot(stacked, matrix, preferred_element_type=F32)
    sums = [out[j : j + n] + out[j + n : j + 2 * n] + out[j + 2 * n : j + 3 * n] for j in range(0, out.shape[0], 3 * n)]
    each = len(sums) // len(xs)
    return [jnp.concatenate(sums[j : j + each], axis=1) for j in range(0, len(sums), each)]


LANES = 128


def tiles(rows, cols):
    return pltpu.VMEM((cols // LANES, rows, LANES), F32)


def put_rows(ref, rows, x):
    for j in range(ref.shape[0]):
        ref[j, rows] = x[:, j * LANES : (j + 1) * LANES]


def get_rows(ref, rows):
    return jnp.concatenate([ref[j, rows] for j in range(ref.shape[0])], axis=1)


def even_odd(ref):
    half = ref.shape[1] // 2
    return pl.ds(0, half, stride=2), pl.ds(1, half, stride=2)


def pair_rows(ref):
    even, odd = even_odd(ref)
    return get_rows(ref, even) + get_rows(ref, odd)


def take_body(what, where, warm, *refs):
    outs, sems = refs[:-1], refs[-1]
    c = where[0]
    copies = []
    for n, ((is_near, lo), out) in enumerate(zip(what, outs)):
        plane = 1 - c if is_near else c
        rows = pl.ds(lo, out.shape[1])
        copies.append(pltpu.make_async_copy(warm.at[:, plane, rows], out, sems.at[n]))
        copies[-1].start()
    for copy in copies:
        copy.wait()


def matrices_body(where, pair, even_col, odd_col, pair_t, even_t, odd_t):
    for dim, (both, even, odd) in enumerate(((pair, even_col, odd_col), (pair_t, even_t, odd_t))):
        cell = lax.broadcasted_iota(jnp.int32, both.shape, dim)
        coarse = 2 * lax.broadcasted_iota(jnp.int32, both.shape, 1 - dim)
        is_even = jnp.where(cell == coarse, 1.0, 0.0)
        is_odd = jnp.where(cell == coarse + 1, 1.0, 0.0)
        even[...] = is_even.astype(jnp.bfloat16)
        odd[...] = is_odd.astype(jnp.bfloat16)
        both[...] = (is_even + is_odd).astype(jnp.bfloat16)


def setup_body(where, phi, cot, gain, own):
    c = where[0]
    for i in range(2):
        plane = c if i == 0 else 1 - c
        for r in blocks(phi.shape[1]):
            rows = slice(r, r + BLOCK)
            v = phi[plane, rows]
            k = 3.0 * v * v - 1.0 + 6.0 * GRADIENT_ENERGY
            g = DAMPING / (1.0 + 6.0 * TIME_STEP * k)
            s0, s1 = cot[0, plane, rows], cot[1, plane, rows]
            gain[i, rows] = g
            own[i, 0, rows] = g * (s0 + k * s1)
            own[i, 1, rows] = g * (s1 - 6.0 * TIME_STEP * s0)


def coarse_setup_body(phi, pair, gain, both):
    for r in blocks(phi.shape[1]):
        rows = slice(r, r + BLOCK)
        a, b = phi[0, rows], phi[1, rows]
        put_rows(both, rows, (3.0 * a * a - 1.0) + (3.0 * b * b - 1.0))
    k = times([pair_rows(both)], pair[...])[0] / 8.0 + 6.0 * COARSE_ENERGY
    gain[...] = DAMPING / (1.0 + 6.0 * COARSE_STEP * k)


def gather_rows(chunks, whole):
    lo = 0
    for chunk in chunks:
        n = chunk.shape[1]
        for r in blocks(n):
            for f in range(2):
                whole[f, slice(lo + r, lo + r + BLOCK)] = chunk[f, slice(r, r + BLOCK)]
        lo += n


def part_body(count, *refs):
    chunks, (near, gain, own, far_out, near_out, far) = refs[:count], refs[count:]
    gather_rows(chunks, far)
    rows_all = far.shape[1]
    for i, (mine, other, out) in enumerate(((far, near, far_out), (near, far, near_out))):
        for r in blocks(rows_all):
            rows = slice(r, r + BLOCK)
            p, nb_p = around(reader(mine, 0), r, rows_all)
            m, nb_m = around(reader(mine, 1), r, rows_all)
            out[0, rows], out[1, rows] = add_terms(
                KEEP * p + own[i, 0, rows],
                KEEP * m + own[i, 1, rows],
                gain[i, rows],
                nb_p + other[0, rows],
                nb_m + other[1, rows],
                GRADIENT_ENERGY,
                TIME_STEP,
            )


def finish_body(i, lo, keep, part, halo, gain, out):
    for r in blocks(halo.shape[1]):
        rows, whole = slice(r, r + BLOCK), slice(lo + r, lo + r + BLOCK)
        hp, hm = halo[0, rows], halo[1, rows]
        if i == 0:
            hp, hm = hp * keep[0], hm * keep[0]
        out[0, rows], out[1, rows] = add_terms(
            part[0, whole], part[1, whole], gain[i, whole], hp, hm, GRADIENT_ENERGY, TIME_STEP
        )


def finish_pool_body(i, lo, keep, part, halo, gain, pair, *refs):
    before, (pool, out, phase, chem) = refs[:-4], refs[-4:]
    for r in blocks(halo.shape[1]):
        rows, whole = slice(r, r + BLOCK), slice(lo + r, lo + r + BLOCK)
        hp, hm = halo[0, rows], halo[1, rows]
        if i == 0:
            hp, hm = hp * keep[0], hm * keep[0]
        p, m = add_terms(
            part[0, whole], part[1, whole], gain[i, whole], hp, hm, GRADIENT_ENERGY, TIME_STEP
        )
        out[0, rows] = p
        out[1, rows] = m
        put_rows(phase, rows, p)
        put_rows(chem, rows, m)
    sums = times([pair_rows(phase), pair_rows(chem)], pair[...])
    for f in range(2):
        for ref in before:
            pool[f, : lo // 2] = ref[f]
        pool[f, lo // 2 if before else 0 :] = sums[f]


def three_body(count, *refs):
    chunks, (even_col, odd_col), outs, tile = refs[:count], refs[count : count + 2], refs[count + 2 : -1], refs[-1]
    for f in range(2):
        lo = 0
        for chunk in chunks:
            for r in blocks(chunk.shape[1]):
                put_rows(tile, slice(lo + r, lo + r + BLOCK), chunk[f, slice(r, r + BLOCK)])
            lo += chunk.shape[1]
        even, odd = even_odd(tile)
        top, bottom = get_rows(tile, even), get_rows(tile, odd)
        first, third = times([top, bottom], even_col[...])
        second = times([top], odd_col[...])[0]
        values = jnp.concatenate([first, second, third], axis=0)
        n = values.shape[0] // len(outs)
        for j, out in enumerate(outs):
            out[f] = values[j * n : (j + 1) * n]


def part_defect_body(count, *refs):
    chunks, (near, gain, own, pair, far_out, near_out, out, far, phase, chem) = refs[:count], refs[count:]
    part_body(count, *chunks, near, gain, own, far_out, near_out, far)
    for r in blocks(near.shape[1]):
        rows = slice(r, r + BLOCK)
        r0, r1 = 0.0, 0.0
        for i, (mine, new) in enumerate(((far, far_out), (near, near_out))):
            dp, dm = new[0, rows] - mine[0, rows], new[1, rows] - mine[1, rows]
            k = (DAMPING - gain[i, rows]) / (6.0 * TIME_STEP * gain[i, rows])
            r0 = r0 + (dp - k * dm)
            r1 = r1 + (dm + 6.0 * TIME_STEP * dp)
        put_rows(phase, rows, r0)
        put_rows(chem, rows, r1)
    sums = times([pair_rows(phase), pair_rows(chem)], pair[...])
    for f in range(2):
        out[f] = sums[f] * (1.0 / (8.0 * DAMPING))


def coarse_first_body(keep, local, far, near, gain, out):
    for r in blocks(local.shape[1]):
        rows = slice(r, r + BLOCK)
        s0 = local[0, rows] - (GRADIENT_ENERGY / 8.0) * (far[1, rows] * keep[0] + near[1, rows])
        s1 = local[1, rows] + (TIME_STEP / 8.0) * (far[0, rows] * keep[0] + near[0, rows])
        g = gain[rows]
        out[0, rows] = g * s0 + ((DAMPING - g) * (1.0 / (6.0 * COARSE_STEP))) * s1
        out[1, rows] = g * (s1 - 6.0 * COARSE_STEP * s0)


def coarse_part_body(fix, own, gain, out):
    rows_all = fix.shape[1]
    for r in blocks(rows_all):
        rows = slice(r, r + BLOCK)
        p, nb_p = around(reader(fix, 0), r, rows_all)
        m, nb_m = around(reader(fix, 1), r, rows_all)
        out[0, rows], out[1, rows] = add_terms(
            KEEP * p + own[0, rows],
            KEEP * m + own[1, rows],
            gain[rows],
            nb_p,
            nb_m,
            COARSE_ENERGY,
            COARSE_STEP,
        )


def coarse_finish_body(keep, part, far, near, gain, out):
    for r in blocks(part.shape[1]):
        rows = slice(r, r + BLOCK)
        out[0, rows], out[1, rows] = add_terms(
            part[0, rows],
            part[1, rows],
            gain[rows],
            far[0, rows] * keep[0] + near[0, rows],
            far[1, rows] * keep[0] + near[1, rows],
            COARSE_ENERGY,
            COARSE_STEP,
        )


def spread_into(tile_a, tile_b, fix_a, fix_b, pair_t):
    for tile, wide in zip((tile_a, tile_b), times([fix_a, fix_b], pair_t)):
        for rows in even_odd(tile):
            put_rows(tile, rows, wide)


def third_body(far, near, fix, near_halo, pair_t, gain, far_out, near_out, fix_p, fix_m, wide_p, wide_m):
    rows_all = near.shape[1]
    spread_into(fix_p, fix_m, fix[0], fix[1], pair_t[...])
    for r in blocks(rows_all):
        rows = slice(r, r + BLOCK)
        wide_p[rows], wide_m[rows] = get_rows(fix_p, rows), get_rows(fix_m, rows)
    for r in blocks(rows_all):
        rows = slice(r, r + BLOCK)
        p, nb_p = around(lambda lo, hi: wide_p[lo:hi], r, rows_all)
        m, nb_m = around(lambda lo, hi: wide_m[lo:hi], r, rows_all)
        nb_p, nb_m = nb_p + p, nb_m + m
        for i, (part, out) in enumerate(((far, far_out), (near, near_out))):
            xp, xm = (near_halo[0, rows], near_halo[1, rows]) if i == 1 else (0.0, 0.0)
            out[0, rows], out[1, rows] = add_terms(
                part[0, rows] + KEEP * p,
                part[1, rows] + KEEP * m,
                gain[i, rows],
                nb_p + xp,
                nb_m + xm,
                GRADIENT_ENERGY,
                TIME_STEP,
            )


def rebuild_body(sums, *refs):
    pieces, (even_t, odd_t, out, halo_p, halo_m) = refs[:-5], refs[-5:]
    half = sums.shape[1]
    for f, tile in enumerate((halo_p, halo_m)):
        values = jnp.concatenate([piece[f] for piece in pieces], axis=0)
        a, b, c = values[:half], values[half : 2 * half], values[2 * half :]
        d = sums[f] - ((a + b) + c)
        even, odd = even_odd(tile)
        (a, c), (b, d) = times([a, c], even_t[...]), times([b, d], odd_t[...])
        put_rows(tile, even, a + b)
        put_rows(tile, odd, c + d)
        for r in blocks(2 * half):
            rows = slice(r, r + BLOCK)
            out[f, rows] = get_rows(tile, rows)


def finish_fix_rows(i, lo, keep, part, halo, pair_t, gain, out, phase, chem, state_nb=None):
    n = out.shape[1]
    coarse = slice(lo // 2, (lo + n) // 2)
    spread_into(phase, chem, halo[0, coarse], halo[1, coarse], pair_t[...])
    for r in blocks(n):
        rows, whole = slice(r, r + BLOCK), slice(lo + r, lo + r + BLOCK)
        hp, hm = get_rows(phase, rows), get_rows(chem, rows)
        if i == 0:
            hp, hm = (hp + state_nb[0, whole]) * keep[0], (hm + state_nb[1, whole]) * keep[0]
        out[0, rows], out[1, rows] = add_terms(
            part[0, whole], part[1, whole], gain[i, whole], hp, hm, GRADIENT_ENERGY, TIME_STEP
        )


def fix_far_body(keep, part, halo, state_nb, pair_t, gain, out, phase, chem):
    finish_fix_rows(0, 0, keep, part, halo, pair_t, gain, out, phase, chem, state_nb)


def fix_near_body(part, halo, pair_t, gain, out, top, bottom, phase, chem):
    finish_fix_rows(1, 0, None, part, halo, pair_t, gain, out, phase, chem)
    n = top.shape[1]
    for f in range(2):
        for r in blocks(n):
            rows = slice(r, r + BLOCK)
            top[f, rows] = out[f, rows]
            bottom[f, rows] = out[f, slice(n + r, n + r + BLOCK)]


def final_rows(i, lo, where, keep, part, halo, gain, phi, psi, adjoint, design, plane_out, grad_out, sems):
    c = where[0]
    plane = c if i == 0 else 1 - c
    rows_all = halo.shape[1]
    step = rows_all // 4
    copies = []
    for n, start in enumerate(range(0, rows_all, step)):
        for r in range(start, start + step, BLOCK):
            rows, whole = slice(r, r + BLOCK), slice(lo + r, lo + r + BLOCK)
            hp, hm = halo[0, rows], halo[1, rows]
            if i == 0:
                hp, hm = hp * keep[0], hm * keep[0]
            p, m = add_terms(
                part[0, whole], part[1, whole], gain[i, whole], hp, hm, GRADIENT_ENERGY, TIME_STEP
            )
            plane_out[0, rows] = p
            plane_out[1, rows] = m
            grad_out[rows] = 6.0 * phi[plane, whole] * psi[plane, whole] * m
        here, there = pl.ds(start, step), pl.ds(lo + start, step)
        copies.append(pltpu.make_async_copy(plane_out.at[:, here], adjoint.at[:, plane, there], sems.at[2 * n]))
        copies.append(pltpu.make_async_copy(grad_out.at[here], design.at[plane, there], sems.at[2 * n + 1]))
        copies[-2].start()
        copies[-1].start()
    return copies


def final_body(which, where, keep, gain, phi, psi, *refs):
    count = len(which)
    halos, refs = refs[: 2 * count], refs[2 * count :]
    scratch = refs[-3 * count :]
    adjoint, design = refs[-3 * count - 2 : -3 * count]
    copies = []
    for n, (i, lo) in enumerate(which):
        part, halo = halos[2 * n : 2 * n + 2]
        copies += final_rows(
            i, lo, where, keep, part, halo, gain, phi, psi, adjoint, design, *scratch[3 * n : 3 * n + 3]
        )
    for copy in copies:
        copy.wait()


def on_device(phase_lin, phase_state, cotangent, warm_start):
    groups, count = lax.axis_size("grp"), lax.axis_size("gx")
    me = lax.axis_index("gx")
    where = jnp.reshape(me % 2, (1,)).astype(jnp.int32)
    keep = jnp.reshape(((me > 0) & (me < count - 1)).astype(F32), (1,))
    across, on_chip = cross_pairs(groups, count), chip_pairs(count)
    rows, cols = phase_lin.shape[1:]
    full, half = (2, rows, cols), (2, rows // 2, cols // 2)
    sizes = early_chunks(rows)
    starts = [sum(sizes[:n]) for n in range(len(sizes))]

    def swap_far(x):
        return lax.ppermute(x, ("grp", "gx"), across)

    def swap_near(x):
        return lax.ppermute(x, "gx", on_chip)

    def after(x, y):
        return lax.optimization_barrier((x, y))

    whole, tile = pltpu.VMEM(full, F32), tiles(rows, cols)

    def run(body, name, outs, args, statics=(), smem=0, **kw):
        specs = [SMEM] * smem + [VMEM] * (len(args) - smem)
        return call(functools.partial(body, *statics), name, outs, args, specs, **kw)

    def take(what, name):
        outs = [(2, n, cols) for _, _, n in what]
        body = functools.partial(take_body, [(is_near, lo) for is_near, lo, _ in what])
        scratch = [pltpu.SemaphoreType.DMA((len(what),))]
        source = pltpu.with_memory_space_constraint(warm_start, pltpu.HBM)
        return call(body, name, outs, (where, source), [SMEM, HBM], scratch=scratch, work=0)

    *far, near = take([(False, lo, n) for lo, n in zip(starts, sizes)] + [(True, 0, rows)], "take")
    far_halo = [swap_far(v) for v in far]
    near_halo = swap_near(near)
    gain, own = run(setup_body, "setup", [full, (2, 2, rows, cols)], (where, phase_lin, cotangent), smem=1)
    coefs = (gain,)
    far_part, near_part = run(part_body, "part", [full] * 2, (*far, near, *coefs, own), (len(far),), scratch=[whole])
    def finish(i, lo, part, halo):
        shape = (2, halo.shape[1], cols)
        return run(finish_body, "finish", [shape], (keep, part, halo, *coefs), (i, lo), smem=1, work=8)[0]

    far = [finish(0, lo, far_part, halo) for lo, halo in zip(starts, far_halo)]
    near_halo, far[-1] = after(near_halo, far[-1])
    near = finish(1, 0, near_part, near_halo)
    later, far[-1] = after(where, far[-1])
    shapes = [(2 * LANES, LANES)] * 3 + [(LANES, 2 * LANES)] * 3
    matrices = run(matrices_body, "matrices", shapes, (later,), smem=1, dtype=jnp.bfloat16)
    pair, even_col, odd_col, pair_t, even_t, odd_t = matrices
    coarse = run(coarse_setup_body, "coarse_setup", [half[1:]], (phase_lin, pair), scratch=[tile])

    far_halo = [swap_far(v) for v in far]
    near_halo = swap_near(near)
    far_part, near_part = run(part_body, "part", [full] * 2, (*far, near, *coefs, own), (len(far),), scratch=[whole])

    def finish_pool(i, lo, part, halo, before=()):
        n = halo.shape[1]
        pool = (2, (n + (lo if before else 0)) // 2, cols // 2)
        args = (keep, part, halo, *coefs, pair, *before)
        outs, scratch = [pool, (2, n, cols)], [tiles(n, cols)] * 2
        return run(finish_pool_body, "finish_pool", outs, args, (i, lo), smem=1, scratch=scratch, work=8)

    far, before = [], ()
    for lo, halo in zip(starts, far_halo):
        far_pool, chunk = finish_pool(0, lo, far_part, halo, before)
        far.append(chunk)
        before = (far_pool,)
    near_pool, near = finish_pool(1, 0, near_part, near_halo)

    far_sums, near_sums = swap_far(far_pool), swap_near(near_pool)
    plane_sums = far_sums
    many = COARSE_SWEEPS - 1
    pieces = [(2, 3 * rows // 2 // many, cols // 2)] * many
    pieces = run(three_body, "three", pieces, (*far, even_col, odd_col), (len(far),), scratch=[tile])
    arrived = [swap_far(pieces[0])]
    near_halo = swap_near(near)
    args, scratch = (*far, near, *coefs, own, pair), [whole, tile, tile]
    far_part, near_part, local = run(
        part_defect_body, "part_defect", [full, full, half], args, (len(far),), scratch=scratch
    )
    fix = run(coarse_first_body, "coarse_first", [half], (keep, local, far_sums, near_sums, *coarse), smem=1, work=8)[0]
    first = fix
    for sweep_index in range(COARSE_SWEEPS - 1):
        far_sums, near_sums = swap_far(fix), swap_near(fix)
        if len(arrived) < len(pieces):
            fix, held = lax.optimization_barrier((fix, pieces[len(arrived)]))
            arrived.append(swap_far(held))
        part = run(coarse_part_body, "coarse_part", [half], (fix, first, *coarse))[0]
        if sweep_index:
            part, arrived[sweep_index - 1] = after(part, arrived[sweep_index - 1])
        args = (keep, part, far_sums, near_sums, *coarse)
        fix = run(coarse_finish_body, "coarse_finish", [half], args, smem=1, work=8)[0]

    far_sums, near_sums = swap_far(fix), swap_near(fix)
    args = (far_part, near_part, fix, near_halo, pair_t, *coefs)
    scratch = [tile] * 2 + [pltpu.VMEM((rows, cols), F32)] * 2
    far_part, near_part = run(third_body, "third", [full, full], args, scratch=scratch)
    plane_sums, far_part = after(plane_sums, far_part)
    state_nb = run(rebuild_body, "rebuild", [full], (plane_sums, *arrived, even_t, odd_t), scratch=[tile] * 2)[0]
    args = (keep, far_part, far_sums, state_nb, pair_t, *coefs)
    far = run(fix_far_body, "fix_far", [full], args, smem=1, scratch=[tile] * 2, work=8)
    starts = [0]
    top = (2, rows // 2, cols)
    args = (near_part, near_sums, pair_t, *coefs)
    near, *near_chunks = run(fix_near_body, "fix_near", [full, top, top], args, scratch=[tile] * 2, work=8)

    far_halo, near_halos = [swap_far(v) for v in far], [swap_near(v) for v in near_chunks]
    far_part, near_part = run(part_body, "part", [full] * 2, (*far, near, *coefs, own), (len(far),), scratch=[whole])
    outs = [(2, 2, rows, cols), full]

    def final(which, fields, done):
        args = (where, keep, *coefs, phase_lin, phase_state, *fields, *done)
        in_specs = [SMEM, SMEM] + [VMEM] * (len(args) - len(done) - 2) + [ANY] * len(done)
        scratch = []
        for halo in fields[1::2]:
            n = halo.shape[1]
            scratch += [pltpu.VMEM((2, n, cols), F32), pltpu.VMEM((n, cols), F32), pltpu.SemaphoreType.DMA((8,))]
        body = functools.partial(final_body, which)
        aliases = {len(args) - 2: 0, len(args) - 1: 1} if done else None
        return call(body, "final", outs, args, in_specs, [ANY, ANY], scratch, aliases, work=10)

    done = ()
    for lo, halo in zip(starts[:-1], far_halo[:-1]):
        done = final([(0, lo)], (far_part, halo), done)
    fields = (near_part, near_halos[0], near_part, near_halos[1])
    done = final([(1, 0), (1, rows // 2)], fields, done)
    done = final([(0, starts[-1])], (far_part, far_halo[-1]), done)
    return tuple(done)


def solution(mesh):
    in_specs = (
        P(("grp", "gx"), None, None),
        P(("grp", "gx"), None, None),
        P(None, ("grp", "gx"), None, None),
        P(None, ("grp", "gx"), None, None),
    )
    out_specs = (P(None, ("grp", "gx"), None, None), P(("grp", "gx"), None, None))
    return jax.shard_map(
        on_device, mesh=mesh, in_specs=in_specs, out_specs=out_specs, check_vma=False
    )
```

```python
import functools

import jax
import jax.numpy as jnp
from jax import lax
from jax.experimental import pallas as pl
from jax.experimental.pallas import tpu as pltpu
from jax.sharding import PartitionSpec as P

SWEEPS = 2
COARSE_SWEEPS = 4

GRADIENT_ENERGY = 1.0
TIME_STEP = 0.02
DAMPING = 0.8
KEEP = 1.0 - DAMPING
COARSE_ENERGY = GRADIENT_ENERGY / 4.0
COARSE_STEP = TIME_STEP / 4.0


VMEM = pl.BlockSpec(memory_space=pltpu.VMEM)
SMEM = pl.BlockSpec(memory_space=pltpu.SMEM)
ANY = pl.BlockSpec(memory_space=pl.ANY)
HBM = pl.BlockSpec(memory_space=pltpu.HBM)
BLOCK = 16
F32 = jnp.float32


def chip_pairs(count):
    return [(i, i ^ 1) for i in range(count)]


def cross_pairs(groups, count):
    pairs = []
    for g in range(groups):
        pairs += [(g * count + i, g * count + i + 1) for i in range(1, count - 1, 2)]
    for g in range(0, groups - 1, 2):
        pairs += [(g * count + i, (g + 1) * count + i) for i in (0, count - 1)]
    swaps = pairs + [(b, a) for a, b in pairs]
    if groups % 2 == 1:
        swaps += [((groups - 1) * count + i,) * 2 for i in (0, count - 1)]
    return swaps


def early_chunks(rows):
    return [5 * rows // 8, 3 * rows // 8]


def call(body, name, outs, args, in_specs=None, out_specs=None, scratch=(), aliases=None, work=30, dtype=F32):
    shapes = [jax.ShapeDtypeStruct(s, dtype) for s in outs]
    size = sum(int(a.size) for a in args)
    made = sum(s.size for s in shapes)
    return pl.pallas_call(
        body,
        out_shape=shapes,
        in_specs=in_specs or [VMEM] * len(args),
        out_specs=out_specs or [VMEM] * len(outs),
        scratch_shapes=list(scratch),
        input_output_aliases=aliases or {},
        name=name,
        cost_estimate=pl.CostEstimate(flops=0, bytes_accessed=4 * (size + made), transcendentals=0),
        compiler_params=pltpu.CompilerParams(vmem_limit_bytes=12 * 1024 * 1024),
    )(*args)


def blocks(rows):
    return range(0, rows, BLOCK)


def around(read, r, rows):
    x = read(r, r + BLOCK)
    cols = x.shape[-1]
    row = lax.broadcasted_iota(jnp.int32, x.shape, 0)
    col = lax.broadcasted_iota(jnp.int32, x.shape, 1)
    up = read(r - 1, r - 1 + BLOCK) if r > 0 else jnp.where(row == 0, 0.0, pltpu.roll(x, 1, 0))
    if r + BLOCK < rows:
        down = read(r + 1, r + 1 + BLOCK)
    else:
        down = jnp.where(row == BLOCK - 1, 0.0, pltpu.roll(x, BLOCK - 1, 0))
    left = jnp.where(col == 0, 0.0, pltpu.roll(x, 1, 1))
    right = jnp.where(col == cols - 1, 0.0, pltpu.roll(x, cols - 1, 1))
    return x, (up + down) + (left + right)


def reader(ref, *lead):
    return lambda lo, hi: ref[(*lead, slice(lo, hi))]


def add_terms(base_p, base_m, gain, nb_p, nb_m, energy, step):
    gain_kt = (DAMPING - gain) * (1.0 / 6.0)
    new_p = base_p - gain * (energy * nb_m) + gain_kt * nb_p
    new_m = base_m + gain * (step * nb_p + (6.0 * step * energy) * nb_m)
    return new_p, new_m


def parts3(x):
    high = x.astype(jnp.bfloat16)
    rest = x - high.astype(F32)
    middle = rest.astype(jnp.bfloat16)
    low = (rest - middle.astype(F32)).astype(jnp.bfloat16)
    return high, middle, low


def times(xs, matrix):
    n, width = xs[0].shape[0], matrix.shape[0]
    pieces = [x[:, j : j + width] for x in xs for j in range(0, x.shape[1], width)]
    stacked = jnp.concatenate([v for piece in pieces for v in parts3(piece)], axis=0)
    out = jnp.dot(stacked, matrix, preferred_element_type=F32)
    sums = [out[j : j + n] + out[j + n : j + 2 * n] + out[j + 2 * n : j + 3 * n] for j in range(0, out.shape[0], 3 * n)]
    each = len(sums) // len(xs)
    return [jnp.concatenate(sums[j : j + each], axis=1) for j in range(0, len(sums), each)]


LANES = 128


def tiles(rows, cols):
    return pltpu.VMEM((cols // LANES, rows, LANES), F32)


def put_rows(ref, rows, x):
    for j in range(ref.shape[0]):
        ref[j, rows] = x[:, j * LANES : (j + 1) * LANES]


def get_rows(ref, rows):
    return jnp.concatenate([ref[j, rows] for j in range(ref.shape[0])], axis=1)


def even_odd(ref):
    half = ref.shape[1] // 2
    return pl.ds(0, half, stride=2), pl.ds(1, half, stride=2)


def pair_rows(ref):
    even, odd = even_odd(ref)
    return get_rows(ref, even) + get_rows(ref, odd)


def take_body(what, where, warm, *refs):
    outs, sems = refs[:-1], refs[-1]
    c = where[0]
    copies = []
    for n, ((is_near, lo), out) in enumerate(zip(what, outs)):
        plane = 1 - c if is_near else c
        rows = pl.ds(lo, out.shape[1])
        copies.append(pltpu.make_async_copy(warm.at[:, plane, rows], out, sems.at[n]))
        copies[-1].start()
    for copy in copies:
        copy.wait()


def matrices_body(where, pair, even_col, odd_col, pair_t, even_t, odd_t):
    for dim, (both, even, odd) in enumerate(((pair, even_col, odd_col), (pair_t, even_t, odd_t))):
        cell = lax.broadcasted_iota(jnp.int32, both.shape, dim)
        coarse = 2 * lax.broadcasted_iota(jnp.int32, both.shape, 1 - dim)
        is_even = jnp.where(cell == coarse, 1.0, 0.0)
        is_odd = jnp.where(cell == coarse + 1, 1.0, 0.0)
        even[...] = is_even.astype(jnp.bfloat16)
        odd[...] = is_odd.astype(jnp.bfloat16)
        both[...] = (is_even + is_odd).astype(jnp.bfloat16)


def setup_body(where, phi, cot, gain, own):
    c = where[0]
    for i in range(2):
        plane = c if i == 0 else 1 - c
        for r in blocks(phi.shape[1]):
            rows = slice(r, r + BLOCK)
            v = phi[plane, rows]
            k = 3.0 * v * v - 1.0 + 6.0 * GRADIENT_ENERGY
            g = DAMPING / (1.0 + 6.0 * TIME_STEP * k)
            s0, s1 = cot[0, plane, rows], cot[1, plane, rows]
            gain[i, rows] = g
            own[i, 0, rows] = g * (s0 + k * s1)
            own[i, 1, rows] = g * (s1 - 6.0 * TIME_STEP * s0)


def coarse_setup_body(phi, pair, gain, both):
    for r in blocks(phi.shape[1]):
        rows = slice(r, r + BLOCK)
        a, b = phi[0, rows], phi[1, rows]
        put_rows(both, rows, (3.0 * a * a - 1.0) + (3.0 * b * b - 1.0))
    k = times([pair_rows(both)], pair[...])[0] / 8.0 + 6.0 * COARSE_ENERGY
    gain[...] = DAMPING / (1.0 + 6.0 * COARSE_STEP * k)


def gather_rows(chunks, whole):
    lo = 0
    for chunk in chunks:
        n = chunk.shape[1]
        for r in blocks(n):
            for f in range(2):
                whole[f, slice(lo + r, lo + r + BLOCK)] = chunk[f, slice(r, r + BLOCK)]
        lo += n


def part_body(count, *refs):
    chunks, (near, gain, own, far_out, near_out, far) = refs[:count], refs[count:]
    gather_rows(chunks, far)
    rows_all = far.shape[1]
    for i, (mine, other, out) in enumerate(((far, near, far_out), (near, far, near_out))):
        for r in blocks(rows_all):
            rows = slice(r, r + BLOCK)
            p, nb_p = around(reader(mine, 0), r, rows_all)
            m, nb_m = around(reader(mine, 1), r, rows_all)
            out[0, rows], out[1, rows] = add_terms(
                KEEP * p + own[i, 0, rows],
                KEEP * m + own[i, 1, rows],
                gain[i, rows],
                nb_p + other[0, rows],
                nb_m + other[1, rows],
                GRADIENT_ENERGY,
                TIME_STEP,
            )


def finish_body(i, lo, keep, part, halo, gain, out):
    for r in blocks(halo.shape[1]):
        rows, whole = slice(r, r + BLOCK), slice(lo + r, lo + r + BLOCK)
        hp, hm = halo[0, rows], halo[1, rows]
        if i == 0:
            hp, hm = hp * keep[0], hm * keep[0]
        out[0, rows], out[1, rows] = add_terms(
            part[0, whole], part[1, whole], gain[i, whole], hp, hm, GRADIENT_ENERGY, TIME_STEP
        )


def finish_pool_body(i, lo, keep, part, halo, gain, pair, *refs):
    before, (pool, out, phase, chem) = refs[:-4], refs[-4:]
    for r in blocks(halo.shape[1]):
        rows, whole = slice(r, r + BLOCK), slice(lo + r, lo + r + BLOCK)
        hp, hm = halo[0, rows], halo[1, rows]
        if i == 0:
            hp, hm = hp * keep[0], hm * keep[0]
        p, m = add_terms(
            part[0, whole], part[1, whole], gain[i, whole], hp, hm, GRADIENT_ENERGY, TIME_STEP
        )
        out[0, rows] = p
        out[1, rows] = m
        put_rows(phase, rows, p)
        put_rows(chem, rows, m)
    sums = times([pair_rows(phase), pair_rows(chem)], pair[...])
    for f in range(2):
        for ref in before:
            pool[f, : lo // 2] = ref[f]
        pool[f, lo // 2 if before else 0 :] = sums[f]


def three_body(count, *refs):
    chunks, (even_col, odd_col), outs, tile = refs[:count], refs[count : count + 2], refs[count + 2 : -1], refs[-1]
    for f in range(2):
        lo = 0
        for chunk in chunks:
            for r in blocks(chunk.shape[1]):
                put_rows(tile, slice(lo + r, lo + r + BLOCK), chunk[f, slice(r, r + BLOCK)])
            lo += chunk.shape[1]
        even, odd = even_odd(tile)
        top, bottom = get_rows(tile, even), get_rows(tile, odd)
        first, third = times([top, bottom], even_col[...])
        second = times([top], odd_col[...])[0]
        values = jnp.concatenate([first, second, third], axis=0)
        n = values.shape[0] // len(outs)
        for j, out in enumerate(outs):
            out[f] = values[j * n : (j + 1) * n]


def part_defect_body(count, *refs):
    chunks, (near, gain, own, pair, far_out, near_out, out, far, phase, chem) = refs[:count], refs[count:]
    part_body(count, *chunks, near, gain, own, far_out, near_out, far)
    for r in blocks(near.shape[1]):
        rows = slice(r, r + BLOCK)
        r0, r1 = 0.0, 0.0
        for i, (mine, new) in enumerate(((far, far_out), (near, near_out))):
            dp, dm = new[0, rows] - mine[0, rows], new[1, rows] - mine[1, rows]
            k = (DAMPING - gain[i, rows]) / (6.0 * TIME_STEP * gain[i, rows])
            r0 = r0 + (dp - k * dm)
            r1 = r1 + (dm + 6.0 * TIME_STEP * dp)
        put_rows(phase, rows, r0)
        put_rows(chem, rows, r1)
    sums = times([pair_rows(phase), pair_rows(chem)], pair[...])
    for f in range(2):
        out[f] = sums[f] * (1.0 / (8.0 * DAMPING))


def coarse_first_body(keep, local, far, near, gain, out):
    for r in blocks(local.shape[1]):
        rows = slice(r, r + BLOCK)
        s0 = local[0, rows] - (GRADIENT_ENERGY / 8.0) * (far[1, rows] * keep[0] + near[1, rows])
        s1 = local[1, rows] + (TIME_STEP / 8.0) * (far[0, rows] * keep[0] + near[0, rows])
        g = gain[rows]
        out[0, rows] = g * s0 + ((DAMPING - g) * (1.0 / (6.0 * COARSE_STEP))) * s1
        out[1, rows] = g * (s1 - 6.0 * COARSE_STEP * s0)


def coarse_part_body(fix, own, gain, out):
    rows_all = fix.shape[1]
    for r in blocks(rows_all):
        rows = slice(r, r + BLOCK)
        p, nb_p = around(reader(fix, 0), r, rows_all)
        m, nb_m = around(reader(fix, 1), r, rows_all)
        out[0, rows], out[1, rows] = add_terms(
            KEEP * p + own[0, rows],
            KEEP * m + own[1, rows],
            gain[rows],
            nb_p,
            nb_m,
            COARSE_ENERGY,
            COARSE_STEP,
        )


def coarse_finish_body(keep, part, far, near, gain, out):
    for r in blocks(part.shape[1]):
        rows = slice(r, r + BLOCK)
        out[0, rows], out[1, rows] = add_terms(
            part[0, rows],
            part[1, rows],
            gain[rows],
            far[0, rows] * keep[0] + near[0, rows],
            far[1, rows] * keep[0] + near[1, rows],
            COARSE_ENERGY,
            COARSE_STEP,
        )


def spread_into(tile_a, tile_b, fix_a, fix_b, pair_t):
    for tile, wide in zip((tile_a, tile_b), times([fix_a, fix_b], pair_t)):
        for rows in even_odd(tile):
            put_rows(tile, rows, wide)


def third_body(far, near, fix, near_halo, pair_t, gain, far_out, near_out, fix_p, fix_m, wide_p, wide_m):
    rows_all = near.shape[1]
    spread_into(fix_p, fix_m, fix[0], fix[1], pair_t[...])
    for r in blocks(rows_all):
        rows = slice(r, r + BLOCK)
        wide_p[rows], wide_m[rows] = get_rows(fix_p, rows), get_rows(fix_m, rows)
    for r in blocks(rows_all):
        rows = slice(r, r + BLOCK)
        p, nb_p = around(lambda lo, hi: wide_p[lo:hi], r, rows_all)
        m, nb_m = around(lambda lo, hi: wide_m[lo:hi], r, rows_all)
        nb_p, nb_m = nb_p + p, nb_m + m
        for i, (part, out) in enumerate(((far, far_out), (near, near_out))):
            xp, xm = (near_halo[0, rows], near_halo[1, rows]) if i == 1 else (0.0, 0.0)
            out[0, rows], out[1, rows] = add_terms(
                part[0, rows] + KEEP * p,
                part[1, rows] + KEEP * m,
                gain[i, rows],
                nb_p + xp,
                nb_m + xm,
                GRADIENT_ENERGY,
                TIME_STEP,
            )


def rebuild_body(sums, *refs):
    pieces, (even_t, odd_t, out, halo_p, halo_m) = refs[:-5], refs[-5:]
    half = sums.shape[1]
    for f, tile in enumerate((halo_p, halo_m)):
        values = jnp.concatenate([piece[f] for piece in pieces], axis=0)
        a, b, c = values[:half], values[half : 2 * half], values[2 * half :]
        d = sums[f] - ((a + b) + c)
        even, odd = even_odd(tile)
        (a, c), (b, d) = times([a, c], even_t[...]), times([b, d], odd_t[...])
        put_rows(tile, even, a + b)
        put_rows(tile, odd, c + d)
        for r in blocks(2 * half):
            rows = slice(r, r + BLOCK)
            out[f, rows] = get_rows(tile, rows)


def finish_fix_rows(i, lo, keep, part, halo, pair_t, gain, out, phase, chem, state_nb=None):
    n = out.shape[1]
    coarse = slice(lo // 2, (lo + n) // 2)
    spread_into(phase, chem, halo[0, coarse], halo[1, coarse], pair_t[...])
    for r in blocks(n):
        rows, whole = slice(r, r + BLOCK), slice(lo + r, lo + r + BLOCK)
        hp, hm = get_rows(phase, rows), get_rows(chem, rows)
        if i == 0:
            hp, hm = (hp + state_nb[0, whole]) * keep[0], (hm + state_nb[1, whole]) * keep[0]
        out[0, rows], out[1, rows] = add_terms(
            part[0, whole], part[1, whole], gain[i, whole], hp, hm, GRADIENT_ENERGY, TIME_STEP
        )


def fix_far_body(keep, part, halo, state_nb, pair_t, gain, out, phase, chem):
    finish_fix_rows(0, 0, keep, part, halo, pair_t, gain, out, phase, chem, state_nb)


def fix_near_body(part, halo, pair_t, gain, out, top, bottom, phase, chem):
    finish_fix_rows(1, 0, None, part, halo, pair_t, gain, out, phase, chem)
    n = top.shape[1]
    for f in range(2):
        for r in blocks(n):
            rows = slice(r, r + BLOCK)
            top[f, rows] = out[f, rows]
            bottom[f, rows] = out[f, slice(n + r, n + r + BLOCK)]


def final_rows(i, lo, where, keep, part, halo, gain, phi, psi, adjoint, design, plane_out, grad_out, sems):
    c = where[0]
    plane = c if i == 0 else 1 - c
    rows_all = halo.shape[1]
    step = rows_all // 4
    copies = []
    for n, start in enumerate(range(0, rows_all, step)):
        for r in range(start, start + step, BLOCK):
            rows, whole = slice(r, r + BLOCK), slice(lo + r, lo + r + BLOCK)
            hp, hm = halo[0, rows], halo[1, rows]
            if i == 0:
                hp, hm = hp * keep[0], hm * keep[0]
            p, m = add_terms(
                part[0, whole], part[1, whole], gain[i, whole], hp, hm, GRADIENT_ENERGY, TIME_STEP
            )
            plane_out[0, rows] = p
            plane_out[1, rows] = m
            grad_out[rows] = 6.0 * phi[plane, whole] * psi[plane, whole] * m
        here, there = pl.ds(start, step), pl.ds(lo + start, step)
        copies.append(pltpu.make_async_copy(plane_out.at[:, here], adjoint.at[:, plane, there], sems.at[2 * n]))
        copies.append(pltpu.make_async_copy(grad_out.at[here], design.at[plane, there], sems.at[2 * n + 1]))
        copies[-2].start()
        copies[-1].start()
    return copies


def final_body(which, where, keep, gain, phi, psi, *refs):
    count = len(which)
    halos, refs = refs[: 2 * count], refs[2 * count :]
    scratch = refs[-3 * count :]
    adjoint, design = refs[-3 * count - 2 : -3 * count]
    copies = []
    for n, (i, lo) in enumerate(which):
        part, halo = halos[2 * n : 2 * n + 2]
        copies += final_rows(
            i, lo, where, keep, part, halo, gain, phi, psi, adjoint, design, *scratch[3 * n : 3 * n + 3]
        )
    for copy in copies:
        copy.wait()


def on_device(phase_lin, phase_state, cotangent, warm_start):
    groups, count = lax.axis_size("grp"), lax.axis_size("gx")
    me = lax.axis_index("gx")
    where = jnp.reshape(me % 2, (1,)).astype(jnp.int32)
    keep = jnp.reshape(((me > 0) & (me < count - 1)).astype(F32), (1,))
    across, on_chip = cross_pairs(groups, count), chip_pairs(count)
    rows, cols = phase_lin.shape[1:]
    full, half = (2, rows, cols), (2, rows // 2, cols // 2)
    sizes = early_chunks(rows)
    starts = [sum(sizes[:n]) for n in range(len(sizes))]

    def swap_far(x):
        return lax.ppermute(x, ("grp", "gx"), across)

    def swap_near(x):
        return lax.ppermute(x, "gx", on_chip)

    def after(x, y):
        return lax.optimization_barrier((x, y))

    whole, tile = pltpu.VMEM(full, F32), tiles(rows, cols)

    def run(body, name, outs, args, statics=(), smem=0, **kw):
        specs = [SMEM] * smem + [VMEM] * (len(args) - smem)
        return call(functools.partial(body, *statics), name, outs, args, specs, **kw)

    def take(what, name):
        outs = [(2, n, cols) for _, _, n in what]
        body = functools.partial(take_body, [(is_near, lo) for is_near, lo, _ in what])
        scratch = [pltpu.SemaphoreType.DMA((len(what),))]
        source = pltpu.with_memory_space_constraint(warm_start, pltpu.HBM)
        return call(body, name, outs, (where, source), [SMEM, HBM], scratch=scratch, work=0)

    *far, near = take([(False, lo, n) for lo, n in zip(starts, sizes)] + [(True, 0, rows)], "take")
    far_halo = [swap_far(v) for v in far]
    near_halo = swap_near(near)
    gain, own = run(setup_body, "setup", [full, (2, 2, rows, cols)], (where, phase_lin, cotangent), smem=1)
    coefs = (gain,)
    far_part, near_part = run(part_body, "part", [full] * 2, (*far, near, *coefs, own), (len(far),), scratch=[whole])
    def finish(i, lo, part, halo):
        shape = (2, halo.shape[1], cols)
        return run(finish_body, "finish", [shape], (keep, part, halo, *coefs), (i, lo), smem=1, work=8)[0]

    far = [finish(0, lo, far_part, halo) for lo, halo in zip(starts, far_halo)]
    near_halo, far[-1] = after(near_halo, far[-1])
    near = finish(1, 0, near_part, near_halo)
    later, far[-1] = after(where, far[-1])
    shapes = [(2 * LANES, LANES)] * 3 + [(LANES, 2 * LANES)] * 3
    matrices = run(matrices_body, "matrices", shapes, (later,), smem=1, dtype=jnp.bfloat16)
    pair, even_col, odd_col, pair_t, even_t, odd_t = matrices
    coarse = run(coarse_setup_body, "coarse_setup", [half[1:]], (phase_lin, pair), scratch=[tile])

    far_halo = [swap_far(v) for v in far]
    near_halo = swap_near(near)
    far_part, near_part = run(part_body, "part", [full] * 2, (*far, near, *coefs, own), (len(far),), scratch=[whole])

    def finish_pool(i, lo, part, halo, before=()):
        n = halo.shape[1]
        pool = (2, (n + (lo if before else 0)) // 2, cols // 2)
        args = (keep, part, halo, *coefs, pair, *before)
        outs, scratch = [pool, (2, n, cols)], [tiles(n, cols)] * 2
        return run(finish_pool_body, "finish_pool", outs, args, (i, lo), smem=1, scratch=scratch, work=8)

    far, before = [], ()
    for lo, halo in zip(starts, far_halo):
        far_pool, chunk = finish_pool(0, lo, far_part, halo, before)
        far.append(chunk)
        before = (far_pool,)
    near_pool, near = finish_pool(1, 0, near_part, near_halo)

    far_sums, near_sums = swap_far(far_pool), swap_near(near_pool)
    plane_sums = far_sums
    many = COARSE_SWEEPS - 1
    pieces = [(2, 3 * rows // 2 // many, cols // 2)] * many
    pieces = run(three_body, "three", pieces, (*far, even_col, odd_col), (len(far),), scratch=[tile])
    arrived = [swap_far(pieces[0])]
    near_halo = swap_near(near)
    args, scratch = (*far, near, *coefs, own, pair), [whole, tile, tile]
    far_part, near_part, local = run(
        part_defect_body, "part_defect", [full, full, half], args, (len(far),), scratch=scratch
    )
    fix = run(coarse_first_body, "coarse_first", [half], (keep, local, far_sums, near_sums, *coarse), smem=1, work=8)[0]
    first = fix
    for sweep_index in range(COARSE_SWEEPS - 1):
        far_sums, near_sums = swap_far(fix), swap_near(fix)
        part = run(coarse_part_body, "coarse_part", [half], (fix, first, *coarse))[0]
        if len(arrived) < len(pieces):
            held, part = after(pieces[len(arrived)], part)
            arrived.append(swap_far(held))
        if sweep_index:
            part, arrived[sweep_index - 1] = after(part, arrived[sweep_index - 1])
        args = (keep, part, far_sums, near_sums, *coarse)
        fix = run(coarse_finish_body, "coarse_finish", [half], args, smem=1, work=8)[0]

    far_sums, near_sums = swap_far(fix), swap_near(fix)
    args = (far_part, near_part, fix, near_halo, pair_t, *coefs)
    scratch = [tile] * 2 + [pltpu.VMEM((rows, cols), F32)] * 2
    far_part, near_part = run(third_body, "third", [full, full], args, scratch=scratch)
    plane_sums, far_part = after(plane_sums, far_part)
    state_nb = run(rebuild_body, "rebuild", [full], (plane_sums, *arrived, even_t, odd_t), scratch=[tile] * 2)[0]
    args = (keep, far_part, far_sums, state_nb, pair_t, *coefs)
    far = run(fix_far_body, "fix_far", [full], args, smem=1, scratch=[tile] * 2, work=8)
    starts = [0]
    top = (2, rows // 2, cols)
    args = (near_part, near_sums, pair_t, *coefs)
    near, *near_chunks = run(fix_near_body, "fix_near", [full, top, top], args, scratch=[tile] * 2, work=8)

    far_halo, near_halos = [swap_far(v) for v in far], [swap_near(v) for v in near_chunks]
    far_part, near_part = run(part_body, "part", [full] * 2, (*far, near, *coefs, own), (len(far),), scratch=[whole])
    outs = [(2, 2, rows, cols), full]

    def final(which, fields, done):
        args = (where, keep, *coefs, phase_lin, phase_state, *fields, *done)
        in_specs = [SMEM, SMEM] + [VMEM] * (len(args) - len(done) - 2) + [ANY] * len(done)
        scratch = []
        for halo in fields[1::2]:
            n = halo.shape[1]
            scratch += [pltpu.VMEM((2, n, cols), F32), pltpu.VMEM((n, cols), F32), pltpu.SemaphoreType.DMA((8,))]
        body = functools.partial(final_body, which)
        aliases = {len(args) - 2: 0, len(args) - 1: 1} if done else None
        return call(body, "final", outs, args, in_specs, [ANY, ANY], scratch, aliases, work=10)

    done = ()
    for lo, halo in zip(starts[:-1], far_halo[:-1]):
        done = final([(0, lo)], (far_part, halo), done)
    fields = (near_part, near_halos[0], near_part, near_halos[1])
    done = final([(1, 0), (1, rows // 2)], fields, done)
    done = final([(0, starts[-1])], (far_part, far_halo[-1]), done)
    return tuple(done)


def solution(mesh):
    in_specs = (
        P(("grp", "gx"), None, None),
        P(("grp", "gx"), None, None),
        P(None, ("grp", "gx"), None, None),
        P(None, ("grp", "gx"), None, None),
    )
    out_specs = (P(None, ("grp", "gx"), None, None), P(("grp", "gx"), None, None))
    return jax.shard_map(
        on_device, mesh=mesh, in_specs=in_specs, out_specs=out_specs, check_vma=False
    )
```
